32 devices in a mesh: seq: 8 (over z, x), ch: 4 (over y, core).
Axes of the slice: x: 2, y: 2, z: 4, core: 2. Of those that a mesh axis runs over, the one named last changes fastest.
Arguments:
- projected: bfloat16 [1024, 3, 4096], P('seq', None, 'ch'), may hold values from -6 to 6
- cotangent: bfloat16 [1024, 4096], P('seq', 'ch'), may hold values from -6 to 6
- short_weight: float32 [3, 7, 4096], P(None, None, 'ch'), may hold values from -2 to 2
- long_filter: float32 [8, 1024], P('ch', 'seq'), may hold values from -0.1875 to 0.1875
Outputs:
- grad_proj: bfloat16 [1024, 3, 4096], P('seq', None, 'ch')
- grad_short: float32 [3, 7, 4096], P(None, None, 'ch')
- grad_filter: float32 [8, 1024], P(None, ('seq', 'ch'))
The draws below stay inside these ranges and needn't reach their ends.
All inputs are finite; a program needn't handle non-finite values.
Results may differ from the reference program's by a relative error of at most 0.00155.
Values may be sent and summed in bfloat16 or wider, within the bound.
A program may use at most 64 MiB of HBM per device.

```python
import math
import jax
import jax.numpy as jnp
from jax import lax

D = 4096
GROUPS = 8
KSHORT = 7
TOKENS = 1024


def level_of(rng, extent, pieces, smallest, top_value):
    loudness = 1.0
    for dim, shards_of in pieces:
        steps = jax.random.uniform(jax.random.fold_in(jax.random.fold_in(rng, 6), dim), (shards_of,), jnp.float32, smallest / len(pieces), top_value / len(pieces))
        loudness = loudness * jnp.repeat(jnp.exp(steps), extent[dim] // shards_of).reshape((-1,) + (1,) * (len(extent) - 1 - dim))
    return loudness


def centred(key, dims, width, reach, shards=(), held_as=jnp.bfloat16):
    loudness = level_of(key, dims, shards, -0.22, 0.18) if shards else 1.0
    entries = jax.random.normal(key, dims, jnp.float32) * width * loudness
    return jnp.minimum(jnp.maximum(entries, -reach), reach).astype(held_as)


def setup_inputs(seed: int = 0) -> dict:
    arg_keys = jax.random.split(jax.random.key(seed), 5)
    projected = centred(arg_keys[0], (TOKENS, 3, D), 1.0, 6.0, ((0, 8), (2, 4)))
    cotangent = centred(arg_keys[1], (TOKENS, D), 1.0, 6.0, ((0, 8), (1, 4)))
    short_weight = centred(arg_keys[2], (3, KSHORT, D), KSHORT ** -0.5, 2.0, ((2, 4),), jnp.float32)
    long_filter = centred(arg_keys[3], (GROUPS, TOKENS), TOKENS ** -0.5, 0.1875, ((0, 4), (1, 8)), jnp.float32)
    return dict(projected=projected, cotangent=cotangent, short_weight=short_weight, long_filter=long_filter)


def group_backward(proj_group, grad_group, weight_group, filter_group):
    tap_count = weight_group.shape[1]
    channels = proj_group.shape[2]
    padded = jnp.concatenate([jnp.zeros((tap_count - 1, 3, channels), jnp.float32), proj_group], 0)
    features = jnp.zeros((TOKENS, 3, channels), jnp.float32)
    for offset in range(tap_count):
        first_row = tap_count - 1 - offset
        features = features + weight_group[:, offset, :][None] * padded[first_row:first_row + TOKENS]
    mixed_input = features[:, 1] * features[:, 2]
    gated_grad = grad_group * features[:, 0]
    length = 2 * TOKENS
    filter_spec = jnp.fft.rfft(filter_group, n=length)[:, None]
    mixed_spec = jnp.fft.rfft(mixed_input, n=length, axis=0)
    gated_spec = jnp.fft.rfft(gated_grad, n=length, axis=0)
    conv_out = jnp.fft.irfft(filter_spec * mixed_spec, n=length, axis=0)[:TOKENS]
    corr_out = jnp.fft.irfft(jnp.conj(filter_spec) * gated_spec, n=length, axis=0)[:TOKENS]
    cross_spec = lax.optimization_barrier(jnp.sum(jnp.conj(mixed_spec) * gated_spec, axis=1))
    filter_grad = jnp.fft.irfft(cross_spec, n=length)[:TOKENS]
    feat_grad = jnp.stack([grad_group * conv_out, corr_out * features[:, 2], corr_out * features[:, 1]], 1)
    padded_grad = jnp.concatenate([feat_grad, jnp.zeros((tap_count - 1, 3, channels), jnp.float32)], 0)
    grad_proj = jnp.zeros((TOKENS, 3, channels), jnp.float32)
    for offset in range(tap_count):
        grad_proj = grad_proj + weight_group[:, offset, :][None] * padded_grad[offset:offset + TOKENS]
    short_terms = []
    for offset in range(tap_count):
        first_row = tap_count - 1 - offset
        short_terms.append(lax.optimization_barrier(jnp.sum(feat_grad * padded[first_row:first_row + TOKENS], axis=0)))
    grad_short = jnp.stack(short_terms, 1) * (1.0 / math.sqrt(TOKENS))
    filter_grad = filter_grad * (1.0 / math.sqrt(TOKENS * channels))
    return (grad_proj.astype(jnp.bfloat16), grad_short, filter_grad)

def reference(projected, cotangent, short_weight, long_filter):
    group_width = D // GROUPS

    def one_group(group_index):
        first_col = group_index * group_width
        proj_group = lax.dynamic_slice_in_dim(projected, first_col, group_width, 2).astype(jnp.float32)
        grad_group = lax.dynamic_slice_in_dim(cotangent, first_col, group_width, 1).astype(jnp.float32)
        weight_group = lax.dynamic_slice_in_dim(short_weight, first_col, group_width, 2)
        filter_group = lax.dynamic_index_in_dim(long_filter, group_index, 0, keepdims=False)
        return group_backward(proj_group, grad_group, weight_group, filter_group)
    grad_proj, grad_short, grad_filter = lax.map(one_group, jnp.arange(GROUPS, dtype=jnp.int32))
    grad_proj = jnp.transpose(grad_proj, (1, 2, 0, 3)).reshape(TOKENS, 3, D)
    grad_short = jnp.transpose(grad_short, (1, 2, 0, 3)).reshape(3, KSHORT, D)
    return (grad_proj, grad_short, grad_filter)
```

```python
import functools
import math

import jax
import jax.numpy as jnp
from jax import lax
from jax.experimental import pallas as pl
from jax.experimental.pallas import tpu as pltpu
from jax.sharding import PartitionSpec as P

highest = lax.Precision.HIGHEST
MESH = pl.DeviceIdType.MESH
LANES = 128
WIDE = 256
ROWS = 64


def passed_along(block, axis, distance):
    devices = range(lax.axis_size(axis))
    route = [(i - distance, i) for i in devices if i - distance in devices]
    return lax.ppermute(block, axis, route)


def einsum_high(form, table, operand):
    return jnp.einsum(form, table, operand, precision=highest)


def angle_table(first, second, length):
    product = first[:, None] * second[None, :] % length
    radians = product.astype(jnp.float32) * (2.0 * math.pi / length)
    return (jnp.cos(radians), jnp.sin(radians))


def complex_dft(cosine, sine, real_part, imag_part, joined, sign):
    table = jnp.stack(
        [jnp.stack([cosine, -sign * sine], 0), jnp.stack([sign * sine, cosine], 0)], 0
    )
    stacked = jnp.stack([real_part, imag_part], 0)
    result = jnp.einsum(joined, table, stacked, precision=highest)
    return (result[0], result[1])


def rotate(real_part, imag_part, cosine, sine, sign):
    return (
        real_part * cosine - sign * imag_part * sine,
        imag_part * cosine + sign * real_part * sine,
    )


def combine(mixed_re, mixed_im, grad_re, grad_im, filt_re, filt_im):
    conv_re = filt_re * mixed_re - filt_im * mixed_im
    conv_im = filt_re * mixed_im + filt_im * mixed_re
    corr_re = filt_re * grad_re + filt_im * grad_im
    corr_im = filt_re * grad_im - filt_im * grad_re
    cross_re = mixed_re * grad_re + mixed_im * grad_im
    cross_im = mixed_re * grad_im - mixed_im * grad_re
    return (conv_re - corr_im, conv_im + corr_re, cross_re, cross_im)


def featurize(extended, weights, row_count):
    tap_count = weights.shape[1]
    accumulated = jnp.zeros((row_count,) + extended.shape[1:], jnp.float32)
    for offset in range(tap_count):
        first_row = tap_count - 1 - offset
        accumulated = accumulated + weights[:, offset, :] * extended[
            first_row : first_row + row_count
        ].astype(jnp.float32)
    return accumulated


def transpose_pair(signals, filters):
    return (
        lax.all_to_all(signals, "seq", split_axis=0, concat_axis=1, tiled=True),
        lax.all_to_all(filters, "seq", split_axis=0, concat_axis=1, tiled=True),
    )


def sequence_plan(mixed_input, gated_grad, long_filter):
    row_count, chan_count = mixed_input.shape
    group_count = long_filter.shape[0]
    seq_count = lax.axis_size("seq")
    seq_index = lax.axis_index("seq")
    per_block = row_count // seq_count
    fft_length = 2 * row_count * seq_count
    freq_index = jnp.arange(2 * seq_count, dtype=jnp.int32)
    block_index = jnp.arange(seq_count, dtype=jnp.int32)
    row_index = jnp.arange(row_count, dtype=jnp.int32)
    signals = jnp.stack([mixed_input, gated_grad], 1)[:, None]
    filters = jnp.transpose(long_filter)[:, None]
    sig_cols, filt_cols = transpose_pair(signals, filters)
    cos_one, sin_one = angle_table(freq_index, block_index, 2 * seq_count)
    sig_re = einsum_high("kb,abxc->kaxc", cos_one, sig_cols)
    sig_im = -einsum_high("kb,abxc->kaxc", sin_one, sig_cols)
    filt_re = einsum_high("kb,abg->kag", cos_one, filt_cols)
    filt_im = -einsum_high("kb,abg->kag", sin_one, filt_cols)
    positions = seq_index * per_block + jnp.arange(per_block, dtype=jnp.int32)
    cos_twist, sin_twist = angle_table(freq_index, positions, fft_length)
    sig_re, sig_im = rotate(
        sig_re, sig_im, cos_twist[:, :, None, None], sin_twist[:, :, None, None], -1.0
    )
    filt_re, filt_im = rotate(filt_re, filt_im, cos_twist[:, :, None], sin_twist[:, :, None], -1.0)
    sig_rows, filt_rows = transpose_pair(
        jnp.stack([sig_re, sig_im], 2), jnp.stack([filt_re, filt_im], 2)
    )
    cos_two, sin_two = angle_table(row_index, row_index, row_count)
    spec_re, spec_im = complex_dft(
        cos_two, sin_two, sig_rows[:, :, 0], sig_rows[:, :, 1], "pqka,qjaxc->pjkxc", -1.0
    )
    hspec_re, hspec_im = complex_dft(
        cos_two, sin_two, filt_rows[:, :, 0], filt_rows[:, :, 1], "pqka,qjag->pjkg", -1.0
    )
    leading = spec_re.shape[:2]
    group_shape = leading + (group_count, chan_count // group_count)
    wave_re, wave_im, cross_re, cross_im = combine(
        spec_re[:, :, 0].reshape(group_shape),
        spec_im[:, :, 0].reshape(group_shape),
        spec_re[:, :, 1].reshape(group_shape),
        spec_im[:, :, 1].reshape(group_shape),
        hspec_re[..., None],
        hspec_im[..., None],
    )
    wave_re = wave_re.reshape(leading + (chan_count,))
    wave_im = wave_im.reshape(leading + (chan_count,))
    cross_re = jnp.sum(cross_re, -1)
    cross_im = jnp.sum(cross_im, -1)
    back_re, back_im = complex_dft(cos_two, sin_two, wave_re, wave_im, "pqak,qjkc->pajc", 1.0)
    cback_re, cback_im = complex_dft(cos_two, sin_two, cross_re, cross_im, "pqak,qjkg->pajg", 1.0)
    pair_freq = seq_index * 2 + jnp.arange(2, dtype=jnp.int32)
    cos_back, sin_back = angle_table(row_index, pair_freq, fft_length)
    back_re, back_im = rotate(back_re, back_im, cos_back[:, :, None], sin_back[:, :, None], 1.0)
    cback_re, cback_im = rotate(cback_re, cback_im, cos_back[:, :, None], sin_back[:, :, None], 1.0)
    wave_cols, cross_cols = transpose_pair(
        jnp.stack([back_re, back_im], 2), jnp.stack([cback_re, cback_im], 2)
    )
    cos_three, sin_three = angle_table(block_index, freq_index, 2 * seq_count)
    time_re, time_im = complex_dft(
        cos_three, sin_three, wave_cols[:, :, 0], wave_cols[:, :, 1], "pqbk,qakc->pbac", 1.0
    )
    cross_time = einsum_high("bk,akg->bag", cos_three, cross_cols[:, :, 0]) - einsum_high(
        "bk,akg->bag", sin_three, cross_cols[:, :, 1]
    )
    inverse_scale = 1.0 / fft_length
    wave_out, cross_out = transpose_pair(
        jnp.stack([time_re, time_im], 2) * inverse_scale, cross_time * inverse_scale
    )
    return (wave_out[0, :, 0], wave_out[0, :, 1], jnp.transpose(cross_out[0]))


def split_halves(value):
    top = value.astype(jnp.bfloat16)
    rest = (value - top.astype(jnp.float32)).astype(jnp.bfloat16)
    return top, rest


def dot32(left, right):
    return jnp.dot(left, right, preferred_element_type=jnp.float32)


def dot32_t(left, right):
    return lax.dot_general(
        left, right, (((1,), (1,)), ((), ())), preferred_element_type=jnp.float32
    )


def tile(index):
    return pl.ds(pl.multiple_of(index * LANES, LANES), LANES)


def send_to(src, dst, send_sem, recv_sem, peer):
    return pltpu.make_async_remote_copy(
        src_ref=src,
        dst_ref=dst,
        send_sem=send_sem,
        recv_sem=recv_sem,
        device_id=peer,
        device_id_type=MESH,
    )


def build_filters(taps, ns, low_hi, low_lo, up_hi, up_lo):
    row = lax.broadcasted_iota(jnp.int32, (LANES, LANES), 0)
    col = lax.broadcasted_iota(jnp.int32, (LANES, LANES), 1)
    flip = (row + col == LANES - 1).astype(jnp.float32)
    zero = jnp.zeros((LANES, LANES), jnp.float32)
    zero16 = zero.astype(jnp.bfloat16)
    flipped = jnp.dot(
        taps[...].reshape(ns * 8, LANES), flip, precision=highest,
        preferred_element_type=jnp.float32,
    )
    last_up, last_low = zero, zero
    top = ns - WIDE // LANES
    low_hi[:, (ns - 1) * LANES :] = jnp.concatenate([zero16, zero16], 0)
    low_lo[:, (ns - 1) * LANES :] = jnp.concatenate([zero16, zero16], 0)
    up_hi[LANES:, :LANES] = zero16
    up_lo[LANES:, :LANES] = zero16
    for d in range(ns):
        forward = jnp.concatenate([taps[d]] * (LANES // 8), 0)
        back = jnp.concatenate([flipped[d * 8 : d * 8 + 8]] * (LANES // 8), 0)
        forward = pltpu.roll(forward, 0, 1, stride=1, stride_axis=0)
        back = pltpu.roll(back, 1, 1, stride=1, stride_axis=0)
        up = split_halves(jnp.where(col >= row, forward, last_up))
        low = split_halves(jnp.where(row >= col, back, last_low))
        last_up, last_low = forward, back
        for u in range(WIDE // LANES):
            v = d + u
            if v < ns:
                up_hi[u * LANES : (u + 1) * LANES, v * LANES : (v + 1) * LANES] = up[0]
                up_lo[u * LANES : (u + 1) * LANES, v * LANES : (v + 1) * LANES] = up[1]
            v = top + u - d
            if 0 <= v < ns:
                low_hi[u * LANES : (u + 1) * LANES, v * LANES : (v + 1) * LANES] = low[0]
                low_lo[u * LANES : (u + 1) * LANES, v * LANES : (v + 1) * LANES] = low[1]


def diagonal_sums(gram, ns):
    row = lax.broadcasted_iota(jnp.int32, (LANES, LANES), 0)
    col = lax.broadcasted_iota(jnp.int32, (LANES, LANES), 1)
    turned = []
    for d in range(ns):
        block = gram[LANES:, d * LANES : (d + 1) * LANES]
        if d + 1 < ns:
            block = block + gram[:LANES, (d + 1) * LANES : (d + 2) * LANES]
        turned.append(pltpu.roll(block, 1, 1, stride=1, stride_axis=0))
    turned.append(jnp.zeros((LANES, LANES), jnp.float32))
    return [
        jnp.sum(jnp.where(col <= row, turned[d], turned[d + 1]), 0, keepdims=True)
        for d in range(ns)
    ]


def resident_kernel(
    ns, nc, kt, groups,
    proj, cot, weight, filt,
    gp_out, gs_out, gf_out,
    pin, cin, wide, feat, mixed, gated, fgrad, gp_send,
    tap_send, taps, low_hi, low_lo, up_hi, up_lo, gram,
    fa_send, fa_recv, fb_send, fb_recv, gs_acc, gs_send, gs_recv,
    in_send, in_recv, gp_ssem, gp_rsem, gs_ssem, gs_rsem,
    fa_ssem, fa_rsem, fb_ssem, fb_rsem,
):
    me = lax.axis_index("seq")
    mych = lax.axis_index("ch")
    total = ns * LANES
    tiles_per_group = ns // groups
    seq_peers = [(lax.rem(me + i, ns), mych) for i in range(1, ns)]
    ch_peers = [(me, lax.rem(mych + i, nc)) for i in range(1, nc)]

    barrier = pltpu.get_barrier_semaphore()
    for peer in seq_peers + ch_peers:
        pl.semaphore_signal(barrier, inc=1, device_id=peer, device_id_type=MESH)
    for g in range(groups):
        tap_send[g] = jnp.broadcast_to(filt[g : g + 1, :], (8, LANES))
    pl.semaphore_wait(barrier, ns + nc - 2)

    sends = []
    for peer in seq_peers:
        q = peer[0]
        copy = send_to(
            tap_send.at[q // tiles_per_group], taps.at[me],
            in_send.at[0, q], in_recv.at[0, me], peer,
        )
        copy.start()
        sends.append(copy)
    for peer in seq_peers:
        q = peer[0]
        for copy in (
            send_to(
                proj.at[:, :, tile(q)], pin.at[:, tile(me), :],
                in_send.at[1, q], in_recv.at[1, me], peer,
            ),
            send_to(
                cot.at[:, tile(q)], cin.at[tile(me), :],
                in_send.at[2, q], in_recv.at[2, me], peer,
            ),
        ):
            copy.start()
            sends.append(copy)

    taps[me] = tap_send[me // tiles_per_group]
    pin[:, tile(me), :] = proj[:, :, tile(me)]
    cin[tile(me), :] = cot[:, tile(me)]
    for j in range(3):
        wide[j, 0:8, :] = jnp.zeros((8, LANES), jnp.float32)
        fgrad[j, total : total + 8, :] = jnp.zeros((8, LANES), jnp.float32)
        for k in range(kt):
            gs_acc[j, k] = jnp.zeros((8, LANES), jnp.float32)
    gram[...] = jnp.zeros(gram.shape, jnp.float32)
    for peer in seq_peers:
        q = peer[0]
        send_to(
            tap_send.at[0], taps.at[q], in_send.at[0, q], in_recv.at[0, q], peer
        ).wait_recv()
    build_filters(taps, ns, low_hi, low_lo, up_hi, up_lo)

    def featurize_block(b, carry):
        @pl.when(b != me)
        def _():
            send_to(
                proj.at[:, :, tile(b)], pin.at[:, tile(b), :],
                in_send.at[1, b], in_recv.at[1, b], (b, mych),
            ).wait_recv()
            send_to(
                cot.at[:, tile(b)], cin.at[tile(b), :],
                in_send.at[2, b], in_recv.at[2, b], (b, mych),
            ).wait_recv()

        base = pl.multiple_of(b * LANES, LANES)
        for j in range(3):
            wide[j, pl.ds(base + 8, LANES), :] = pin[j, pl.ds(base, LANES), :].astype(jnp.float32)
        for part in range(LANES // ROWS):
            first = base + part * ROWS
            feats = []
            for j in range(3):
                acc = jnp.zeros((ROWS, LANES), jnp.float32)
                for k in range(kt):
                    acc = acc + weight[j, k : k + 1, tile(me)] * wide[
                        j, pl.ds(first + 8 - k, ROWS), :
                    ]
                feats.append(acc)
            rows = pl.ds(first, ROWS)
            feat[0, rows, :] = feats[1]
            feat[1, rows, :] = feats[2]
            top, rest = split_halves(feats[1] * feats[2])
            mixed[rows, 0:LANES] = top
            mixed[rows, LANES:WIDE] = rest
            top, rest = split_halves(cin[rows, :].astype(jnp.float32) * feats[0])
            gated[rows, 0:LANES] = top
            gated[rows, LANES:WIDE] = rest
        return carry

    lax.fori_loop(0, ns, featurize_block, 0)

    steps = total // WIDE
    for b in range(steps):
        rows = slice(b * WIDE, (b + 1) * WIDE)
        upto = (b + 1) * WIDE
        start = total - upto
        both = dot32(low_hi[:, start:], mixed[:upto, :])
        conv = both[:, :LANES] + both[:, LANES:]
        conv = conv + dot32(low_lo[:, start:], mixed[:upto, :LANES])
        fgrad[0, rows, :] = cin[rows, :].astype(jnp.float32) * conv
        span = total - b * WIDE
        both = dot32(up_hi[:, :span], gated[b * WIDE :, :])
        corr = both[:, :LANES] + both[:, LANES:]
        corr = corr + dot32(up_lo[:, :span], gated[b * WIDE :, :LANES])
        fgrad[1, rows, :] = corr * feat[1, rows, :]
        fgrad[2, rows, :] = corr * feat[0, rows, :]

    def finish_block(i, carry):
        b = lax.rem(me + 1 + i, ns)
        base = pl.multiple_of(b * LANES, LANES)
        for part in range(LANES // ROWS):
            first = base + part * ROWS
            for j in range(3):
                acc = jnp.zeros((ROWS, LANES), jnp.float32)
                source = wide[j, pl.ds(first + 8, ROWS), :]
                for k in range(kt):
                    shifted = fgrad[j, pl.ds(first + k, ROWS), :]
                    acc = acc + weight[j, k : k + 1, tile(me)] * shifted
                    terms = (shifted * source).reshape(ROWS // 8, 8, LANES)
                    gs_acc[j, k] += jnp.sum(terms, 0)
                gp_send[j, pl.ds(first, ROWS), :] = acc.astype(jnp.bfloat16)

        @pl.when(b != me)
        def _():
            send_to(
                gp_send.at[:, tile(b), :], gp_out.at[:, :, tile(me)],
                gp_ssem.at[b], gp_rsem.at[me], (b, mych),
            ).start()

        return carry

    lax.fori_loop(0, ns, finish_block, 0)
    gp_out[:, :, tile(me)] = gp_send[:, tile(me), :]

    short_scale = 1.0 / math.sqrt(total)
    for j in range(3):
        lines = [jnp.sum(gs_acc[j, k], 0, keepdims=True) for k in range(kt)]
        lines += [jnp.zeros((1, LANES), jnp.float32)] * (8 - kt)
        gs_send[j] = jnp.concatenate(lines, 0) * short_scale
    for peer in seq_peers:
        q = peer[0]
        copy = send_to(gs_send, gs_recv.at[me], gs_ssem.at[q], gs_rsem.at[me], peer)
        copy.start()
        sends.append(copy)
    gs_recv[me] = gs_send[...]

    flip = (
        lax.broadcasted_iota(jnp.int32, (WIDE, WIDE), 0)
        + lax.broadcasted_iota(jnp.int32, (WIDE, WIDE), 1)
        == WIDE - 1
    ).astype(jnp.float32).astype(jnp.bfloat16)
    for b in range(steps):
        left = dot32(flip, mixed[b * WIDE : (b + 1) * WIDE, :]).astype(jnp.bfloat16)
        for d in range(steps - b):
            right = gated[(b + d) * WIDE : (b + d + 1) * WIDE, :]
            top = right[:, :LANES]
            cols = slice(d * WIDE, (d + 1) * WIDE)
            gram[:, cols] += dot32_t(left, jnp.concatenate([top, top], 1)) + dot32_t(
                left[:, :LANES], right[:, LANES:]
            )
    filter_scale = 1.0 / math.sqrt(total * tiles_per_group * LANES)
    for d, line in enumerate(diagonal_sums(gram, ns)):
        fa_send[d] = jnp.broadcast_to(line * filter_scale, (8, LANES))
    for peer in seq_peers:
        q = peer[0]
        copy = send_to(fa_send.at[q], fa_recv.at[me], fa_ssem.at[q], fa_rsem.at[me], peer)
        copy.start()
        sends.append(copy)
    fa_recv[me] = fa_send[me]
    for peer in seq_peers:
        q = peer[0]
        send_to(fa_send.at[q], fa_recv.at[q], fa_ssem.at[q], fa_rsem.at[q], peer).wait_recv()
    for g in range(groups):
        summed = fa_recv[g * tiles_per_group]
        for q in range(g * tiles_per_group + 1, (g + 1) * tiles_per_group):
            summed = summed + fa_recv[q]
        fb_send[g] = summed
    for peer in ch_peers:
        c = peer[1]
        copy = send_to(fb_send, fb_recv.at[mych], fb_ssem.at[c], fb_rsem.at[mych], peer)
        copy.start()
        sends.append(copy)
    fb_recv[mych] = fb_send[...]
    for peer in ch_peers:
        c = peer[1]
        send_to(fb_send, fb_recv.at[c], fb_ssem.at[c], fb_rsem.at[c], peer).wait_recv()
    width = LANES // nc
    for c in range(nc):
        for g in range(groups):
            line = fb_recv[c, g]
            mine = line[:, 0:width]
            for other in range(1, nc):
                piece = line[:, other * width : (other + 1) * width]
                mine = jnp.where(mych == other, piece, mine)
            at = c * groups + g
            gf_out[at : at + 1, :] = mine[0:1, :]

    for peer in seq_peers:
        q = peer[0]
        send_to(gs_send, gs_recv.at[q], gs_ssem.at[q], gs_rsem.at[q], peer).wait_recv()
    for q in range(ns):
        for j in range(3):
            gs_out[j, :, q * LANES : (q + 1) * LANES] = gs_recv[q, j, 0:kt, :]
    for peer in seq_peers:
        q = peer[0]
        copy = send_to(
            gp_send.at[:, tile(q), :], gp_out.at[:, :, tile(q)],
            gp_ssem.at[q], gp_rsem.at[q], peer,
        )
        copy.wait_send()
        copy.wait_recv()
    for copy in sends:
        copy.wait_send()


def resident(projected, cotangent, short_weight, long_filter):
    row_count, streams, chan_count = projected.shape
    kt = short_weight.shape[1]
    groups = long_filter.shape[0]
    ns, nc = lax.axis_size("seq"), lax.axis_size("ch")
    total = row_count * ns
    f32, bf16 = jnp.float32, jnp.bfloat16
    dma = pltpu.SemaphoreType.DMA
    vmem = pl.BlockSpec(memory_space=pltpu.VMEM)
    grad_proj, grad_short, grad_filter = pl.pallas_call(
        functools.partial(resident_kernel, ns, nc, kt, groups),
        out_shape=(
            jax.ShapeDtypeStruct((streams, row_count, chan_count), bf16),
            jax.ShapeDtypeStruct((streams, kt, chan_count), f32),
            jax.ShapeDtypeStruct((groups * nc, row_count // nc), f32),
        ),
        in_specs=[vmem] * 4,
        out_specs=(vmem, vmem, vmem),
        scratch_shapes=[
            pltpu.VMEM((3, total, LANES), bf16),
            pltpu.VMEM((total, LANES), bf16),
            pltpu.VMEM((3, total + 8, LANES), f32),
            pltpu.VMEM((2, total, LANES), f32),
            pltpu.VMEM((total, WIDE), bf16),
            pltpu.VMEM((total, WIDE), bf16),
            pltpu.VMEM((3, total + 8, LANES), f32),
            pltpu.VMEM((3, total, LANES), bf16),
            pltpu.VMEM((groups, 8, LANES), f32),
            pltpu.VMEM((ns, 8, LANES), f32),
            pltpu.VMEM((WIDE, total), bf16),
            pltpu.VMEM((WIDE, total), bf16),
            pltpu.VMEM((WIDE, total), bf16),
            pltpu.VMEM((WIDE, total), bf16),
            pltpu.VMEM((WIDE, total), f32),
            pltpu.VMEM((ns, 8, LANES), f32),
            pltpu.VMEM((ns, 8, LANES), f32),
            pltpu.VMEM((groups, 8, LANES), f32),
            pltpu.VMEM((nc, groups, 8, LANES), f32),
            pltpu.VMEM((3, 8, 8, LANES), f32),
            pltpu.VMEM((3, 8, LANES), f32),
            pltpu.VMEM((ns, 3, 8, LANES), f32),
            dma((3, ns)), dma((3, ns)),
            dma((ns,)), dma((ns,)),
            dma((ns,)), dma((ns,)),
            dma((ns,)), dma((ns,)),
            dma((nc,)), dma((nc,)),
        ],
        compiler_params=pltpu.CompilerParams(
            collective_id=0, has_side_effects=True, vmem_limit_bytes=40 * 1024 * 1024
        ),
    )(jnp.transpose(projected, (1, 0, 2)), cotangent, short_weight, long_filter)
    return jnp.transpose(grad_proj, (1, 0, 2)), grad_short, grad_filter


def spread(projected, cotangent, short_weight, long_filter):
    tap_count = short_weight.shape[1]
    row_count = projected.shape[0]
    margin = tap_count - 1
    front_rows = passed_along(projected[row_count - margin :], "seq", 1)
    extended = jnp.concatenate([front_rows, projected], 0)
    features = featurize(extended, short_weight, row_count)
    grad_out = cotangent.astype(jnp.float32)
    mixed_input = features[:, 1] * features[:, 2]
    gated_grad = grad_out * features[:, 0]
    conv_out, corr_out, filt_grad = sequence_plan(mixed_input, gated_grad, long_filter)
    token_count = row_count * lax.axis_size("seq")
    group_width = mixed_input.shape[1] // long_filter.shape[0]
    scaled_grad = filt_grad * (1.0 / math.sqrt(token_count * group_width))
    owned_grad = lax.all_to_all(scaled_grad, "ch", split_axis=1, concat_axis=0, tiled=True)
    feat_grad = jnp.stack(
        [grad_out * conv_out, corr_out * features[:, 2], corr_out * features[:, 1]], 1
    )
    next_rows = passed_along(feat_grad[:margin].astype(jnp.bfloat16), "seq", -1).astype(jnp.float32)
    extended_grad = jnp.concatenate([feat_grad, next_rows], 0)
    grad_proj = jnp.zeros(feat_grad.shape, jnp.float32)
    for offset in range(tap_count):
        grad_proj = (
            grad_proj + short_weight[:, offset, :] * extended_grad[offset : offset + row_count]
        )
    short_terms = []
    for offset in range(tap_count):
        first_row = margin - offset
        short_terms.append(
            jnp.sum(feat_grad * extended[first_row : first_row + row_count].astype(jnp.float32), 0)
        )
    grad_short = lax.psum(jnp.stack(short_terms, 1), "seq") * (1.0 / math.sqrt(token_count))
    return (grad_proj.astype(jnp.bfloat16), grad_short, owned_grad)


def local(projected, cotangent, short_weight, long_filter):
    row_count, _, chan_count = projected.shape
    seq_count = lax.axis_size("seq")
    group_width = chan_count // long_filter.shape[0]
    fits = (
        row_count == LANES
        and chan_count == LANES * seq_count
        and group_width % LANES == 0
        and row_count * seq_count % WIDE == 0
        and short_weight.shape[1] <= 8
    )
    plan = resident if fits else spread
    return plan(projected, cotangent, short_weight, long_filter)


def solution(mesh):
    return jax.shard_map(
        local,
        mesh=mesh,
        in_specs=(P("seq", None, "ch"), P("seq", "ch"), P(None, None, "ch"), P("ch", "seq")),
        out_specs=(P("seq", None, "ch"), P(None, None, "ch"), P(None, ("seq", "ch"))),
        check_vma=False,
    )
```

```python
import functools
import math

import jax
import jax.numpy as jnp
from jax import lax
from jax.experimental import pallas as pl
from jax.experimental.pallas import tpu as pltpu
from jax.sharding import PartitionSpec as P

highest = lax.Precision.HIGHEST
MESH = pl.DeviceIdType.MESH
LANES = 128
WIDE = 256
ROWS = 64


def passed_along(block, axis, distance):
    devices = range(lax.axis_size(axis))
    route = [(i - distance, i) for i in devices if i - distance in devices]
    return lax.ppermute(block, axis, route)


def einsum_high(form, table, operand):
    return jnp.einsum(form, table, operand, precision=highest)


def angle_table(first, second, length):
    product = first[:, None] * second[None, :] % length
    radians = product.astype(jnp.float32) * (2.0 * math.pi / length)
    return (jnp.cos(radians), jnp.sin(radians))


def complex_dft(cosine, sine, real_part, imag_part, joined, sign):
    table = jnp.stack(
        [jnp.stack([cosine, -sign * sine], 0), jnp.stack([sign * sine, cosine], 0)], 0
    )
    stacked = jnp.stack([real_part, imag_part], 0)
    result = jnp.einsum(joined, table, stacked, precision=highest)
    return (result[0], result[1])


def rotate(real_part, imag_part, cosine, sine, sign):
    return (
        real_part * cosine - sign * imag_part * sine,
        imag_part * cosine + sign * real_part * sine,
    )


def combine(mixed_re, mixed_im, grad_re, grad_im, filt_re, filt_im):
    conv_re = filt_re * mixed_re - filt_im * mixed_im
    conv_im = filt_re * mixed_im + filt_im * mixed_re
    corr_re = filt_re * grad_re + filt_im * grad_im
    corr_im = filt_re * grad_im - filt_im * grad_re
    cross_re = mixed_re * grad_re + mixed_im * grad_im
    cross_im = mixed_re * grad_im - mixed_im * grad_re
    return (conv_re - corr_im, conv_im + corr_re, cross_re, cross_im)


def featurize(extended, weights, row_count):
    tap_count = weights.shape[1]
    accumulated = jnp.zeros((row_count,) + extended.shape[1:], jnp.float32)
    for offset in range(tap_count):
        first_row = tap_count - 1 - offset
        accumulated = accumulated + weights[:, offset, :] * extended[
            first_row : first_row + row_count
        ].astype(jnp.float32)
    return accumulated


def transpose_pair(signals, filters):
    return (
        lax.all_to_all(signals, "seq", split_axis=0, concat_axis=1, tiled=True),
        lax.all_to_all(filters, "seq", split_axis=0, concat_axis=1, tiled=True),
    )


def sequence_plan(mixed_input, gated_grad, long_filter):
    row_count, chan_count = mixed_input.shape
    group_count = long_filter.shape[0]
    seq_count = lax.axis_size("seq")
    seq_index = lax.axis_index("seq")
    per_block = row_count // seq_count
    fft_length = 2 * row_count * seq_count
    freq_index = jnp.arange(2 * seq_count, dtype=jnp.int32)
    block_index = jnp.arange(seq_count, dtype=jnp.int32)
    row_index = jnp.arange(row_count, dtype=jnp.int32)
    signals = jnp.stack([mixed_input, gated_grad], 1)[:, None]
    filters = jnp.transpose(long_filter)[:, None]
    sig_cols, filt_cols = transpose_pair(signals, filters)
    cos_one, sin_one = angle_table(freq_index, block_index, 2 * seq_count)
    sig_re = einsum_high("kb,abxc->kaxc", cos_one, sig_cols)
    sig_im = -einsum_high("kb,abxc->kaxc", sin_one, sig_cols)
    filt_re = einsum_high("kb,abg->kag", cos_one, filt_cols)
    filt_im = -einsum_high("kb,abg->kag", sin_one, filt_cols)
    positions = seq_index * per_block + jnp.arange(per_block, dtype=jnp.int32)
    cos_twist, sin_twist = angle_table(freq_index, positions, fft_length)
    sig_re, sig_im = rotate(
        sig_re, sig_im, cos_twist[:, :, None, None], sin_twist[:, :, None, None], -1.0
    )
    filt_re, filt_im = rotate(filt_re, filt_im, cos_twist[:, :, None], sin_twist[:, :, None], -1.0)
    sig_rows, filt_rows = transpose_pair(
        jnp.stack([sig_re, sig_im], 2), jnp.stack([filt_re, filt_im], 2)
    )
    cos_two, sin_two = angle_table(row_index, row_index, row_count)
    spec_re, spec_im = complex_dft(
        cos_two, sin_two, sig_rows[:, :, 0], sig_rows[:, :, 1], "pqka,qjaxc->pjkxc", -1.0
    )
    hspec_re, hspec_im = complex_dft(
        cos_two, sin_two, filt_rows[:, :, 0], filt_rows[:, :, 1], "pqka,qjag->pjkg", -1.0
    )
    leading = spec_re.shape[:2]
    group_shape = leading + (group_count, chan_count // group_count)
    wave_re, wave_im, cross_re, cross_im = combine(
        spec_re[:, :, 0].reshape(group_shape),
        spec_im[:, :, 0].reshape(group_shape),
        spec_re[:, :, 1].reshape(group_shape),
        spec_im[:, :, 1].reshape(group_shape),
        hspec_re[..., None],
        hspec_im[..., None],
    )
    wave_re = wave_re.reshape(leading + (chan_count,))
    wave_im = wave_im.reshape(leading + (chan_count,))
    cross_re = jnp.sum(cross_re, -1)
    cross_im = jnp.sum(cross_im, -1)
    back_re, back_im = complex_dft(cos_two, sin_two, wave_re, wave_im, "pqak,qjkc->pajc", 1.0)
    cback_re, cback_im = complex_dft(cos_two, sin_two, cross_re, cross_im, "pqak,qjkg->pajg", 1.0)
    pair_freq = seq_index * 2 + jnp.arange(2, dtype=jnp.int32)
    cos_back, sin_back = angle_table(row_index, pair_freq, fft_length)
    back_re, back_im = rotate(back_re, back_im, cos_back[:, :, None], sin_back[:, :, None], 1.0)
    cback_re, cback_im = rotate(cback_re, cback_im, cos_back[:, :, None], sin_back[:, :, None], 1.0)
    wave_cols, cross_cols = transpose_pair(
        jnp.stack([back_re, back_im], 2), jnp.stack([cback_re, cback_im], 2)
    )
    cos_three, sin_three = angle_table(block_index, freq_index, 2 * seq_count)
    time_re, time_im = complex_dft(
        cos_three, sin_three, wave_cols[:, :, 0], wave_cols[:, :, 1], "pqbk,qakc->pbac", 1.0
    )
    cross_time = einsum_high("bk,akg->bag", cos_three, cross_cols[:, :, 0]) - einsum_high(
        "bk,akg->bag", sin_three, cross_cols[:, :, 1]
    )
    inverse_scale = 1.0 / fft_length
    wave_out, cross_out = transpose_pair(
        jnp.stack([time_re, time_im], 2) * inverse_scale, cross_time * inverse_scale
    )
    return (wave_out[0, :, 0], wave_out[0, :, 1], jnp.transpose(cross_out[0]))


def split_halves(value):
    top = value.astype(jnp.bfloat16)
    rest = (value - top.astype(jnp.float32)).astype(jnp.bfloat16)
    return top, rest


def dot32(left, right):
    return jnp.dot(left, right, preferred_element_type=jnp.float32)


def dot32_t(left, right):
    return lax.dot_general(
        left, right, (((1,), (1,)), ((), ())), preferred_element_type=jnp.float32
    )


def tile(index, width=LANES):
    return pl.ds(pl.multiple_of(index * width, width), width)


def send_to(src, dst, send_sem, recv_sem, peer):
    return pltpu.make_async_remote_copy(
        src_ref=src,
        dst_ref=dst,
        send_sem=send_sem,
        recv_sem=recv_sem,
        device_id=peer,
        device_id_type=MESH,
    )


def build_filters(taps, ns, low_hi, low_lo, up_hi, up_lo):
    row = lax.broadcasted_iota(jnp.int32, (LANES, LANES), 0)
    col = lax.broadcasted_iota(jnp.int32, (LANES, LANES), 1)
    flip = (row + col == LANES - 1).astype(jnp.float32)
    zero = jnp.zeros((LANES, LANES), jnp.float32)
    zero16 = zero.astype(jnp.bfloat16)
    flipped = jnp.dot(
        taps[...].reshape(ns * 8, LANES), flip, precision=highest,
        preferred_element_type=jnp.float32,
    )
    last_up, last_low = zero, zero
    top = ns - WIDE // LANES
    low_hi[:, (ns - 1) * LANES :] = jnp.concatenate([zero16, zero16], 0)
    low_lo[:, (ns - 1) * LANES :] = jnp.concatenate([zero16, zero16], 0)
    up_hi[LANES:, :LANES] = zero16
    up_lo[LANES:, :LANES] = zero16
    for d in range(ns):
        forward = jnp.concatenate([taps[d]] * (LANES // 8), 0)
        back = jnp.concatenate([flipped[d * 8 : d * 8 + 8]] * (LANES // 8), 0)
        forward = pltpu.roll(forward, 0, 1, stride=1, stride_axis=0)
        back = pltpu.roll(back, 1, 1, stride=1, stride_axis=0)
        up = split_halves(jnp.where(col >= row, forward, last_up))
        low = split_halves(jnp.where(row >= col, back, last_low))
        last_up, last_low = forward, back
        for u in range(WIDE // LANES):
            v = d + u
            if v < ns:
                up_hi[u * LANES : (u + 1) * LANES, v * LANES : (v + 1) * LANES] = up[0]
                up_lo[u * LANES : (u + 1) * LANES, v * LANES : (v + 1) * LANES] = up[1]
            v = top + u - d
            if 0 <= v < ns:
                low_hi[u * LANES : (u + 1) * LANES, v * LANES : (v + 1) * LANES] = low[0]
                low_lo[u * LANES : (u + 1) * LANES, v * LANES : (v + 1) * LANES] = low[1]


def diagonal_sums(gram, ns):
    row = lax.broadcasted_iota(jnp.int32, (LANES, LANES), 0)
    col = lax.broadcasted_iota(jnp.int32, (LANES, LANES), 1)
    turned = []
    for d in range(ns):
        block = gram[LANES:, d * LANES : (d + 1) * LANES]
        if d + 1 < ns:
            block = block + gram[:LANES, (d + 1) * LANES : (d + 2) * LANES]
        turned.append(pltpu.roll(block, 1, 1, stride=1, stride_axis=0))
    turned.append(jnp.zeros((LANES, LANES), jnp.float32))
    return [
        jnp.sum(jnp.where(col <= row, turned[d], turned[d + 1]), 0, keepdims=True)
        for d in range(ns)
    ]


def dot_three(hi, lo, signal):
    width = signal.shape[1] // 2
    both = dot32(hi, signal)
    return both[:, :width] + both[:, width:] + dot32(lo, signal[:, :width])


def resident_kernel(
    ns, nc, kt, groups,
    proj, cot, weight_in, filt_in,
    gp_out, gs_out, gf_out,
    weight, filt, pin, cin, halo, wide, feat, mixed, gated, part, part_edge, fgrad, gp_send,
    tap_send, taps, low_hi, low_lo, up_hi, up_lo, gram,
    fa_send, fa_recv, fb_send, fb_recv, gs_acc, gs_send, gs_pair, gs_sum, gs_recv,
    local_sem, in_send, in_recv, gp_ssem, gp_rsem, gs_ssem, gs_rsem,
    fa_ssem, fa_rsem, fb_ssem, fb_rsem, pair_sem,
):
    me = lax.axis_index("seq")
    mych = lax.axis_index("ch")
    hs = ns // 2
    total = ns * LANES
    span = total // 2
    half = me // hs
    mine = lax.rem(me, hs)
    own_base = pl.multiple_of(half * span, span)
    group_owners = hs // groups
    near = [half * hs + lax.rem(mine + i, hs) for i in range(1, hs)]
    far = [(1 - half) * hs + lax.rem(mine + i, hs) for i in range(hs)]
    everyone = near + far
    ch_peers = [(me, lax.rem(mych + i, nc)) for i in range(1, nc)]
    lanes_of = lambda q: tile(lax.rem(q, hs), WIDE)

    own = [
        pltpu.make_async_copy(filt_in, filt, local_sem.at[0]),
        pltpu.make_async_copy(weight_in.at[:, :, lanes_of(me)], weight, local_sem.at[1]),
        pltpu.make_async_copy(proj.at[:, :, lanes_of(me)], pin.at[:, tile(me), :], local_sem.at[2]),
        pltpu.make_async_copy(cot.at[:, lanes_of(me)], cin.at[tile(me), :], local_sem.at[3]),
    ]
    for copy in own:
        copy.start()
    barrier = pltpu.get_barrier_semaphore()
    for q in everyone:
        pl.semaphore_signal(barrier, inc=1, device_id=(q, mych), device_id_type=MESH)
    for peer in ch_peers:
        pl.semaphore_signal(barrier, inc=1, device_id=peer, device_id_type=MESH)
    own[0].wait()
    for g in range(groups):
        tap_send[g] = jnp.broadcast_to(filt[g : g + 1, :], (8, LANES))
    pl.semaphore_wait(barrier, ns + nc - 2)

    def tap_copy(q, src):
        return send_to(
            tap_send.at[lax.rem(q, hs) // group_owners], taps.at[src],
            in_send.at[0, q], in_recv.at[0, src], (q, mych),
        )

    def halo_copy(q, src, first):
        return send_to(
            proj.at[:, pl.ds(first, 16), lanes_of(q)], halo,
            in_send.at[3, q], in_recv.at[3, 0], (q, mych),
        )

    def near_copies(q, src):
        return (
            send_to(
                proj.at[:, :, lanes_of(q)], pin.at[:, tile(src), :],
                in_send.at[1, q], in_recv.at[1, src], (q, mych),
            ),
            send_to(
                cot.at[:, lanes_of(q)], cin.at[tile(src), :],
                in_send.at[2, q], in_recv.at[2, src], (q, mych),
            ),
        )

    def mix_copy(q, src):
        return send_to(
            proj.at[1:3, :, lanes_of(q)], pin.at[1:3, tile(src), :],
            in_send.at[1, q], in_recv.at[1, src], (q, mych),
        )

    def gate_copies(q, src):
        return (
            send_to(
                proj.at[0:1, :, lanes_of(q)], pin.at[0:1, tile(src), :],
                in_send.at[1, q], in_recv.at[1, src], (q, mych),
            ),
            near_copies(q, src)[1],
        )

    for q in everyone:
        tap_copy(q, me).start()

    @pl.when(me == hs - 1)
    def _():
        for q in far:
            halo_copy(q, me, LANES - 16).start()

    @pl.when(me == hs)
    def _():
        for q in far:
            halo_copy(q, me, 0).start()

    for i in range(hs):
        @pl.when(half == 0)
        def _():
            mix_copy(far[i], me).start()

        @pl.when(half == 1)
        def _():
            for copy in gate_copies(far[i], me):
                copy.start()

        if i < hs - 1:
            for copy in near_copies(near[i], me):
                copy.start()

    taps[me] = tap_send[mine // group_owners]
    gram[...] = jnp.zeros(gram.shape, jnp.float32)
    for j in range(3):
        for t in range(2):
            wide[j, t, 0:8, :] = jnp.zeros((8, LANES), jnp.float32)
            fgrad[j, t, span : span + 16, :] = jnp.zeros((16, LANES), jnp.float32)
        for k in range(kt):
            gs_acc[j, k] = jnp.zeros((8, WIDE), jnp.float32)
    for q in everyone:
        tap_copy(q, q).wait_recv()
    build_filters(taps, ns, low_hi, low_lo, up_hi, up_lo)
    for copy in own[1:]:
        copy.wait()
    halo_copy(far[0], 0, 0).wait_recv()

    sides = [slice(0, LANES), slice(LANES, WIDE)]

    def to_wide(j, first, rows):
        for t, lanes in enumerate(sides):
            wide[j, t, pl.ds(first + 8, rows), :] = pin[j, pl.ds(first, rows), lanes].astype(
                jnp.float32
            )

    def feature(j, first, rows):
        sums = []
        for t, lanes in enumerate(sides):
            acc = jnp.zeros((rows, LANES), jnp.float32)
            for k in range(kt):
                shifted = wide[j, t, pl.ds(first + 8 - k, rows), :]
                acc = acc + weight[j, k : k + 1, lanes] * shifted
            sums.append(acc)
        return jnp.concatenate(sums, 1)

    def keep(store, rows, value):
        top, rest = split_halves(value)
        store[rows, 0:WIDE] = top
        store[rows, WIDE:] = rest

    def near_block(i, carry):
        b = half * hs + i

        @pl.when(b != me)
        def _():
            for copy in near_copies(b, b):
                copy.wait_recv()

        base = pl.multiple_of(b * LANES, LANES)
        for j in range(3):
            to_wide(j, base, LANES)
        def piece(p, carry):
            first = pl.multiple_of(base + p * ROWS, ROWS)
            rows = pl.ds(first, ROWS)
            kept = pl.ds(pl.multiple_of(i * LANES + p * ROWS, ROWS), ROWS)
            one, two = feature(1, first, ROWS), feature(2, first, ROWS)
            feat[0, kept, :] = one
            feat[1, kept, :] = two
            keep(mixed, rows, one * two)
            keep(gated, rows, cin[rows, :].astype(jnp.float32) * feature(0, first, ROWS))
            return carry

        return lax.fori_loop(0, LANES // ROWS, piece, carry)

    def far_block(early, i, carry):
        b = (1 - half) * hs + i
        base = pl.multiple_of(b * LANES, LANES)
        for copy in gate_copies(b, b) if early else (mix_copy(b, b),):
            copy.wait_recv()
        for j in (0,) if early else (1, 2):
            to_wide(j, base, LANES)
        def piece(p, carry):
            first = pl.multiple_of(base + p * ROWS, ROWS)
            rows = pl.ds(first, ROWS)
            if early:
                keep(gated, rows, cin[rows, :].astype(jnp.float32) * feature(0, first, ROWS))
            else:
                keep(mixed, rows, feature(1, first, ROWS) * feature(2, first, ROWS))
            return carry

        return lax.fori_loop(0, LANES // ROWS, piece, carry)

    flip = (
        lax.broadcasted_iota(jnp.int32, (WIDE, WIDE), 0)
        + lax.broadcasted_iota(jnp.int32, (WIDE, WIDE), 1)
        == WIDE - 1
    ).astype(jnp.float32).astype(jnp.bfloat16)

    def add_gram(pairs, lanes):
        for b in sorted({b for b, _ in pairs}):
            left = dot32(flip, mixed[b * WIDE : (b + 1) * WIDE, :]).astype(jnp.bfloat16)
            left_top, left_rest = left[:, :WIDE][:, lanes], left[:, WIDE:][:, lanes]
            for c in sorted(c for first, c in pairs if first == b):
                right = gated[c * WIDE : (c + 1) * WIDE, :]
                right_top, right_rest = right[:, :WIDE][:, lanes], right[:, WIDE:][:, lanes]
                cols = slice((c - b) * WIDE, (c - b + 1) * WIDE)
                gram[:, cols] += (
                    dot32_t(left_top, right_top)
                    + dot32_t(left_rest, right_top)
                    + dot32_t(left_top, right_rest)
                )

    def conv_of(b, first, last, rows=WIDE):
        start = total - (b + 1) * WIDE
        cols = slice(start + first, start + last)
        return dot_three(low_hi[:rows, cols], low_lo[:rows, cols], mixed[first:last, :])

    def corr_of(a, first, last, rows=WIDE):
        cols = slice(first - a * WIDE, last - a * WIDE)
        return dot_three(up_hi[:rows, cols], up_lo[:rows, cols], gated[first:last, :])

    def keep_grad(j, rows, value):
        for t, lanes in enumerate(sides):
            fgrad[j, t, rows, :] = value[:, lanes]

    def grads_of(rows, conv=None, corr=None):
        if conv is not None:
            at = pl.ds(own_base + rows.start, rows.stop - rows.start)
            keep_grad(0, rows, cin[at, :].astype(jnp.float32) * conv)
        if corr is not None:
            keep_grad(1, rows, corr * feat[1, rows, :])
            keep_grad(2, rows, corr * feat[0, rows, :])

    per = span // WIDE
    local_rows = [slice(b * WIDE, (b + 1) * WIDE) for b in range(per)]
    edge = slice(span, span + 16)
    near_pairs = [(b, c) for b in range(per) for c in range(b, per)]
    far_pairs = [(b, c) for b in range(per) for c in range(per, 2 * per)]

    @pl.when(half == 0)
    def _():
        for j in (1, 2):
            for t, lanes in enumerate(sides):
                wide[j, t, 8 + span : 8 + span + 16, :] = halo[j, :, lanes].astype(jnp.float32)
        lax.fori_loop(0, hs, near_block, 0)
        mixed[span : span + LANES, :] = jnp.zeros((LANES, 2 * WIDE), jnp.bfloat16)
        one, two = feature(1, span, 16), feature(2, span, 16)
        feat[0, edge, :] = one
        feat[1, edge, :] = two
        keep(mixed, edge, one * two)
        for b in range(per):
            grads_of(local_rows[b], conv=conv_of(b, 0, (b + 1) * WIDE))
            part[local_rows[b], :] = corr_of(b, b * WIDE, span)
        part_edge[...] = conv_of(per, 0, span + LANES, 16)
        add_gram(near_pairs, slice(0, WIDE))
        lax.fori_loop(0, hs, functools.partial(far_block, True), 0)
        for b in range(per):
            grads_of(local_rows[b], corr=part[local_rows[b], :] + corr_of(b, span, total))
        grads_of(edge, conv=part_edge[...], corr=corr_of(per, span, total, 16))

    @pl.when(half == 1)
    def _():
        for j in range(3):
            for t, lanes in enumerate(sides):
                wide[j, t, 8 + span - 16 : 8 + span, :] = halo[j, :, lanes].astype(jnp.float32)
        lax.fori_loop(0, hs, near_block, 0)
        for b in range(per):
            grads_of(local_rows[b], corr=corr_of(per + b, span + b * WIDE, total))
            part[local_rows[b], :] = conv_of(per + b, span, span + (b + 1) * WIDE)
        add_gram([(per + b, per + c) for b, c in near_pairs], slice(0, WIDE))
        lax.fori_loop(0, hs, functools.partial(far_block, False), 0)
        for b in range(per):
            grads_of(local_rows[b], conv=part[local_rows[b], :] + conv_of(per + b, 0, span))

    def finish_block(i, carry):
        b = lax.rem(mine + 1 + i, hs)
        base = pl.multiple_of(b * LANES, LANES)

        def piece(p, carry):
            first = pl.multiple_of(base + p * ROWS, ROWS)
            for j in range(3):
                for t, lanes in enumerate(sides):
                    acc = jnp.zeros((ROWS, LANES), jnp.float32)
                    source = wide[j, t, pl.ds(own_base + first + 8, ROWS), :]
                    for k in range(kt):
                        shifted = fgrad[j, t, pl.ds(first + k, ROWS), :]
                        acc = acc + weight[j, k : k + 1, lanes] * shifted
                        terms = (shifted * source).reshape(ROWS // 8, 8, LANES)
                        gs_acc[j, k, :, lanes] += jnp.sum(terms, 0)
                    gp_send[j, pl.ds(first, ROWS), lanes] = acc.astype(jnp.bfloat16)
            return carry

        lax.fori_loop(0, LANES // ROWS, piece, 0)

        @pl.when(b != mine)
        def _():
            q = half * hs + b
            send_to(
                gp_send.at[:, tile(b), :], gp_out.at[:, :, lanes_of(me)],
                gp_ssem.at[q], gp_rsem.at[me], (q, mych),
            ).start()

        return carry

    lax.fori_loop(0, hs, finish_block, 0)

    short_scale = 1.0 / math.sqrt(total)
    for j in range(3):
        lines = [jnp.sum(gs_acc[j, k], 0, keepdims=True) for k in range(kt)]
        lines += [jnp.zeros((1, WIDE), jnp.float32)] * (8 - kt)
        gs_send[j] = jnp.concatenate(lines, 0) * short_scale
    partner = far[0]
    pair = send_to(gs_send, gs_pair, pair_sem.at[0], pair_sem.at[1], (partner, mych))
    pair.start()
    gp_out[:, :, lanes_of(me)] = gp_send[:, tile(mine), :]

    @pl.when(half == 0)
    def _():
        add_gram(far_pairs, slice(0, LANES))

    @pl.when(half == 1)
    def _():
        add_gram(far_pairs, slice(LANES, WIDE))

    filter_scale = 1.0 / math.sqrt(total * group_owners * WIDE)
    for d, line in enumerate(diagonal_sums(gram, ns)):
        fa_send[d] = jnp.broadcast_to(line * filter_scale, (8, LANES))
    fa_copy = lambda q, src: send_to(
        fa_send.at[q], fa_recv.at[src], fa_ssem.at[q], fa_rsem.at[src], (q, mych)
    )
    for q in everyone:
        fa_copy(q, me).start()
    fa_recv[me] = fa_send[me]

    pair.wait()
    gs_sum[...] = gs_send[...] + gs_pair[...]
    gs_copy = lambda q, src: send_to(
        gs_sum, gs_recv.at[lax.rem(src, hs)], gs_ssem.at[q], gs_rsem.at[src], (q, mych)
    )
    for q in near:
        gs_copy(q, me).start()
    gs_recv[mine] = gs_sum[...]

    for q in everyone:
        fa_copy(q, q).wait_recv()
    for g in range(groups):
        owners = [h * hs + g * group_owners + i for h in range(2) for i in range(group_owners)]
        summed = fa_recv[owners[0]]
        for q in owners[1:]:
            summed = summed + fa_recv[q]
        fb_send[g] = summed
    fb_copy = lambda c, src: send_to(
        fb_send, fb_recv.at[src], fb_ssem.at[c], fb_rsem.at[src], (me, c)
    )
    for _, c in ch_peers:
        fb_copy(c, mych).start()
    fb_recv[mych] = fb_send[...]
    for _, c in ch_peers:
        fb_copy(c, c).wait_recv()
    width = LANES // nc
    for c in range(nc):
        for g in range(groups):
            line = fb_recv[c, g]
            piece = line[:, 0:width]
            for other in range(1, nc):
                piece = jnp.where(
                    mych == other, line[:, other * width : (other + 1) * width], piece
                )
            at = c * groups + g
            gf_out[at : at + 1, :] = piece[0:1, :]

    for q in near:
        gs_copy(q, q).wait_recv()
    for q in range(hs):
        for j in range(3):
            gs_out[j, :, q * WIDE : (q + 1) * WIDE] = gs_recv[q, j, 0:kt, :]

    for q in everyone:
        tap_copy(q, me).wait_send()
        fa_copy(q, me).wait_send()
    for q in near:
        for copy in near_copies(q, me):
            copy.wait_send()
        gs_copy(q, me).wait_send()
        send_to(
            gp_send.at[:, tile(lax.rem(q, hs)), :], gp_out.at[:, :, lanes_of(q)],
            gp_ssem.at[q], gp_rsem.at[q], (q, mych),
        ).wait()
    for _, c in ch_peers:
        fb_copy(c, mych).wait_send()

    @pl.when(half == 0)
    def _():
        for q in far:
            mix_copy(q, me).wait_send()

    @pl.when(half == 1)
    def _():
        for q in far:
            for copy in gate_copies(q, me):
                copy.wait_send()

    @pl.when((me == hs - 1) | (me == hs))
    def _():
        for q in far:
            halo_copy(q, me, 0).wait_send()


def resident(projected, cotangent, short_weight, long_filter):
    row_count, streams, chan_count = projected.shape
    kt = short_weight.shape[1]
    groups = long_filter.shape[0]
    ns, nc = lax.axis_size("seq"), lax.axis_size("ch")
    total = row_count * ns
    span = total // 2
    f32, bf16 = jnp.float32, jnp.bfloat16
    dma = pltpu.SemaphoreType.DMA
    vmem = pl.BlockSpec(memory_space=pltpu.VMEM)
    anywhere = pl.BlockSpec(memory_space=pl.ANY)
    grad_proj, grad_short, grad_filter = pl.pallas_call(
        functools.partial(resident_kernel, ns, nc, kt, groups),
        out_shape=(
            jax.ShapeDtypeStruct((streams, row_count, chan_count), bf16),
            jax.ShapeDtypeStruct((streams, kt, chan_count), f32),
            jax.ShapeDtypeStruct((groups * nc, row_count // nc), f32),
        ),
        in_specs=[anywhere] * 4,
        out_specs=(vmem, vmem, vmem),
        scratch_shapes=[
            pltpu.VMEM((3, kt, WIDE), f32),
            pltpu.VMEM((groups, LANES), f32),
            pltpu.VMEM((3, total, WIDE), bf16),
            pltpu.VMEM((total, WIDE), bf16),
            pltpu.VMEM((3, 16, WIDE), bf16),
            pltpu.VMEM((3, 2, total + 8, LANES), f32),
            pltpu.VMEM((2, span + 16, WIDE), f32),
            pltpu.VMEM((total, 2 * WIDE), bf16),
            pltpu.VMEM((total, 2 * WIDE), bf16),
            pltpu.VMEM((span, WIDE), f32),
            pltpu.VMEM((16, WIDE), f32),
            pltpu.VMEM((3, 2, span + 16, LANES), f32),
            pltpu.VMEM((3, span, WIDE), bf16),
            pltpu.VMEM((groups, 8, LANES), f32),
            pltpu.VMEM((ns, 8, LANES), f32),
            pltpu.VMEM((WIDE, total), bf16),
            pltpu.VMEM((WIDE, total), bf16),
            pltpu.VMEM((WIDE, total), bf16),
            pltpu.VMEM((WIDE, total), bf16),
            pltpu.VMEM((WIDE, total), f32),
            pltpu.VMEM((ns, 8, LANES), f32),
            pltpu.VMEM((ns, 8, LANES), f32),
            pltpu.VMEM((groups, 8, LANES), f32),
            pltpu.VMEM((nc, groups, 8, LANES), f32),
            pltpu.VMEM((3, 8, 8, WIDE), f32),
            pltpu.VMEM((3, 8, WIDE), f32),
            pltpu.VMEM((3, 8, WIDE), f32),
            pltpu.VMEM((3, 8, WIDE), f32),
            pltpu.VMEM((ns // 2, 3, 8, WIDE), f32),
            dma((4,)),
            dma((4, ns)), dma((4, ns)),
            dma((ns,)), dma((ns,)),
            dma((ns,)), dma((ns,)),
            dma((ns,)), dma((ns,)),
            dma((nc,)), dma((nc,)),
            dma((2,)),
        ],
        compiler_params=pltpu.CompilerParams(
            collective_id=0, has_side_effects=True, vmem_limit_bytes=48 * 1024 * 1024
        ),
    )(jnp.transpose(projected, (1, 0, 2)), cotangent, short_weight, long_filter)
    return jnp.transpose(grad_proj, (1, 0, 2)), grad_short, grad_filter


def spread(projected, cotangent, short_weight, long_filter):
    tap_count = short_weight.shape[1]
    row_count = projected.shape[0]
    margin = tap_count - 1
    front_rows = passed_along(projected[row_count - margin :], "seq", 1)
    extended = jnp.concatenate([front_rows, projected], 0)
    features = featurize(extended, short_weight, row_count)
    grad_out = cotangent.astype(jnp.float32)
    mixed_input = features[:, 1] * features[:, 2]
    gated_grad = grad_out * features[:, 0]
    conv_out, corr_out, filt_grad = sequence_plan(mixed_input, gated_grad, long_filter)
    token_count = row_count * lax.axis_size("seq")
    group_width = mixed_input.shape[1] // long_filter.shape[0]
    scaled_grad = filt_grad * (1.0 / math.sqrt(token_count * group_width))
    owned_grad = lax.all_to_all(scaled_grad, "ch", split_axis=1, concat_axis=0, tiled=True)
    feat_grad = jnp.stack(
        [grad_out * conv_out, corr_out * features[:, 2], corr_out * features[:, 1]], 1
    )
    next_rows = passed_along(feat_grad[:margin].astype(jnp.bfloat16), "seq", -1).astype(jnp.float32)
    extended_grad = jnp.concatenate([feat_grad, next_rows], 0)
    grad_proj = jnp.zeros(feat_grad.shape, jnp.float32)
    for offset in range(tap_count):
        grad_proj = (
            grad_proj + short_weight[:, offset, :] * extended_grad[offset : offset + row_count]
        )
    short_terms = []
    for offset in range(tap_count):
        first_row = margin - offset
        short_terms.append(
            jnp.sum(feat_grad * extended[first_row : first_row + row_count].astype(jnp.float32), 0)
        )
    grad_short = lax.psum(jnp.stack(short_terms, 1), "seq") * (1.0 / math.sqrt(token_count))
    return (grad_proj.astype(jnp.bfloat16), grad_short, owned_grad)


def local(projected, cotangent, short_weight, long_filter):
    row_count, _, chan_count = projected.shape
    seq_count = lax.axis_size("seq")
    group_width = chan_count // long_filter.shape[0]
    fits = (
        row_count == LANES
        and seq_count % 4 == 0
        and chan_count == WIDE * (seq_count // 2)
        and group_width % WIDE == 0
        and short_weight.shape[1] <= 8
    )
    plan = resident if fits else spread
    return plan(projected, cotangent, short_weight, long_filter)


def solution(mesh):
    return jax.shard_map(
        local,
        mesh=mesh,
        in_specs=(P("seq", None, "ch"), P("seq", "ch"), P(None, None, "ch"), P("ch", "seq")),
        out_specs=(P("seq", None, "ch"), P(None, None, "ch"), P(None, ("seq", "ch"))),
        check_vma=False,
    )
```

```python
import functools
import math

import jax
import jax.numpy as jnp
from jax import lax
from jax.experimental import pallas as pl
from jax.experimental.pallas import tpu as pltpu
from jax.sharding import PartitionSpec as P

highest = lax.Precision.HIGHEST
MESH = pl.DeviceIdType.MESH
LANES = 128
WIDE = 256
ROWS = 64


def passed_along(block, axis, distance):
    devices = range(lax.axis_size(axis))
    route = [(i - distance, i) for i in devices if i - distance in devices]
    return lax.ppermute(block, axis, route)


def einsum_high(form, table, operand):
    return jnp.einsum(form, table, operand, precision=highest)


def angle_table(first, second, length):
    product = first[:, None] * second[None, :] % length
    radians = product.astype(jnp.float32) * (2.0 * math.pi / length)
    return (jnp.cos(radians), jnp.sin(radians))


def complex_dft(cosine, sine, real_part, imag_part, joined, sign):
    table = jnp.stack(
        [jnp.stack([cosine, -sign * sine], 0), jnp.stack([sign * sine, cosine], 0)], 0
    )
    stacked = jnp.stack([real_part, imag_part], 0)
    result = jnp.einsum(joined, table, stacked, precision=highest)
    return (result[0], result[1])


def rotate(real_part, imag_part, cosine, sine, sign):
    return (
        real_part * cosine - sign * imag_part * sine,
        imag_part * cosine + sign * real_part * sine,
    )


def combine(mixed_re, mixed_im, grad_re, grad_im, filt_re, filt_im):
    conv_re = filt_re * mixed_re - filt_im * mixed_im
    conv_im = filt_re * mixed_im + filt_im * mixed_re
    corr_re = filt_re * grad_re + filt_im * grad_im
    corr_im = filt_re * grad_im - filt_im * grad_re
    cross_re = mixed_re * grad_re + mixed_im * grad_im
    cross_im = mixed_re * grad_im - mixed_im * grad_re
    return (conv_re - corr_im, conv_im + corr_re, cross_re, cross_im)


def featurize(extended, weights, row_count):
    tap_count = weights.shape[1]
    accumulated = jnp.zeros((row_count,) + extended.shape[1:], jnp.float32)
    for offset in range(tap_count):
        first_row = tap_count - 1 - offset
        accumulated = accumulated + weights[:, offset, :] * extended[
            first_row : first_row + row_count
        ].astype(jnp.float32)
    return accumulated


def transpose_pair(signals, filters):
    return (
        lax.all_to_all(signals, "seq", split_axis=0, concat_axis=1, tiled=True),
        lax.all_to_all(filters, "seq", split_axis=0, concat_axis=1, tiled=True),
    )


def sequence_plan(mixed_input, gated_grad, long_filter):
    row_count, chan_count = mixed_input.shape
    group_count = long_filter.shape[0]
    seq_count = lax.axis_size("seq")
    seq_index = lax.axis_index("seq")
    per_block = row_count // seq_count
    fft_length = 2 * row_count * seq_count
    freq_index = jnp.arange(2 * seq_count, dtype=jnp.int32)
    block_index = jnp.arange(seq_count, dtype=jnp.int32)
    row_index = jnp.arange(row_count, dtype=jnp.int32)
    signals = jnp.stack([mixed_input, gated_grad], 1)[:, None]
    filters = jnp.transpose(long_filter)[:, None]
    sig_cols, filt_cols = transpose_pair(signals, filters)
    cos_one, sin_one = angle_table(freq_index, block_index, 2 * seq_count)
    sig_re = einsum_high("kb,abxc->kaxc", cos_one, sig_cols)
    sig_im = -einsum_high("kb,abxc->kaxc", sin_one, sig_cols)
    filt_re = einsum_high("kb,abg->kag", cos_one, filt_cols)
    filt_im = -einsum_high("kb,abg->kag", sin_one, filt_cols)
    positions = seq_index * per_block + jnp.arange(per_block, dtype=jnp.int32)
    cos_twist, sin_twist = angle_table(freq_index, positions, fft_length)
    sig_re, sig_im = rotate(
        sig_re, sig_im, cos_twist[:, :, None, None], sin_twist[:, :, None, None], -1.0
    )
    filt_re, filt_im = rotate(filt_re, filt_im, cos_twist[:, :, None], sin_twist[:, :, None], -1.0)
    sig_rows, filt_rows = transpose_pair(
        jnp.stack([sig_re, sig_im], 2), jnp.stack([filt_re, filt_im], 2)
    )
    cos_two, sin_two = angle_table(row_index, row_index, row_count)
    spec_re, spec_im = complex_dft(
        cos_two, sin_two, sig_rows[:, :, 0], sig_rows[:, :, 1], "pqka,qjaxc->pjkxc", -1.0
    )
    hspec_re, hspec_im = complex_dft(
        cos_two, sin_two, filt_rows[:, :, 0], filt_rows[:, :, 1], "pqka,qjag->pjkg", -1.0
    )
    leading = spec_re.shape[:2]
    group_shape = leading + (group_count, chan_count // group_count)
    wave_re, wave_im, cross_re, cross_im = combine(
        spec_re[:, :, 0].reshape(group_shape),
        spec_im[:, :, 0].reshape(group_shape),
        spec_re[:, :, 1].reshape(group_shape),
        spec_im[:, :, 1].reshape(group_shape),
        hspec_re[..., None],
        hspec_im[..., None],
    )
    wave_re = wave_re.reshape(leading + (chan_count,))
    wave_im = wave_im.reshape(leading + (chan_count,))
    cross_re = jnp.sum(cross_re, -1)
    cross_im = jnp.sum(cross_im, -1)
    back_re, back_im = complex_dft(cos_two, sin_two, wave_re, wave_im, "pqak,qjkc->pajc", 1.0)
    cback_re, cback_im = complex_dft(cos_two, sin_two, cross_re, cross_im, "pqak,qjkg->pajg", 1.0)
    pair_freq = seq_index * 2 + jnp.arange(2, dtype=jnp.int32)
    cos_back, sin_back = angle_table(row_index, pair_freq, fft_length)
    back_re, back_im = rotate(back_re, back_im, cos_back[:, :, None], sin_back[:, :, None], 1.0)
    cback_re, cback_im = rotate(cback_re, cback_im, cos_back[:, :, None], sin_back[:, :, None], 1.0)
    wave_cols, cross_cols = transpose_pair(
        jnp.stack([back_re, back_im], 2), jnp.stack([cback_re, cback_im], 2)
    )
    cos_three, sin_three = angle_table(block_index, freq_index, 2 * seq_count)
    time_re, time_im = complex_dft(
        cos_three, sin_three, wave_cols[:, :, 0], wave_cols[:, :, 1], "pqbk,qakc->pbac", 1.0
    )
    cross_time = einsum_high("bk,akg->bag", cos_three, cross_cols[:, :, 0]) - einsum_high(
        "bk,akg->bag", sin_three, cross_cols[:, :, 1]
    )
    inverse_scale = 1.0 / fft_length
    wave_out, cross_out = transpose_pair(
        jnp.stack([time_re, time_im], 2) * inverse_scale, cross_time * inverse_scale
    )
    return (wave_out[0, :, 0], wave_out[0, :, 1], jnp.transpose(cross_out[0]))


def split_halves(value):
    top = value.astype(jnp.bfloat16)
    rest = (value - top.astype(jnp.float32)).astype(jnp.bfloat16)
    return top, rest


def dot32(left, right):
    return jnp.dot(left, right, preferred_element_type=jnp.float32)


def dot32_t(left, right):
    return lax.dot_general(
        left, right, (((1,), (1,)), ((), ())), preferred_element_type=jnp.float32
    )


def tile(index, width=LANES):
    return pl.ds(pl.multiple_of(index * width, width), width)


def send_to(src, dst, send_sem, recv_sem, peer):
    return pltpu.make_async_remote_copy(
        src_ref=src,
        dst_ref=dst,
        send_sem=send_sem,
        recv_sem=recv_sem,
        device_id=peer,
        device_id_type=MESH,
    )


def build_filters(taps, ns, low_hi, low_lo, up_hi, up_lo):
    row = lax.broadcasted_iota(jnp.int32, (LANES, LANES), 0)
    col = lax.broadcasted_iota(jnp.int32, (LANES, LANES), 1)
    flip = (row + col == LANES - 1).astype(jnp.float32)
    zero = jnp.zeros((LANES, LANES), jnp.float32)
    zero16 = zero.astype(jnp.bfloat16)
    flipped = jnp.dot(
        taps[...].reshape(ns * 8, LANES), flip, precision=highest,
        preferred_element_type=jnp.float32,
    )
    last_up, last_low = zero, zero
    top = ns - WIDE // LANES
    low_hi[:, (ns - 1) * LANES :] = jnp.concatenate([zero16, zero16], 0)
    low_lo[:, (ns - 1) * LANES :] = jnp.concatenate([zero16, zero16], 0)
    up_hi[LANES:, :LANES] = zero16
    up_lo[LANES:, :LANES] = zero16
    for d in range(ns):
        forward = jnp.concatenate([taps[d]] * (LANES // 8), 0)
        back = jnp.concatenate([flipped[d * 8 : d * 8 + 8]] * (LANES // 8), 0)
        forward = pltpu.roll(forward, 0, 1, stride=1, stride_axis=0)
        back = pltpu.roll(back, 1, 1, stride=1, stride_axis=0)
        up = split_halves(jnp.where(col >= row, forward, last_up))
        low = split_halves(jnp.where(row >= col, back, last_low))
        last_up, last_low = forward, back
        for u in range(WIDE // LANES):
            v = d + u
            if v < ns:
                up_hi[u * LANES : (u + 1) * LANES, v * LANES : (v + 1) * LANES] = up[0]
                up_lo[u * LANES : (u + 1) * LANES, v * LANES : (v + 1) * LANES] = up[1]
            v = top + u - d
            if 0 <= v < ns:
                low_hi[u * LANES : (u + 1) * LANES, v * LANES : (v + 1) * LANES] = low[0]
                low_lo[u * LANES : (u + 1) * LANES, v * LANES : (v + 1) * LANES] = low[1]


def diagonal_sums(gram, ns):
    row = lax.broadcasted_iota(jnp.int32, (LANES, LANES), 0)
    col = lax.broadcasted_iota(jnp.int32, (LANES, LANES), 1)
    turned = []
    for d in range(ns):
        block = gram[LANES:, d * LANES : (d + 1) * LANES]
        if d + 1 < ns:
            block = block + gram[:LANES, (d + 1) * LANES : (d + 2) * LANES]
        turned.append(pltpu.roll(block, 1, 1, stride=1, stride_axis=0))
    turned.append(jnp.zeros((LANES, LANES), jnp.float32))
    return [
        jnp.sum(jnp.where(col <= row, turned[d], turned[d + 1]), 0, keepdims=True)
        for d in range(ns)
    ]


def dot_three(hi, lo, signal):
    width = signal.shape[1] // 2
    both = dot32(hi, signal)
    return both[:, :width] + both[:, width:] + dot32(lo, signal[:, :width])


def resident_kernel(
    ns, nc, kt, groups,
    proj, cot, weight_in, filt_in,
    gp_out, gs_out, gf_out,
    weight, filt, pin, cin, halo, wide, feat, mixed, gated, part, part_edge, fgrad, gp_send,
    tap_send, taps, low_hi, low_lo, up_hi, up_lo, gram,
    fa_send, fa_recv, fb_send, fb_recv, gs_acc, gs_send, gs_pair, gs_sum, gs_recv,
    local_sem, tap_ssem, tap_rsem, in_send, in_recv, gp_ssem, gp_rsem, gs_ssem, gs_rsem,
    fa_ssem, fa_rsem, fb_ssem, fb_rsem, pair_sem,
):
    me = lax.axis_index("seq")
    mych = lax.axis_index("ch")
    hs = ns // 2
    total = ns * LANES
    span = total // 2
    half = me // hs
    mine = lax.rem(me, hs)
    own_base = pl.multiple_of(half * span, span)
    group_owners = hs // groups
    near = [half * hs + lax.rem(mine + i, hs) for i in range(1, hs)]
    far = [(1 - half) * hs + lax.rem(mine + i, hs) for i in range(hs)]
    everyone = near + far
    ch_peers = [(me, lax.rem(mych + i, nc)) for i in range(1, nc)]
    lanes_of = lambda q, t: tile(lax.rem(q, hs) * 2 + t)

    own = [
        pltpu.make_async_copy(filt_in, filt, local_sem.at[0]),
    ]
    for t in range(2):
        lanes, at = lanes_of(me, t), tile(me)
        own += [
            pltpu.make_async_copy(
                weight_in.at[:, :, lanes], weight.at[t], local_sem.at[1 + 3 * t]
            ),
            pltpu.make_async_copy(
                proj.at[:, :, lanes], pin.at[t, :, at, :], local_sem.at[2 + 3 * t]
            ),
            pltpu.make_async_copy(cot.at[:, lanes], cin.at[t, at, :], local_sem.at[3 + 3 * t]),
        ]
    for copy in own:
        copy.start()
    barrier = pltpu.get_barrier_semaphore()
    for q in everyone:
        pl.semaphore_signal(barrier, inc=1, device_id=(q, mych), device_id_type=MESH)
    for peer in ch_peers:
        pl.semaphore_signal(barrier, inc=1, device_id=peer, device_id_type=MESH)
    own[0].wait()
    for g in range(groups):
        tap_send[g] = jnp.broadcast_to(filt[g : g + 1, :], (8, LANES))
    pl.semaphore_wait(barrier, ns + nc - 2)

    def tap_copy(q, src):
        return send_to(
            tap_send.at[lax.rem(q, hs) // group_owners], taps.at[src],
            tap_ssem.at[q], tap_rsem.at[src], (q, mych),
        )

    def halo_copy(q, t, src, first):
        return send_to(
            proj.at[:, pl.ds(first, 16), lanes_of(q, t)], halo.at[t],
            in_send.at[t, 2, q], in_recv.at[t, 2, 0], (q, mych),
        )

    def stream_copy(q, t, src, streams):
        return send_to(
            proj.at[streams, :, lanes_of(q, t)], pin.at[t, streams, tile(src), :],
            in_send.at[t, 0, q], in_recv.at[t, 0, src], (q, mych),
        )

    def cot_copy(q, t, src):
        return send_to(
            cot.at[:, lanes_of(q, t)], cin.at[t, tile(src), :],
            in_send.at[t, 1, q], in_recv.at[t, 1, src], (q, mych),
        )

    def near_copies(q, t, src):
        return (stream_copy(q, t, src, slice(0, 3)), cot_copy(q, t, src))

    def mix_copy(q, t, src):
        return stream_copy(q, t, src, slice(1, 3))

    def gate_copies(q, t, src):
        return (stream_copy(q, t, src, slice(0, 1)), cot_copy(q, t, src))

    for q in everyone:
        tap_copy(q, me).start()

    @pl.when(me == hs - 1)
    def _():
        for t in range(2):
            for q in far:
                halo_copy(q, t, me, LANES - 16).start()

    @pl.when(me == hs)
    def _():
        for t in range(2):
            for q in far:
                halo_copy(q, t, me, 0).start()

    for t in range(2):
        for i in range(hs):
            @pl.when(half == 0)
            def _():
                mix_copy(far[i], t, me).start()

            @pl.when(half == 1)
            def _():
                for copy in gate_copies(far[i], t, me):
                    copy.start()

            if i < hs - 1:
                for copy in near_copies(near[i], t, me):
                    copy.start()

    taps[me] = tap_send[mine // group_owners]
    gram[...] = jnp.zeros(gram.shape, jnp.float32)
    for j in range(3):
        wide[j, 0:8, :] = jnp.zeros((8, LANES), jnp.float32)
        fgrad[j, span : span + 16, :] = jnp.zeros((16, LANES), jnp.float32)
        for t in range(2):
            for k in range(kt):
                gs_acc[t, j, k] = jnp.zeros((8, LANES), jnp.float32)
    for q in everyone:
        tap_copy(q, q).wait_recv()
    build_filters(taps, ns, low_hi, low_lo, up_hi, up_lo)
    for copy in own[1:]:
        copy.wait()
    for t in range(2):
        halo_copy(far[0], t, 0, 0).wait_recv()

    def to_wide(t, j, first):
        wide[j, pl.ds(first + 8, LANES), :] = pin[t, j, pl.ds(first, LANES), :].astype(jnp.float32)

    def feature(t, j, first, rows):
        acc = jnp.zeros((rows, LANES), jnp.float32)
        for k in range(kt):
            acc = acc + weight[t, j, k : k + 1, :] * wide[j, pl.ds(first + 8 - k, rows), :]
        return acc

    def keep(store, rows, value):
        top, rest = split_halves(value)
        store[rows, 0:LANES] = top
        store[rows, LANES:] = rest

    def near_block(t, i, carry):
        b = half * hs + i

        @pl.when(b != me)
        def _():
            for copy in near_copies(b, t, b):
                copy.wait_recv()

        base = pl.multiple_of(b * LANES, LANES)
        for j in range(3):
            to_wide(t, j, base)
        for p in range(LANES // ROWS):
            first = base + p * ROWS
            rows = pl.ds(first, ROWS)
            kept = pl.ds(pl.multiple_of(i * LANES, LANES) + p * ROWS, ROWS)
            one, two = feature(t, 1, first, ROWS), feature(t, 2, first, ROWS)
            feat[0, kept, :] = one
            feat[1, kept, :] = two
            keep(mixed, rows, one * two)
            keep(gated, rows, cin[t, rows, :].astype(jnp.float32) * feature(t, 0, first, ROWS))
        return carry

    def far_block(early, t, i, carry):
        b = (1 - half) * hs + i
        base = pl.multiple_of(b * LANES, LANES)
        for copy in gate_copies(b, t, b) if early else (mix_copy(b, t, b),):
            copy.wait_recv()
        for j in (0,) if early else (1, 2):
            to_wide(t, j, base)
        for p in range(LANES // ROWS):
            first = base + p * ROWS
            rows = pl.ds(first, ROWS)
            if early:
                gate = feature(t, 0, first, ROWS)
                keep(gated, rows, cin[t, rows, :].astype(jnp.float32) * gate)
            else:
                keep(mixed, rows, feature(t, 1, first, ROWS) * feature(t, 2, first, ROWS))
        return carry

    flip = (
        lax.broadcasted_iota(jnp.int32, (WIDE, WIDE), 0)
        + lax.broadcasted_iota(jnp.int32, (WIDE, WIDE), 1)
        == WIDE - 1
    ).astype(jnp.float32).astype(jnp.bfloat16)

    def add_gram(pairs):
        for b in sorted({b for b, _ in pairs}):
            left = dot32(flip, mixed[b * WIDE : (b + 1) * WIDE, :]).astype(jnp.bfloat16)
            for c in sorted(c for first, c in pairs if first == b):
                right = gated[c * WIDE : (c + 1) * WIDE, :]
                top = right[:, :LANES]
                cols = slice((c - b) * WIDE, (c - b + 1) * WIDE)
                gram[:, cols] += dot32_t(left, jnp.concatenate([top, top], 1)) + dot32_t(
                    left[:, :LANES], right[:, LANES:]
                )

    def conv_of(b, first, last, rows=WIDE):
        start = total - (b + 1) * WIDE
        cols = slice(start + first, start + last)
        return dot_three(low_hi[:rows, cols], low_lo[:rows, cols], mixed[first:last, :])

    def corr_of(a, first, last, rows=WIDE):
        cols = slice(first - a * WIDE, last - a * WIDE)
        return dot_three(up_hi[:rows, cols], up_lo[:rows, cols], gated[first:last, :])

    def grads_of(t, rows, conv=None, corr=None):
        if conv is not None:
            at = pl.ds(own_base + rows.start, rows.stop - rows.start)
            fgrad[0, rows, :] = cin[t, at, :].astype(jnp.float32) * conv
        if corr is not None:
            fgrad[1, rows, :] = corr * feat[1, rows, :]
            fgrad[2, rows, :] = corr * feat[0, rows, :]

    per = span // WIDE
    local_rows = [slice(b * WIDE, (b + 1) * WIDE) for b in range(per)]
    edge = slice(span, span + 16)
    near_pairs = [(b, c) for b in range(per) for c in range(b, per)]
    far_pairs = [(b, c) for b in range(per) for c in range(per, 2 * per)]

    def early_part(t):
        for j in (1, 2):
            wide[j, 8 + span : 8 + span + 16, :] = halo[t, j].astype(jnp.float32)
        lax.fori_loop(0, hs, functools.partial(near_block, t), 0)
        mixed[span : span + LANES, :] = jnp.zeros((LANES, WIDE), jnp.bfloat16)
        one, two = feature(t, 1, span, 16), feature(t, 2, span, 16)
        feat[0, edge, :] = one
        feat[1, edge, :] = two
        keep(mixed, edge, one * two)
        for b in range(per):
            grads_of(t, local_rows[b], conv=conv_of(b, 0, (b + 1) * WIDE))
            part[local_rows[b], :] = corr_of(b, b * WIDE, span)
        part_edge[...] = conv_of(per, 0, span + LANES, 16)
        add_gram(near_pairs)
        lax.fori_loop(0, hs, functools.partial(far_block, True, t), 0)
        for b in range(per):
            grads_of(t, local_rows[b], corr=part[local_rows[b], :] + corr_of(b, span, total))
        grads_of(t, edge, conv=part_edge[...], corr=corr_of(per, span, total, 16))

    def late_part(t):
        for j in range(3):
            wide[j, 8 + span - 16 : 8 + span, :] = halo[t, j].astype(jnp.float32)
        lax.fori_loop(0, hs, functools.partial(near_block, t), 0)
        for b in range(per):
            grads_of(t, local_rows[b], corr=corr_of(per + b, span + b * WIDE, total))
            part[local_rows[b], :] = conv_of(per + b, span, span + (b + 1) * WIDE)
        add_gram([(per + b, per + c) for b, c in near_pairs])
        lax.fori_loop(0, hs, functools.partial(far_block, False, t), 0)
        for b in range(per):
            grads_of(t, local_rows[b], conv=part[local_rows[b], :] + conv_of(per + b, 0, span))

    def finish_block(t, i, carry):
        b = lax.rem(mine + 1 + i, hs)
        base = pl.multiple_of(b * LANES, LANES)
        for p in range(LANES // ROWS):
            first = base + p * ROWS
            for j in range(3):
                acc = jnp.zeros((ROWS, LANES), jnp.float32)
                source = wide[j, pl.ds(own_base + first + 8, ROWS), :]
                for k in range(kt):
                    shifted = fgrad[j, pl.ds(first + k, ROWS), :]
                    acc = acc + weight[t, j, k : k + 1, :] * shifted
                    terms = (shifted * source).reshape(ROWS // 8, 8, LANES)
                    gs_acc[t, j, k] += jnp.sum(terms, 0)
                gp_send[t, j, pl.ds(first, ROWS), :] = acc.astype(jnp.bfloat16)

        @pl.when(b != mine)
        def _():
            gp_copy(half * hs + b, t, me).start()

        return carry

    def gp_copy(q, t, src):
        return send_to(
            gp_send.at[t, :, tile(lax.rem(q, hs)), :], gp_out.at[:, :, lanes_of(src, t)],
            gp_ssem.at[t, q], gp_rsem.at[t, src], (q, mych),
        )

    def one_tile(t, carry):
        @pl.when(half == 0)
        def _():
            early_part(t)

        @pl.when(half == 1)
        def _():
            late_part(t)

        lax.fori_loop(0, hs, functools.partial(finish_block, t), 0)
        gp_out[:, :, lanes_of(me, t)] = gp_send[t, :, tile(mine), :]

        @pl.when(t == half)
        def _():
            add_gram(far_pairs)

        return carry

    lax.fori_loop(0, 2, one_tile, 0)

    short_scale = 1.0 / math.sqrt(total)
    for t in range(2):
        for j in range(3):
            lines = [jnp.sum(gs_acc[t, j, k], 0, keepdims=True) for k in range(kt)]
            lines += [jnp.zeros((1, LANES), jnp.float32)] * (8 - kt)
            gs_send[t, j] = jnp.concatenate(lines, 0) * short_scale
    partner = far[0]
    pair = send_to(gs_send, gs_pair, pair_sem.at[0], pair_sem.at[1], (partner, mych))
    pair.start()

    filter_scale = 1.0 / math.sqrt(total * group_owners * WIDE)
    for d, line in enumerate(diagonal_sums(gram, ns)):
        fa_send[d] = jnp.broadcast_to(line * filter_scale, (8, LANES))
    fa_copy = lambda q, src: send_to(
        fa_send.at[q], fa_recv.at[src], fa_ssem.at[q], fa_rsem.at[src], (q, mych)
    )
    for q in everyone:
        fa_copy(q, me).start()
    fa_recv[me] = fa_send[me]

    pair.wait()
    gs_sum[...] = gs_send[...] + gs_pair[...]
    gs_copy = lambda q, src: send_to(
        gs_sum, gs_recv.at[lax.rem(src, hs)], gs_ssem.at[q], gs_rsem.at[src], (q, mych)
    )
    for q in near:
        gs_copy(q, me).start()
    gs_recv[mine] = gs_sum[...]

    for q in everyone:
        fa_copy(q, q).wait_recv()
    for g in range(groups):
        owners = [h * hs + g * group_owners + i for h in range(2) for i in range(group_owners)]
        summed = fa_recv[owners[0]]
        for q in owners[1:]:
            summed = summed + fa_recv[q]
        fb_send[g] = summed
    fb_copy = lambda c, src: send_to(
        fb_send, fb_recv.at[src], fb_ssem.at[c], fb_rsem.at[src], (me, c)
    )
    for _, c in ch_peers:
        fb_copy(c, mych).start()
    fb_recv[mych] = fb_send[...]
    for _, c in ch_peers:
        fb_copy(c, c).wait_recv()
    width = LANES // nc
    for c in range(nc):
        for g in range(groups):
            line = fb_recv[c, g]
            piece = line[:, 0:width]
            for other in range(1, nc):
                piece = jnp.where(
                    mych == other, line[:, other * width : (other + 1) * width], piece
                )
            at = c * groups + g
            gf_out[at : at + 1, :] = piece[0:1, :]

    for q in near:
        gs_copy(q, q).wait_recv()
    for q in range(hs):
        for t in range(2):
            lanes = slice((2 * q + t) * LANES, (2 * q + t + 1) * LANES)
            for j in range(3):
                gs_out[j, :, lanes] = gs_recv[q, t, j, 0:kt, :]

    for q in everyone:
        tap_copy(q, me).wait_send()
        fa_copy(q, me).wait_send()
    for q in near:
        gs_copy(q, me).wait_send()
        for t in range(2):
            for copy in near_copies(q, t, me):
                copy.wait_send()
            gp_copy(q, t, me).wait_send()
            gp_copy(q, t, q).wait_recv()
    for _, c in ch_peers:
        fb_copy(c, mych).wait_send()

    @pl.when(half == 0)
    def _():
        for q in far:
            for t in range(2):
                mix_copy(q, t, me).wait_send()

    @pl.when(half == 1)
    def _():
        for q in far:
            for t in range(2):
                for copy in gate_copies(q, t, me):
                    copy.wait_send()

    @pl.when((me == hs - 1) | (me == hs))
    def _():
        for q in far:
            for t in range(2):
                halo_copy(q, t, me, 0).wait_send()


def resident(projected, cotangent, short_weight, long_filter):
    row_count, streams, chan_count = projected.shape
    kt = short_weight.shape[1]
    groups = long_filter.shape[0]
    ns, nc = lax.axis_size("seq"), lax.axis_size("ch")
    total = row_count * ns
    span = total // 2
    f32, bf16 = jnp.float32, jnp.bfloat16
    dma = pltpu.SemaphoreType.DMA
    vmem = pl.BlockSpec(memory_space=pltpu.VMEM)
    anywhere = pl.BlockSpec(memory_space=pltpu.HBM)
    grad_proj, grad_short, grad_filter = pl.pallas_call(
        functools.partial(resident_kernel, ns, nc, kt, groups),
        out_shape=(
            jax.ShapeDtypeStruct((streams, row_count, chan_count), bf16),
            jax.ShapeDtypeStruct((streams, kt, chan_count), f32),
            jax.ShapeDtypeStruct((groups * nc, row_count // nc), f32),
        ),
        in_specs=[anywhere] * 4,
        out_specs=(vmem, vmem, vmem),
        scratch_shapes=[
            pltpu.VMEM((2, 3, kt, LANES), f32),
            pltpu.VMEM((groups, LANES), f32),
            pltpu.VMEM((2, 3, total, LANES), bf16),
            pltpu.VMEM((2, total, LANES), bf16),
            pltpu.VMEM((2, 3, 16, LANES), bf16),
            pltpu.VMEM((3, total + 8, LANES), f32),
            pltpu.VMEM((2, span + 16, LANES), f32),
            pltpu.VMEM((total, WIDE), bf16),
            pltpu.VMEM((total, WIDE), bf16),
            pltpu.VMEM((span, LANES), f32),
            pltpu.VMEM((16, LANES), f32),
            pltpu.VMEM((3, span + 16, LANES), f32),
            pltpu.VMEM((2, 3, span, LANES), bf16),
            pltpu.VMEM((groups, 8, LANES), f32),
            pltpu.VMEM((ns, 8, LANES), f32),
            pltpu.VMEM((WIDE, total), bf16),
            pltpu.VMEM((WIDE, total), bf16),
            pltpu.VMEM((WIDE, total), bf16),
            pltpu.VMEM((WIDE, total), bf16),
            pltpu.VMEM((WIDE, total), f32),
            pltpu.VMEM((ns, 8, LANES), f32),
            pltpu.VMEM((ns, 8, LANES), f32),
            pltpu.VMEM((groups, 8, LANES), f32),
            pltpu.VMEM((nc, groups, 8, LANES), f32),
            pltpu.VMEM((2, 3, 8, 8, LANES), f32),
            pltpu.VMEM((2, 3, 8, LANES), f32),
            pltpu.VMEM((2, 3, 8, LANES), f32),
            pltpu.VMEM((2, 3, 8, LANES), f32),
            pltpu.VMEM((ns // 2, 2, 3, 8, LANES), f32),
            dma((7,)),
            dma((ns,)), dma((ns,)),
            dma((2, 3, ns)), dma((2, 3, ns)),
            dma((2, ns)), dma((2, ns)),
            dma((ns,)), dma((ns,)),
            dma((ns,)), dma((ns,)),
            dma((nc,)), dma((nc,)),
            dma((2,)),
        ],
        compiler_params=pltpu.CompilerParams(
            collective_id=0, has_side_effects=True, vmem_limit_bytes=56 * 1024 * 1024
        ),
    )(jnp.transpose(projected, (1, 0, 2)), cotangent, short_weight, long_filter)
    return jnp.transpose(grad_proj, (1, 0, 2)), grad_short, grad_filter


def spread(projected, cotangent, short_weight, long_filter):
    tap_count = short_weight.shape[1]
    row_count = projected.shape[0]
    margin = tap_count - 1
    front_rows = passed_along(projected[row_count - margin :], "seq", 1)
    extended = jnp.concatenate([front_rows, projected], 0)
    features = featurize(extended, short_weight, row_count)
    grad_out = cotangent.astype(jnp.float32)
    mixed_input = features[:, 1] * features[:, 2]
    gated_grad = grad_out * features[:, 0]
    conv_out, corr_out, filt_grad = sequence_plan(mixed_input, gated_grad, long_filter)
    token_count = row_count * lax.axis_size("seq")
    group_width = mixed_input.shape[1] // long_filter.shape[0]
    scaled_grad = filt_grad * (1.0 / math.sqrt(token_count * group_width))
    owned_grad = lax.all_to_all(scaled_grad, "ch", split_axis=1, concat_axis=0, tiled=True)
    feat_grad = jnp.stack(
        [grad_out * conv_out, corr_out * features[:, 2], corr_out * features[:, 1]], 1
    )
    next_rows = passed_along(feat_grad[:margin].astype(jnp.bfloat16), "seq", -1).astype(jnp.float32)
    extended_grad = jnp.concatenate([feat_grad, next_rows], 0)
    grad_proj = jnp.zeros(feat_grad.shape, jnp.float32)
    for offset in range(tap_count):
        grad_proj = (
            grad_proj + short_weight[:, offset, :] * extended_grad[offset : offset + row_count]
        )
    short_terms = []
    for offset in range(tap_count):
        first_row = margin - offset
        short_terms.append(
            jnp.sum(feat_grad * extended[first_row : first_row + row_count].astype(jnp.float32), 0)
        )
    grad_short = lax.psum(jnp.stack(short_terms, 1), "seq") * (1.0 / math.sqrt(token_count))
    return (grad_proj.astype(jnp.bfloat16), grad_short, owned_grad)


def local(projected, cotangent, short_weight, long_filter):
    row_count, _, chan_count = projected.shape
    seq_count = lax.axis_size("seq")
    group_width = chan_count // long_filter.shape[0]
    fits = (
        row_count == LANES
        and seq_count % 4 == 0
        and chan_count == WIDE * (seq_count // 2)
        and group_width % WIDE == 0
        and short_weight.shape[1] <= 8
    )
    plan = resident if fits else spread
    return plan(projected, cotangent, short_weight, long_filter)


def solution(mesh):
    return jax.shard_map(
        local,
        mesh=mesh,
        in_specs=(P("seq", None, "ch"), P("seq", "ch"), P(None, None, "ch"), P("ch", "seq")),
        out_specs=(P("seq", None, "ch"), P(None, None, "ch"), P(None, ("seq", "ch"))),
        check_vma=False,
    )
```

```python
import functools
import math

import jax
import jax.numpy as jnp
from jax import lax
from jax.experimental import pallas as pl
from jax.experimental.pallas import tpu as pltpu
from jax.sharding import PartitionSpec as P

highest = lax.Precision.HIGHEST
MESH = pl.DeviceIdType.MESH
LANES = 128
WIDE = 256
ROWS = 64


def passed_along(block, axis, distance):
    devices = range(lax.axis_size(axis))
    route = [(i - distance, i) for i in devices if i - distance in devices]
    return lax.ppermute(block, axis, route)


def einsum_high(form, table, operand):
    return jnp.einsum(form, table, operand, precision=highest)


def angle_table(first, second, length):
    product = first[:, None] * second[None, :] % length
    radians = product.astype(jnp.float32) * (2.0 * math.pi / length)
    return (jnp.cos(radians), jnp.sin(radians))


def complex_dft(cosine, sine, real_part, imag_part, joined, sign):
    table = jnp.stack(
        [jnp.stack([cosine, -sign * sine], 0), jnp.stack([sign * sine, cosine], 0)], 0
    )
    stacked = jnp.stack([real_part, imag_part], 0)
    result = jnp.einsum(joined, table, stacked, precision=highest)
    return (result[0], result[1])


def rotate(real_part, imag_part, cosine, sine, sign):
    return (
        real_part * cosine - sign * imag_part * sine,
        imag_part * cosine + sign * real_part * sine,
    )


def combine(mixed_re, mixed_im, grad_re, grad_im, filt_re, filt_im):
    conv_re = filt_re * mixed_re - filt_im * mixed_im
    conv_im = filt_re * mixed_im + filt_im * mixed_re
    corr_re = filt_re * grad_re + filt_im * grad_im
    corr_im = filt_re * grad_im - filt_im * grad_re
    cross_re = mixed_re * grad_re + mixed_im * grad_im
    cross_im = mixed_re * grad_im - mixed_im * grad_re
    return (conv_re - corr_im, conv_im + corr_re, cross_re, cross_im)


def featurize(extended, weights, row_count):
    tap_count = weights.shape[1]
    accumulated = jnp.zeros((row_count,) + extended.shape[1:], jnp.float32)
    for offset in range(tap_count):
        first_row = tap_count - 1 - offset
        accumulated = accumulated + weights[:, offset, :] * extended[
            first_row : first_row + row_count
        ].astype(jnp.float32)
    return accumulated


def transpose_pair(signals, filters):
    return (
        lax.all_to_all(signals, "seq", split_axis=0, concat_axis=1, tiled=True),
        lax.all_to_all(filters, "seq", split_axis=0, concat_axis=1, tiled=True),
    )


def sequence_plan(mixed_input, gated_grad, long_filter):
    row_count, chan_count = mixed_input.shape
    group_count = long_filter.shape[0]
    seq_count = lax.axis_size("seq")
    seq_index = lax.axis_index("seq")
    per_block = row_count // seq_count
    fft_length = 2 * row_count * seq_count
    freq_index = jnp.arange(2 * seq_count, dtype=jnp.int32)
    block_index = jnp.arange(seq_count, dtype=jnp.int32)
    row_index = jnp.arange(row_count, dtype=jnp.int32)
    signals = jnp.stack([mixed_input, gated_grad], 1)[:, None]
    filters = jnp.transpose(long_filter)[:, None]
    sig_cols, filt_cols = transpose_pair(signals, filters)
    cos_one, sin_one = angle_table(freq_index, block_index, 2 * seq_count)
    sig_re = einsum_high("kb,abxc->kaxc", cos_one, sig_cols)
    sig_im = -einsum_high("kb,abxc->kaxc", sin_one, sig_cols)
    filt_re = einsum_high("kb,abg->kag", cos_one, filt_cols)
    filt_im = -einsum_high("kb,abg->kag", sin_one, filt_cols)
    positions = seq_index * per_block + jnp.arange(per_block, dtype=jnp.int32)
    cos_twist, sin_twist = angle_table(freq_index, positions, fft_length)
    sig_re, sig_im = rotate(
        sig_re, sig_im, cos_twist[:, :, None, None], sin_twist[:, :, None, None], -1.0
    )
    filt_re, filt_im = rotate(filt_re, filt_im, cos_twist[:, :, None], sin_twist[:, :, None], -1.0)
    sig_rows, filt_rows = transpose_pair(
        jnp.stack([sig_re, sig_im], 2), jnp.stack([filt_re, filt_im], 2)
    )
    cos_two, sin_two = angle_table(row_index, row_index, row_count)
    spec_re, spec_im = complex_dft(
        cos_two, sin_two, sig_rows[:, :, 0], sig_rows[:, :, 1], "pqka,qjaxc->pjkxc", -1.0
    )
    hspec_re, hspec_im = complex_dft(
        cos_two, sin_two, filt_rows[:, :, 0], filt_rows[:, :, 1], "pqka,qjag->pjkg", -1.0
    )
    leading = spec_re.shape[:2]
    group_shape = leading + (group_count, chan_count // group_count)
    wave_re, wave_im, cross_re, cross_im = combine(
        spec_re[:, :, 0].reshape(group_shape),
        spec_im[:, :, 0].reshape(group_shape),
        spec_re[:, :, 1].reshape(group_shape),
        spec_im[:, :, 1].reshape(group_shape),
        hspec_re[..., None],
        hspec_im[..., None],
    )
    wave_re = wave_re.reshape(leading + (chan_count,))
    wave_im = wave_im.reshape(leading + (chan_count,))
    cross_re = jnp.sum(cross_re, -1)
    cross_im = jnp.sum(cross_im, -1)
    back_re, back_im = complex_dft(cos_two, sin_two, wave_re, wave_im, "pqak,qjkc->pajc", 1.0)
    cback_re, cback_im = complex_dft(cos_two, sin_two, cross_re, cross_im, "pqak,qjkg->pajg", 1.0)
    pair_freq = seq_index * 2 + jnp.arange(2, dtype=jnp.int32)
    cos_back, sin_back = angle_table(row_index, pair_freq, fft_length)
    back_re, back_im = rotate(back_re, back_im, cos_back[:, :, None], sin_back[:, :, None], 1.0)
    cback_re, cback_im = rotate(cback_re, cback_im, cos_back[:, :, None], sin_back[:, :, None], 1.0)
    wave_cols, cross_cols = transpose_pair(
        jnp.stack([back_re, back_im], 2), jnp.stack([cback_re, cback_im], 2)
    )
    cos_three, sin_three = angle_table(block_index, freq_index, 2 * seq_count)
    time_re, time_im = complex_dft(
        cos_three, sin_three, wave_cols[:, :, 0], wave_cols[:, :, 1], "pqbk,qakc->pbac", 1.0
    )
    cross_time = einsum_high("bk,akg->bag", cos_three, cross_cols[:, :, 0]) - einsum_high(
        "bk,akg->bag", sin_three, cross_cols[:, :, 1]
    )
    inverse_scale = 1.0 / fft_length
    wave_out, cross_out = transpose_pair(
        jnp.stack([time_re, time_im], 2) * inverse_scale, cross_time * inverse_scale
    )
    return (wave_out[0, :, 0], wave_out[0, :, 1], jnp.transpose(cross_out[0]))


def split_halves(value):
    top = value.astype(jnp.bfloat16)
    rest = (value - top.astype(jnp.float32)).astype(jnp.bfloat16)
    return top, rest


def dot32(left, right):
    return jnp.dot(left, right, preferred_element_type=jnp.float32)


def dot32_t(left, right):
    return lax.dot_general(
        left, right, (((1,), (1,)), ((), ())), preferred_element_type=jnp.float32
    )


def tile(index, width=LANES):
    return pl.ds(pl.multiple_of(index * width, width), width)


def send_to(src, dst, send_sem, recv_sem, peer):
    return pltpu.make_async_remote_copy(
        src_ref=src,
        dst_ref=dst,
        send_sem=send_sem,
        recv_sem=recv_sem,
        device_id=peer,
        device_id_type=MESH,
    )


def build_filters(taps, ns, low_hi, low_lo, up_hi, up_lo):
    row = lax.broadcasted_iota(jnp.int32, (LANES, LANES), 0)
    col = lax.broadcasted_iota(jnp.int32, (LANES, LANES), 1)
    flip = (row + col == LANES - 1).astype(jnp.float32)
    zero = jnp.zeros((LANES, LANES), jnp.float32)
    zero16 = zero.astype(jnp.bfloat16)
    flipped = jnp.dot(
        taps[...].reshape(ns * 8, LANES), flip, precision=highest,
        preferred_element_type=jnp.float32,
    )
    last_up, last_low = zero, zero
    top = ns - WIDE // LANES
    low_hi[:, (ns - 1) * LANES :] = jnp.concatenate([zero16, zero16], 0)
    low_lo[:, (ns - 1) * LANES :] = jnp.concatenate([zero16, zero16], 0)
    up_hi[LANES:, :LANES] = zero16
    up_lo[LANES:, :LANES] = zero16
    for d in range(ns):
        forward = jnp.concatenate([taps[d]] * (LANES // 8), 0)
        back = jnp.concatenate([flipped[d * 8 : d * 8 + 8]] * (LANES // 8), 0)
        forward = pltpu.roll(forward, 0, 1, stride=1, stride_axis=0)
        back = pltpu.roll(back, 1, 1, stride=1, stride_axis=0)
        up = split_halves(jnp.where(col >= row, forward, last_up))
        low = split_halves(jnp.where(row >= col, back, last_low))
        last_up, last_low = forward, back
        for u in range(WIDE // LANES):
            v = d + u
            if v < ns:
                up_hi[u * LANES : (u + 1) * LANES, v * LANES : (v + 1) * LANES] = up[0]
                up_lo[u * LANES : (u + 1) * LANES, v * LANES : (v + 1) * LANES] = up[1]
            v = top + u - d
            if 0 <= v < ns:
                low_hi[u * LANES : (u + 1) * LANES, v * LANES : (v + 1) * LANES] = low[0]
                low_lo[u * LANES : (u + 1) * LANES, v * LANES : (v + 1) * LANES] = low[1]


def diagonal_sums(gram, ns):
    row = lax.broadcasted_iota(jnp.int32, (LANES, LANES), 0)
    col = lax.broadcasted_iota(jnp.int32, (LANES, LANES), 1)
    turned = []
    for d in range(ns):
        block = gram[LANES:, d * LANES : (d + 1) * LANES]
        if d + 1 < ns:
            block = block + gram[:LANES, (d + 1) * LANES : (d + 2) * LANES]
        turned.append(pltpu.roll(block, 1, 1, stride=1, stride_axis=0))
    turned.append(jnp.zeros((LANES, LANES), jnp.float32))
    return [
        jnp.sum(jnp.where(col <= row, turned[d], turned[d + 1]), 0, keepdims=True)
        for d in range(ns)
    ]


def dot_three(hi, lo, signal):
    width = signal.shape[1] // 2
    both = dot32(hi, signal)
    return both[:, :width] + both[:, width:] + dot32(lo, signal[:, :width])


def resident_kernel(
    ns, nc, kt, groups,
    proj, cot, weight_in, filt_in,
    gp_out, gs_out, gf_out,
    weight, filt, pin, cin, halo, wide, feat, mixed, gated, part, part_edge, fgrad, gp_send,
    tap_send, taps, low_hi, low_lo, up_hi, up_lo, gram,
    fa_send, fa_recv, fb_send, fb_recv, gs_acc, gs_send, gs_pair, gs_sum, gs_recv,
    local_sem, tap_ssem, tap_rsem, in_send, in_recv, gp_ssem, gp_rsem, gs_ssem, gs_rsem,
    fa_ssem, fa_rsem, fb_ssem, fb_rsem, pair_sem,
):
    me = lax.axis_index("seq")
    mych = lax.axis_index("ch")
    hs = ns // 2
    total = ns * LANES
    span = total // 2
    half = me // hs
    mine = lax.rem(me, hs)
    own_base = pl.multiple_of(half * span, span)
    group_owners = hs // groups
    near = [half * hs + lax.rem(mine + i, hs) for i in range(1, hs)]
    far = [(1 - half) * hs + lax.rem(mine + i, hs) for i in range(hs)]
    everyone = near + far
    ch_peers = [(me, lax.rem(mych + i, nc)) for i in range(1, nc)]
    lanes_of = lambda q, t: tile(lax.rem(q, hs) * 2 + t)

    own = [
        pltpu.make_async_copy(filt_in, filt, local_sem.at[0]),
    ]
    for t in range(2):
        lanes, at = lanes_of(me, t), tile(me)
        own += [
            pltpu.make_async_copy(
                weight_in.at[:, :, lanes], weight.at[t], local_sem.at[1 + 3 * t]
            ),
            pltpu.make_async_copy(
                proj.at[:, :, lanes], pin.at[t, :, at, :], local_sem.at[2 + 3 * t]
            ),
            pltpu.make_async_copy(cot.at[:, lanes], cin.at[t, at, :], local_sem.at[3 + 3 * t]),
        ]
    for copy in own:
        copy.start()
    barrier = pltpu.get_barrier_semaphore()
    for q in everyone:
        pl.semaphore_signal(barrier, inc=1, device_id=(q, mych), device_id_type=MESH)
    for peer in ch_peers:
        pl.semaphore_signal(barrier, inc=1, device_id=peer, device_id_type=MESH)
    own[0].wait()
    for g in range(groups):
        tap_send[g] = jnp.broadcast_to(filt[g : g + 1, :], (8, LANES))
    pl.semaphore_wait(barrier, ns + nc - 2)

    def tap_copy(q, src):
        return send_to(
            tap_send.at[lax.rem(q, hs) // group_owners], taps.at[src],
            tap_ssem.at[q], tap_rsem.at[src], (q, mych),
        )

    def halo_copy(q, t, src, first):
        return send_to(
            proj.at[:, pl.ds(first, 16), lanes_of(q, t)], halo.at[t],
            in_send.at[t, 2, q], in_recv.at[t, 2, 0], (q, mych),
        )

    def stream_copy(q, t, src, streams):
        return send_to(
            proj.at[streams, :, lanes_of(q, t)], pin.at[t, streams, tile(src), :],
            in_send.at[t, 0, q], in_recv.at[t, 0, src], (q, mych),
        )

    def cot_copy(q, t, src):
        return send_to(
            cot.at[:, lanes_of(q, t)], cin.at[t, tile(src), :],
            in_send.at[t, 1, q], in_recv.at[t, 1, src], (q, mych),
        )

    def near_copies(q, t, src):
        return (stream_copy(q, t, src, slice(0, 3)), cot_copy(q, t, src))

    def mix_copy(q, t, src):
        return stream_copy(q, t, src, slice(1, 3))

    def gate_copies(q, t, src):
        return (stream_copy(q, t, src, slice(0, 1)), cot_copy(q, t, src))

    for q in everyone:
        tap_copy(q, me).start()

    @pl.when(me == hs - 1)
    def _():
        for t in range(2):
            for q in far:
                halo_copy(q, t, me, LANES - 16).start()

    @pl.when(me == hs)
    def _():
        for t in range(2):
            for q in far:
                halo_copy(q, t, me, 0).start()

    for t in range(2):
        for i in range(hs):
            @pl.when(half == 0)
            def _():
                mix_copy(far[i], t, me).start()

            @pl.when(half == 1)
            def _():
                for copy in gate_copies(far[i], t, me):
                    copy.start()

            if i < hs - 1:
                for copy in near_copies(near[i], t, me):
                    copy.start()

    taps[me] = tap_send[mine // group_owners]
    gram[...] = jnp.zeros(gram.shape, jnp.float32)
    for j in range(3):
        wide[j, 0:8, :] = jnp.zeros((8, LANES), jnp.float32)
        fgrad[j, span : span + 16, :] = jnp.zeros((16, LANES), jnp.float32)
        for t in range(2):
            for k in range(kt):
                gs_acc[t, j, k] = jnp.zeros((8, LANES), jnp.float32)
    for q in everyone:
        tap_copy(q, q).wait_recv()
    build_filters(taps, ns, low_hi, low_lo, up_hi, up_lo)
    for copy in own[1:]:
        copy.wait()
    for t in range(2):
        halo_copy(far[0], t, 0, 0).wait_recv()

    def to_wide(t, j, first):
        wide[j, pl.ds(first + 8, LANES), :] = pin[t, j, pl.ds(first, LANES), :].astype(jnp.float32)

    def feature(t, j, first, rows):
        acc = jnp.zeros((rows, LANES), jnp.float32)
        for k in range(kt):
            acc = acc + weight[t, j, k : k + 1, :] * wide[j, pl.ds(first + 8 - k, rows), :]
        return acc

    def keep(store, rows, value):
        top, rest = split_halves(value)
        store[rows, 0:LANES] = top
        store[rows, LANES:] = rest

    def near_block(t, i, carry):
        b = half * hs + i

        @pl.when(b != me)
        def _():
            for copy in near_copies(b, t, b):
                copy.wait_recv()

        base = pl.multiple_of(b * LANES, LANES)
        for j in range(3):
            to_wide(t, j, base)
        for p in range(LANES // ROWS):
            first = base + p * ROWS
            rows = pl.ds(first, ROWS)
            kept = pl.ds(pl.multiple_of(i * LANES, LANES) + p * ROWS, ROWS)
            one, two = feature(t, 1, first, ROWS), feature(t, 2, first, ROWS)
            feat[0, kept, :] = one
            feat[1, kept, :] = two
            keep(mixed, rows, one * two)
            keep(gated, rows, cin[t, rows, :].astype(jnp.float32) * feature(t, 0, first, ROWS))
        return carry

    def far_block(early, t, i, carry):
        b = (1 - half) * hs + i
        base = pl.multiple_of(b * LANES, LANES)
        for copy in gate_copies(b, t, b) if early else (mix_copy(b, t, b),):
            copy.wait_recv()
        for j in (0,) if early else (1, 2):
            to_wide(t, j, base)
        for p in range(LANES // ROWS):
            first = base + p * ROWS
            rows = pl.ds(first, ROWS)
            if early:
                gate = feature(t, 0, first, ROWS)
                keep(gated, rows, cin[t, rows, :].astype(jnp.float32) * gate)
            else:
                keep(mixed, rows, feature(t, 1, first, ROWS) * feature(t, 2, first, ROWS))
        return carry

    flip = (
        lax.broadcasted_iota(jnp.int32, (WIDE, WIDE), 0)
        + lax.broadcasted_iota(jnp.int32, (WIDE, WIDE), 1)
        == WIDE - 1
    ).astype(jnp.float32).astype(jnp.bfloat16)

    def add_gram(pairs):
        for b in sorted({b for b, _ in pairs}):
            left = dot32(flip, mixed[b * WIDE : (b + 1) * WIDE, :]).astype(jnp.bfloat16)
            for c in sorted(c for first, c in pairs if first == b):
                right = gated[c * WIDE : (c + 1) * WIDE, :]
                top = right[:, :LANES]
                cols = slice((c - b) * WIDE, (c - b + 1) * WIDE)
                gram[:, cols] += dot32_t(left, jnp.concatenate([top, top], 1)) + dot32_t(
                    left[:, :LANES], right[:, LANES:]
                )

    def conv_of(b, first, last, rows=WIDE):
        start = total - (b + 1) * WIDE
        cols = slice(start + first, start + last)
        return dot_three(low_hi[:rows, cols], low_lo[:rows, cols], mixed[first:last, :])

    def corr_of(a, first, last, rows=WIDE):
        cols = slice(first - a * WIDE, last - a * WIDE)
        return dot_three(up_hi[:rows, cols], up_lo[:rows, cols], gated[first:last, :])

    def grads_of(t, rows, conv=None, corr=None):
        if conv is not None:
            at = pl.ds(own_base + rows.start, rows.stop - rows.start)
            fgrad[0, rows, :] = cin[t, at, :].astype(jnp.float32) * conv
        if corr is not None:
            fgrad[1, rows, :] = corr * feat[1, rows, :]
            fgrad[2, rows, :] = corr * feat[0, rows, :]

    per = span // WIDE
    local_rows = [slice(b * WIDE, (b + 1) * WIDE) for b in range(per)]
    edge = slice(span, span + 16)
    near_pairs = [(b, c) for b in range(per) for c in range(b, per)]
    far_pairs = [(b, c) for b in range(per) for c in range(per, 2 * per)]

    def early_part(t):
        for j in (1, 2):
            wide[j, 8 + span : 8 + span + 16, :] = halo[t, j].astype(jnp.float32)
        lax.fori_loop(0, hs, functools.partial(near_block, t), 0)
        mixed[span : span + LANES, :] = jnp.zeros((LANES, WIDE), jnp.bfloat16)
        one, two = feature(t, 1, span, 16), feature(t, 2, span, 16)
        feat[0, edge, :] = one
        feat[1, edge, :] = two
        keep(mixed, edge, one * two)
        for b in range(per):
            grads_of(t, local_rows[b], conv=conv_of(b, 0, (b + 1) * WIDE))
            part[local_rows[b], :] = corr_of(b, b * WIDE, span)
        part_edge[...] = conv_of(per, 0, span + LANES, 16)
        add_gram(near_pairs)
        lax.fori_loop(0, hs, functools.partial(far_block, True, t), 0)
        for b in range(per):
            grads_of(t, local_rows[b], corr=part[local_rows[b], :] + corr_of(b, span, total))
        grads_of(t, edge, conv=part_edge[...], corr=corr_of(per, span, total, 16))

    def late_part(t):
        for j in range(3):
            wide[j, 8 + span - 16 : 8 + span, :] = halo[t, j].astype(jnp.float32)
        lax.fori_loop(0, hs, functools.partial(near_block, t), 0)
        for b in range(per):
            grads_of(t, local_rows[b], corr=corr_of(per + b, span + b * WIDE, total))
            part[local_rows[b], :] = conv_of(per + b, span, span + (b + 1) * WIDE)
        add_gram([(per + b, per + c) for b, c in near_pairs])
        lax.fori_loop(0, hs, functools.partial(far_block, False, t), 0)
        for b in range(per):
            grads_of(t, local_rows[b], conv=part[local_rows[b], :] + conv_of(per + b, 0, span))

    def finish_block(t, i, carry):
        b = lax.rem(mine + 1 + i, hs)
        base = pl.multiple_of(b * LANES, LANES)
        for p in range(LANES // ROWS):
            first = base + p * ROWS
            for j in range(3):
                acc = jnp.zeros((ROWS, LANES), jnp.float32)
                source = wide[j, pl.ds(own_base + first + 8, ROWS), :]
                for k in range(kt):
                    shifted = fgrad[j, pl.ds(first + k, ROWS), :]
                    acc = acc + weight[t, j, k : k + 1, :] * shifted
                    terms = (shifted * source).reshape(ROWS // 8, 8, LANES)
                    gs_acc[t, j, k] += jnp.sum(terms, 0)
                gp_send[t, j, pl.ds(first, ROWS), :] = acc.astype(jnp.bfloat16)

        @pl.when(i < hs - 1)
        def _():
            gp_copy(half * hs + b, t, me).start()

        return carry

    def gp_copy(q, t, src):
        return send_to(
            gp_send.at[t, :, tile(lax.rem(q, hs)), :], gp_out.at[:, :, lanes_of(src, t)],
            gp_ssem.at[t, q], gp_rsem.at[t, src], (q, mych),
        )

    filter_scale = 1.0 / math.sqrt(total * group_owners * WIDE)
    fa_copy = lambda q, src: send_to(
        fa_send.at[q], fa_recv.at[src], fa_ssem.at[q], fa_rsem.at[src], (q, mych)
    )

    def one_tile(t, carry):
        @pl.when(half == 0)
        def _():
            early_part(t)

        @pl.when(half == 1)
        def _():
            late_part(t)

        lax.fori_loop(0, hs - 1, functools.partial(finish_block, t), 0)

        @pl.when(t == half)
        def _():
            add_gram(far_pairs)

        @pl.when(t == 1)
        def _():
            for d, line in enumerate(diagonal_sums(gram, ns)):
                fa_send[d] = jnp.broadcast_to(line * filter_scale, (8, LANES))
            for q in everyone:
                fa_copy(q, me).start()
            fa_recv[me] = fa_send[me]

        finish_block(t, hs - 1, carry)
        gp_out[:, :, lanes_of(me, t)] = gp_send[t, :, tile(mine), :]
        return carry

    lax.fori_loop(0, 2, one_tile, 0)

    short_scale = 1.0 / math.sqrt(total)
    for t in range(2):
        for j in range(3):
            lines = [jnp.sum(gs_acc[t, j, k], 0, keepdims=True) for k in range(kt)]
            lines += [jnp.zeros((1, LANES), jnp.float32)] * (8 - kt)
            gs_send[t, j] = jnp.concatenate(lines, 0) * short_scale
    partner = far[0]
    pair = send_to(gs_send, gs_pair, pair_sem.at[0], pair_sem.at[1], (partner, mych))
    pair.start()

    for q in everyone:
        fa_copy(q, q).wait_recv()
    for g in range(groups):
        owners = [h * hs + g * group_owners + i for h in range(2) for i in range(group_owners)]
        summed = fa_recv[owners[0]]
        for q in owners[1:]:
            summed = summed + fa_recv[q]
        fb_send[g] = summed
    fb_copy = lambda c, src: send_to(
        fb_send, fb_recv.at[src], fb_ssem.at[c], fb_rsem.at[src], (me, c)
    )
    for _, c in ch_peers:
        fb_copy(c, mych).start()
    fb_recv[mych] = fb_send[...]
    pair.wait()
    gs_sum[...] = gs_send[...] + gs_pair[...]
    gs_copy = lambda q, src: send_to(
        gs_sum, gs_recv.at[lax.rem(src, hs)], gs_ssem.at[q], gs_rsem.at[src], (q, mych)
    )
    for q in near:
        gs_copy(q, me).start()
    gs_recv[mine] = gs_sum[...]

    for _, c in ch_peers:
        fb_copy(c, c).wait_recv()
    width = LANES // nc
    for c in range(nc):
        for g in range(groups):
            line = fb_recv[c, g]
            piece = line[:, 0:width]
            for other in range(1, nc):
                piece = jnp.where(
                    mych == other, line[:, other * width : (other + 1) * width], piece
                )
            at = c * groups + g
            gf_out[at : at + 1, :] = piece[0:1, :]

    for q in near:
        gs_copy(q, q).wait_recv()
    for q in range(hs):
        for t in range(2):
            lanes = slice((2 * q + t) * LANES, (2 * q + t + 1) * LANES)
            for j in range(3):
                gs_out[j, :, lanes] = gs_recv[q, t, j, 0:kt, :]

    for q in everyone:
        tap_copy(q, me).wait_send()
        fa_copy(q, me).wait_send()
    for q in near:
        gs_copy(q, me).wait_send()
        for t in range(2):
            for copy in near_copies(q, t, me):
                copy.wait_send()
            gp_copy(q, t, me).wait_send()
            gp_copy(q, t, q).wait_recv()
    for _, c in ch_peers:
        fb_copy(c, mych).wait_send()

    @pl.when(half == 0)
    def _():
        for q in far:
            for t in range(2):
                mix_copy(q, t, me).wait_send()

    @pl.when(half == 1)
    def _():
        for q in far:
            for t in range(2):
                for copy in gate_copies(q, t, me):
                    copy.wait_send()

    @pl.when((me == hs - 1) | (me == hs))
    def _():
        for q in far:
            for t in range(2):
                halo_copy(q, t, me, 0).wait_send()


def resident(projected, cotangent, short_weight, long_filter):
    row_count, streams, chan_count = projected.shape
    kt = short_weight.shape[1]
    groups = long_filter.shape[0]
    ns, nc = lax.axis_size("seq"), lax.axis_size("ch")
    total = row_count * ns
    span = total // 2
    f32, bf16 = jnp.float32, jnp.bfloat16
    dma = pltpu.SemaphoreType.DMA
    vmem = pl.BlockSpec(memory_space=pltpu.VMEM)
    anywhere = pl.BlockSpec(memory_space=pltpu.HBM)
    operands = [
        pltpu.with_memory_space_constraint(x, pltpu.HBM)
        for x in (jnp.transpose(projected, (1, 0, 2)), cotangent, short_weight, long_filter)
    ]
    grad_proj, grad_short, grad_filter = pl.pallas_call(
        functools.partial(resident_kernel, ns, nc, kt, groups),
        out_shape=(
            jax.ShapeDtypeStruct((streams, row_count, chan_count), bf16),
            jax.ShapeDtypeStruct((streams, kt, chan_count), f32),
            jax.ShapeDtypeStruct((groups * nc, row_count // nc), f32),
        ),
        in_specs=[anywhere] * 4,
        out_specs=(vmem, vmem, vmem),
        scratch_shapes=[
            pltpu.VMEM((2, 3, kt, LANES), f32),
            pltpu.VMEM((groups, LANES), f32),
            pltpu.VMEM((2, 3, total, LANES), bf16),
            pltpu.VMEM((2, total, LANES), bf16),
            pltpu.VMEM((2, 3, 16, LANES), bf16),
            pltpu.VMEM((3, total + 8, LANES), f32),
            pltpu.VMEM((2, span + 16, LANES), f32),
            pltpu.VMEM((total, WIDE), bf16),
            pltpu.VMEM((total, WIDE), bf16),
            pltpu.VMEM((span, LANES), f32),
            pltpu.VMEM((16, LANES), f32),
            pltpu.VMEM((3, span + 16, LANES), f32),
            pltpu.VMEM((2, 3, span, LANES), bf16),
            pltpu.VMEM((groups, 8, LANES), f32),
            pltpu.VMEM((ns, 8, LANES), f32),
            pltpu.VMEM((WIDE, total), bf16),
            pltpu.VMEM((WIDE, total), bf16),
            pltpu.VMEM((WIDE, total), bf16),
            pltpu.VMEM((WIDE, total), bf16),
            pltpu.VMEM((WIDE, total), f32),
            pltpu.VMEM((ns, 8, LANES), f32),
            pltpu.VMEM((ns, 8, LANES), f32),
            pltpu.VMEM((groups, 8, LANES), f32),
            pltpu.VMEM((nc, groups, 8, LANES), f32),
            pltpu.VMEM((2, 3, 8, 8, LANES), f32),
            pltpu.VMEM((2, 3, 8, LANES), f32),
            pltpu.VMEM((2, 3, 8, LANES), f32),
            pltpu.VMEM((2, 3, 8, LANES), f32),
            pltpu.VMEM((ns // 2, 2, 3, 8, LANES), f32),
            dma((7,)),
            dma((ns,)), dma((ns,)),
            dma((2, 3, ns)), dma((2, 3, ns)),
            dma((2, ns)), dma((2, ns)),
            dma((ns,)), dma((ns,)),
            dma((ns,)), dma((ns,)),
            dma((nc,)), dma((nc,)),
            dma((2,)),
        ],
        compiler_params=pltpu.CompilerParams(
            collective_id=0, has_side_effects=True, vmem_limit_bytes=48 * 1024 * 1024
        ),
    )(*operands)
    return jnp.transpose(grad_proj, (1, 0, 2)), grad_short, grad_filter


def spread(projected, cotangent, short_weight, long_filter):
    tap_count = short_weight.shape[1]
    row_count = projected.shape[0]
    margin = tap_count - 1
    front_rows = passed_along(projected[row_count - margin :], "seq", 1)
    extended = jnp.concatenate([front_rows, projected], 0)
    features = featurize(extended, short_weight, row_count)
    grad_out = cotangent.astype(jnp.float32)
    mixed_input = features[:, 1] * features[:, 2]
    gated_grad = grad_out * features[:, 0]
    conv_out, corr_out, filt_grad = sequence_plan(mixed_input, gated_grad, long_filter)
    token_count = row_count * lax.axis_size("seq")
    group_width = mixed_input.shape[1] // long_filter.shape[0]
    scaled_grad = filt_grad * (1.0 / math.sqrt(token_count * group_width))
    owned_grad = lax.all_to_all(scaled_grad, "ch", split_axis=1, concat_axis=0, tiled=True)
    feat_grad = jnp.stack(
        [grad_out * conv_out, corr_out * features[:, 2], corr_out * features[:, 1]], 1
    )
    next_rows = passed_along(feat_grad[:margin].astype(jnp.bfloat16), "seq", -1).astype(jnp.float32)
    extended_grad = jnp.concatenate([feat_grad, next_rows], 0)
    grad_proj = jnp.zeros(feat_grad.shape, jnp.float32)
    for offset in range(tap_count):
        grad_proj = (
            grad_proj + short_weight[:, offset, :] * extended_grad[offset : offset + row_count]
        )
    short_terms = []
    for offset in range(tap_count):
        first_row = margin - offset
        short_terms.append(
            jnp.sum(feat_grad * extended[first_row : first_row + row_count].astype(jnp.float32), 0)
        )
    grad_short = lax.psum(jnp.stack(short_terms, 1), "seq") * (1.0 / math.sqrt(token_count))
    return (grad_proj.astype(jnp.bfloat16), grad_short, owned_grad)


def local(projected, cotangent, short_weight, long_filter):
    row_count, _, chan_count = projected.shape
    seq_count = lax.axis_size("seq")
    group_width = chan_count // long_filter.shape[0]
    fits = (
        row_count == LANES
        and seq_count % 4 == 0
        and chan_count == WIDE * (seq_count // 2)
        and group_width % WIDE == 0
        and short_weight.shape[1] <= 8
    )
    plan = resident if fits else spread
    return plan(projected, cotangent, short_weight, long_filter)


def solution(mesh):
    return jax.shard_map(
        local,
        mesh=mesh,
        in_specs=(P("seq", None, "ch"), P("seq", "ch"), P(None, None, "ch"), P("ch", "seq")),
        out_specs=(P("seq", None, "ch"), P(None, None, "ch"), P(None, ("seq", "ch"))),
        check_vma=False,
    )
```

```python
import functools
import math

import jax
import jax.numpy as jnp
from jax import lax
from jax.experimental import pallas as pl
from jax.experimental.pallas import tpu as pltpu
from jax.sharding import PartitionSpec as P

highest = lax.Precision.HIGHEST
MESH = pl.DeviceIdType.MESH
LANES = 128
WIDE = 256
ROWS = 64


def passed_along(block, axis, distance):
    devices = range(lax.axis_size(axis))
    route = [(i - distance, i) for i in devices if i - distance in devices]
    return lax.ppermute(block, axis, route)


def einsum_high(form, table, operand):
    return jnp.einsum(form, table, operand, precision=highest)


def angle_table(first, second, length):
    product = first[:, None] * second[None, :] % length
    radians = product.astype(jnp.float32) * (2.0 * math.pi / length)
    return (jnp.cos(radians), jnp.sin(radians))


def complex_dft(cosine, sine, real_part, imag_part, joined, sign):
    table = jnp.stack(
        [jnp.stack([cosine, -sign * sine], 0), jnp.stack([sign * sine, cosine], 0)], 0
    )
    stacked = jnp.stack([real_part, imag_part], 0)
    result = jnp.einsum(joined, table, stacked, precision=highest)
    return (result[0], result[1])


def rotate(real_part, imag_part, cosine, sine, sign):
    return (
        real_part * cosine - sign * imag_part * sine,
        imag_part * cosine + sign * real_part * sine,
    )


def combine(mixed_re, mixed_im, grad_re, grad_im, filt_re, filt_im):
    conv_re = filt_re * mixed_re - filt_im * mixed_im
    conv_im = filt_re * mixed_im + filt_im * mixed_re
    corr_re = filt_re * grad_re + filt_im * grad_im
    corr_im = filt_re * grad_im - filt_im * grad_re
    cross_re = mixed_re * grad_re + mixed_im * grad_im
    cross_im = mixed_re * grad_im - mixed_im * grad_re
    return (conv_re - corr_im, conv_im + corr_re, cross_re, cross_im)


def featurize(extended, weights, row_count):
    tap_count = weights.shape[1]
    accumulated = jnp.zeros((row_count,) + extended.shape[1:], jnp.float32)
    for offset in range(tap_count):
        first_row = tap_count - 1 - offset
        accumulated = accumulated + weights[:, offset, :] * extended[
            first_row : first_row + row_count
        ].astype(jnp.float32)
    return accumulated


def transpose_pair(signals, filters):
    return (
        lax.all_to_all(signals, "seq", split_axis=0, concat_axis=1, tiled=True),
        lax.all_to_all(filters, "seq", split_axis=0, concat_axis=1, tiled=True),
    )


def sequence_plan(mixed_input, gated_grad, long_filter):
    row_count, chan_count = mixed_input.shape
    group_count = long_filter.shape[0]
    seq_count = lax.axis_size("seq")
    seq_index = lax.axis_index("seq")
    per_block = row_count // seq_count
    fft_length = 2 * row_count * seq_count
    freq_index = jnp.arange(2 * seq_count, dtype=jnp.int32)
    block_index = jnp.arange(seq_count, dtype=jnp.int32)
    row_index = jnp.arange(row_count, dtype=jnp.int32)
    signals = jnp.stack([mixed_input, gated_grad], 1)[:, None]
    filters = jnp.transpose(long_filter)[:, None]
    sig_cols, filt_cols = transpose_pair(signals, filters)
    cos_one, sin_one = angle_table(freq_index, block_index, 2 * seq_count)
    sig_re = einsum_high("kb,abxc->kaxc", cos_one, sig_cols)
    sig_im = -einsum_high("kb,abxc->kaxc", sin_one, sig_cols)
    filt_re = einsum_high("kb,abg->kag", cos_one, filt_cols)
    filt_im = -einsum_high("kb,abg->kag", sin_one, filt_cols)
    positions = seq_index * per_block + jnp.arange(per_block, dtype=jnp.int32)
    cos_twist, sin_twist = angle_table(freq_index, positions, fft_length)
    sig_re, sig_im = rotate(
        sig_re, sig_im, cos_twist[:, :, None, None], sin_twist[:, :, None, None], -1.0
    )
    filt_re, filt_im = rotate(filt_re, filt_im, cos_twist[:, :, None], sin_twist[:, :, None], -1.0)
    sig_rows, filt_rows = transpose_pair(
        jnp.stack([sig_re, sig_im], 2), jnp.stack([filt_re, filt_im], 2)
    )
    cos_two, sin_two = angle_table(row_index, row_index, row_count)
    spec_re, spec_im = complex_dft(
        cos_two, sin_two, sig_rows[:, :, 0], sig_rows[:, :, 1], "pqka,qjaxc->pjkxc", -1.0
    )
    hspec_re, hspec_im = complex_dft(
        cos_two, sin_two, filt_rows[:, :, 0], filt_rows[:, :, 1], "pqka,qjag->pjkg", -1.0
    )
    leading = spec_re.shape[:2]
    group_shape = leading + (group_count, chan_count // group_count)
    wave_re, wave_im, cross_re, cross_im = combine(
        spec_re[:, :, 0].reshape(group_shape),
        spec_im[:, :, 0].reshape(group_shape),
        spec_re[:, :, 1].reshape(group_shape),
        spec_im[:, :, 1].reshape(group_shape),
        hspec_re[..., None],
        hspec_im[..., None],
    )
    wave_re = wave_re.reshape(leading + (chan_count,))
    wave_im = wave_im.reshape(leading + (chan_count,))
    cross_re = jnp.sum(cross_re, -1)
    cross_im = jnp.sum(cross_im, -1)
    back_re, back_im = complex_dft(cos_two, sin_two, wave_re, wave_im, "pqak,qjkc->pajc", 1.0)
    cback_re, cback_im = complex_dft(cos_two, sin_two, cross_re, cross_im, "pqak,qjkg->pajg", 1.0)
    pair_freq = seq_index * 2 + jnp.arange(2, dtype=jnp.int32)
    cos_back, sin_back = angle_table(row_index, pair_freq, fft_length)
    back_re, back_im = rotate(back_re, back_im, cos_back[:, :, None], sin_back[:, :, None], 1.0)
    cback_re, cback_im = rotate(cback_re, cback_im, cos_back[:, :, None], sin_back[:, :, None], 1.0)
    wave_cols, cross_cols = transpose_pair(
        jnp.stack([back_re, back_im], 2), jnp.stack([cback_re, cback_im], 2)
    )
    cos_three, sin_three = angle_table(block_index, freq_index, 2 * seq_count)
    time_re, time_im = complex_dft(
        cos_three, sin_three, wave_cols[:, :, 0], wave_cols[:, :, 1], "pqbk,qakc->pbac", 1.0
    )
    cross_time = einsum_high("bk,akg->bag", cos_three, cross_cols[:, :, 0]) - einsum_high(
        "bk,akg->bag", sin_three, cross_cols[:, :, 1]
    )
    inverse_scale = 1.0 / fft_length
    wave_out, cross_out = transpose_pair(
        jnp.stack([time_re, time_im], 2) * inverse_scale, cross_time * inverse_scale
    )
    return (wave_out[0, :, 0], wave_out[0, :, 1], jnp.transpose(cross_out[0]))


def split_halves(value):
    top = value.astype(jnp.bfloat16)
    rest = (value - top.astype(jnp.float32)).astype(jnp.bfloat16)
    return top, rest


def dot32(left, right):
    return jnp.dot(left, right, preferred_element_type=jnp.float32)


def dot32_t(left, right):
    return lax.dot_general(
        left, right, (((1,), (1,)), ((), ())), preferred_element_type=jnp.float32
    )


def tile(index, width=LANES):
    return pl.ds(pl.multiple_of(index * width, width), width)


def send_to(src, dst, send_sem, recv_sem, peer):
    return pltpu.make_async_remote_copy(
        src_ref=src,
        dst_ref=dst,
        send_sem=send_sem,
        recv_sem=recv_sem,
        device_id=peer,
        device_id_type=MESH,
    )


def build_filters(taps, ns, low_hi, low_lo, up_hi, up_lo):
    row = lax.broadcasted_iota(jnp.int32, (LANES, LANES), 0)
    col = lax.broadcasted_iota(jnp.int32, (LANES, LANES), 1)
    flip = (row + col == LANES - 1).astype(jnp.float32)
    zero = jnp.zeros((LANES, LANES), jnp.float32)
    zero16 = zero.astype(jnp.bfloat16)
    flipped = jnp.dot(
        taps[...].reshape(ns * 8, LANES), flip, precision=highest,
        preferred_element_type=jnp.float32,
    )
    last_up, last_low = zero, zero
    top = ns - WIDE // LANES
    low_hi[:, (ns - 1) * LANES :] = jnp.concatenate([zero16, zero16], 0)
    low_lo[:, (ns - 1) * LANES :] = jnp.concatenate([zero16, zero16], 0)
    up_hi[LANES:, :LANES] = zero16
    up_lo[LANES:, :LANES] = zero16
    for d in range(ns):
        forward = jnp.concatenate([taps[d]] * (LANES // 8), 0)
        back = jnp.concatenate([flipped[d * 8 : d * 8 + 8]] * (LANES // 8), 0)
        forward = pltpu.roll(forward, 0, 1, stride=1, stride_axis=0)
        back = pltpu.roll(back, 1, 1, stride=1, stride_axis=0)
        up = split_halves(jnp.where(col >= row, forward, last_up))
        low = split_halves(jnp.where(row >= col, back, last_low))
        last_up, last_low = forward, back
        for u in range(WIDE // LANES):
            v = d + u
            if v < ns:
                up_hi[u * LANES : (u + 1) * LANES, v * LANES : (v + 1) * LANES] = up[0]
                up_lo[u * LANES : (u + 1) * LANES, v * LANES : (v + 1) * LANES] = up[1]
            v = top + u - d
            if 0 <= v < ns:
                low_hi[u * LANES : (u + 1) * LANES, v * LANES : (v + 1) * LANES] = low[0]
                low_lo[u * LANES : (u + 1) * LANES, v * LANES : (v + 1) * LANES] = low[1]


def diagonal_sums(gram, ns):
    row = lax.broadcasted_iota(jnp.int32, (LANES, LANES), 0)
    col = lax.broadcasted_iota(jnp.int32, (LANES, LANES), 1)
    turned = []
    for d in range(ns):
        block = gram[LANES:, d * LANES : (d + 1) * LANES]
        if d + 1 < ns:
            block = block + gram[:LANES, (d + 1) * LANES : (d + 2) * LANES]
        turned.append(pltpu.roll(block, 1, 1, stride=1, stride_axis=0))
    turned.append(jnp.zeros((LANES, LANES), jnp.float32))
    return [
        jnp.sum(jnp.where(col <= row, turned[d], turned[d + 1]), 0, keepdims=True)
        for d in range(ns)
    ]


def dot_three(hi, lo, signal):
    width = signal.shape[1] // 2
    both = dot32(hi, signal)
    return both[:, :width] + both[:, width:] + dot32(lo, signal[:, :width])


def resident_kernel(
    ns, nc, kt, groups,
    proj, cot, weight_in, filt_in,
    gp_out, gs_out, gf_out,
    weight, filt, packed, pin, halo, wide, feat, mixed, gated, part, part_edge, fgrad, gp_send,
    tap_send, taps, low_hi, low_lo, up_hi, up_lo, gram,
    fa_send, fa_recv, fb_send, fb_recv, gs_acc, gs_send, gs_pair, gs_sum, gs_recv,
    local_sem, pack_sem, tap_ssem, tap_rsem, in_send, in_recv, gp_ssem, gp_rsem, gs_ssem, gs_rsem,
    fa_ssem, fa_rsem, fb_ssem, fb_rsem, pair_sem,
):
    me = lax.axis_index("seq")
    mych = lax.axis_index("ch")
    hs = ns // 2
    total = ns * LANES
    span = total // 2
    half = me // hs
    mine = lax.rem(me, hs)
    own_base = pl.multiple_of(half * span, span)
    group_owners = hs // groups
    near = [half * hs + lax.rem(mine + i, hs) for i in range(1, hs)]
    far = [(1 - half) * hs + lax.rem(mine + i, hs) for i in range(hs)]
    everyone = near + far
    ch_peers = [(me, lax.rem(mych + i, nc)) for i in range(1, nc)]
    lanes_of = lambda q, t: tile(lax.rem(q, hs) * 2 + t)

    own = [
        pltpu.make_async_copy(filt_in, filt, local_sem.at[0]),
    ]
    for t in range(2):
        own.append(
            pltpu.make_async_copy(
                weight_in.at[:, :, lanes_of(me, t)], weight.at[t], local_sem.at[1 + t]
            )
        )
    packs = []
    for c in range(2 * hs):
        lanes = slice(c * LANES, (c + 1) * LANES)
        packs += [
            pltpu.make_async_copy(
                proj.at[1:3, :, lanes], packed.at[c, 0:2], pack_sem.at[0, c]
            ),
            pltpu.make_async_copy(
                proj.at[0:1, :, lanes], packed.at[c, 2:3], pack_sem.at[1, c]
            ),
            pltpu.make_async_copy(cot.at[:, lanes], packed.at[c, 3], pack_sem.at[2, c]),
        ]
    own += packs
    for copy in own:
        copy.start()
    barrier = pltpu.get_barrier_semaphore()
    for q in everyone:
        pl.semaphore_signal(barrier, inc=1, device_id=(q, mych), device_id_type=MESH)
    for peer in ch_peers:
        pl.semaphore_signal(barrier, inc=1, device_id=peer, device_id_type=MESH)
    own[0].wait()
    for g in range(groups):
        tap_send[g] = jnp.broadcast_to(filt[g : g + 1, :], (8, LANES))
    pl.semaphore_wait(barrier, ns + nc - 2)

    def tap_copy(q, src):
        return send_to(
            tap_send.at[lax.rem(q, hs) // group_owners], taps.at[src],
            tap_ssem.at[q], tap_rsem.at[src], (q, mych),
        )

    def halo_copy(q, t, src, first):
        return send_to(
            packed.at[lax.rem(q, hs) * 2 + t, 0:3, pl.ds(first, 16)], halo.at[t],
            in_send.at[t, 1, q], in_recv.at[t, 1, 0], (q, mych),
        )

    def stream_copy(q, t, src, streams):
        return send_to(
            packed.at[lax.rem(q, hs) * 2 + t, streams], pin.at[t, src, streams],
            in_send.at[t, 0, q], in_recv.at[t, 0, src], (q, mych),
        )

    def near_copies(q, t, src):
        return (stream_copy(q, t, src, slice(0, 4)),)

    def mix_copy(q, t, src):
        return stream_copy(q, t, src, slice(0, 2))

    def gate_copies(q, t, src):
        return (stream_copy(q, t, src, slice(2, 4)),)

    for q in everyone:
        tap_copy(q, me).start()
    for copy in packs:
        copy.wait()

    @pl.when(me == hs - 1)
    def _():
        for t in range(2):
            for q in far:
                halo_copy(q, t, me, LANES - 16).start()

    @pl.when(me == hs)
    def _():
        for t in range(2):
            for q in far:
                halo_copy(q, t, me, 0).start()

    for t in range(2):
        for i in range(hs):
            @pl.when(half == 0)
            def _():
                mix_copy(far[i], t, me).start()

            @pl.when(half == 1)
            def _():
                for copy in gate_copies(far[i], t, me):
                    copy.start()

            if i < hs - 1:
                for copy in near_copies(near[i], t, me):
                    copy.start()

    taps[me] = tap_send[mine // group_owners]
    gram[...] = jnp.zeros(gram.shape, jnp.float32)
    for j in range(3):
        wide[j, 0:8, :] = jnp.zeros((8, LANES), jnp.float32)
        fgrad[j, span : span + 16, :] = jnp.zeros((16, LANES), jnp.float32)
        for t in range(2):
            for k in range(kt):
                gs_acc[t, j, k] = jnp.zeros((8, LANES), jnp.float32)
    for q in everyone:
        tap_copy(q, q).wait_recv()
    build_filters(taps, ns, low_hi, low_lo, up_hi, up_lo)
    for copy in own[1:3]:
        copy.wait()
    for t in range(2):
        pin[t, me] = packed[mine * 2 + t]
    for t in range(2):
        halo_copy(far[0], t, 0, 0).wait_recv()

    place = (2, 0, 1)

    def to_wide(t, j, b):
        first = pl.multiple_of(b * LANES, LANES)
        block = pin[t, b, place[j]]
        wide[j, pl.ds(first + 8, LANES), :] = block.astype(jnp.float32)

    def cot_rows(t, b, first, rows):
        return pin[t, b, 3, pl.ds(first, rows), :].astype(jnp.float32)

    def feature(t, j, first, rows):
        acc = jnp.zeros((rows, LANES), jnp.float32)
        for k in range(kt):
            acc = acc + weight[t, j, k : k + 1, :] * wide[j, pl.ds(first + 8 - k, rows), :]
        return acc

    def keep(store, rows, value):
        top, rest = split_halves(value)
        store[rows, 0:LANES] = top
        store[rows, LANES:] = rest

    def near_block(t, i, carry):
        b = half * hs + i

        @pl.when(b != me)
        def _():
            for copy in near_copies(b, t, b):
                copy.wait_recv()

        base = pl.multiple_of(b * LANES, LANES)
        for j in range(3):
            to_wide(t, j, b)
        for p in range(LANES // ROWS):
            first = base + p * ROWS
            rows = pl.ds(first, ROWS)
            kept = pl.ds(pl.multiple_of(i * LANES, LANES) + p * ROWS, ROWS)
            one, two = feature(t, 1, first, ROWS), feature(t, 2, first, ROWS)
            feat[0, kept, :] = one
            feat[1, kept, :] = two
            keep(mixed, rows, one * two)
            keep(gated, rows, cot_rows(t, b, p * ROWS, ROWS) * feature(t, 0, first, ROWS))
        return carry

    def far_block(early, t, i, carry):
        b = (1 - half) * hs + i
        base = pl.multiple_of(b * LANES, LANES)
        for copy in gate_copies(b, t, b) if early else (mix_copy(b, t, b),):
            copy.wait_recv()
        for j in (0,) if early else (1, 2):
            to_wide(t, j, b)
        for p in range(LANES // ROWS):
            first = base + p * ROWS
            rows = pl.ds(first, ROWS)
            if early:
                gate = feature(t, 0, first, ROWS)
                keep(gated, rows, cot_rows(t, b, p * ROWS, ROWS) * gate)
            else:
                keep(mixed, rows, feature(t, 1, first, ROWS) * feature(t, 2, first, ROWS))
        return carry

    flip = (
        lax.broadcasted_iota(jnp.int32, (WIDE, WIDE), 0)
        + lax.broadcasted_iota(jnp.int32, (WIDE, WIDE), 1)
        == WIDE - 1
    ).astype(jnp.float32).astype(jnp.bfloat16)

    def add_gram(pairs):
        for b in sorted({b for b, _ in pairs}):
            left = dot32(flip, mixed[b * WIDE : (b + 1) * WIDE, :]).astype(jnp.bfloat16)
            for c in sorted(c for first, c in pairs if first == b):
                right = gated[c * WIDE : (c + 1) * WIDE, :]
                top = right[:, :LANES]
                cols = slice((c - b) * WIDE, (c - b + 1) * WIDE)
                gram[:, cols] += dot32_t(left, jnp.concatenate([top, top], 1)) + dot32_t(
                    left[:, :LANES], right[:, LANES:]
                )

    def conv_of(b, first, last, rows=WIDE):
        start = total - (b + 1) * WIDE
        cols = slice(start + first, start + last)
        return dot_three(low_hi[:rows, cols], low_lo[:rows, cols], mixed[first:last, :])

    def corr_of(a, first, last, rows=WIDE):
        cols = slice(first - a * WIDE, last - a * WIDE)
        return dot_three(up_hi[:rows, cols], up_lo[:rows, cols], gated[first:last, :])

    def grads_of(t, rows, conv=None, corr=None):
        if conv is not None:
            size = min(rows.stop - rows.start, LANES)
            blocks = range(rows.start // LANES, max(rows.stop // LANES, rows.start // LANES + 1))
            grads = [cot_rows(t, half * hs + b, 0, size) for b in blocks]
            fgrad[0, rows, :] = jnp.concatenate(grads, 0) * conv
        if corr is not None:
            fgrad[1, rows, :] = corr * feat[1, rows, :]
            fgrad[2, rows, :] = corr * feat[0, rows, :]

    per = span // WIDE
    local_rows = [slice(b * WIDE, (b + 1) * WIDE) for b in range(per)]
    edge = slice(span, span + 16)
    near_pairs = [(b, c) for b in range(per) for c in range(b, per)]
    far_pairs = [(b, c) for b in range(per) for c in range(per, 2 * per)]

    def early_part(t):
        for j in (1, 2):
            wide[j, 8 + span : 8 + span + 16, :] = halo[t, place[j]].astype(jnp.float32)
        lax.fori_loop(0, hs, functools.partial(near_block, t), 0)
        mixed[span : span + LANES, :] = jnp.zeros((LANES, WIDE), jnp.bfloat16)
        one, two = feature(t, 1, span, 16), feature(t, 2, span, 16)
        feat[0, edge, :] = one
        feat[1, edge, :] = two
        keep(mixed, edge, one * two)
        for b in range(per):
            grads_of(t, local_rows[b], conv=conv_of(b, 0, (b + 1) * WIDE))
            part[local_rows[b], :] = corr_of(b, b * WIDE, span)
        part_edge[...] = conv_of(per, 0, span + LANES, 16)
        add_gram(near_pairs)
        lax.fori_loop(0, hs, functools.partial(far_block, True, t), 0)
        for b in range(per):
            grads_of(t, local_rows[b], corr=part[local_rows[b], :] + corr_of(b, span, total))
        grads_of(t, edge, conv=part_edge[...], corr=corr_of(per, span, total, 16))

    def late_part(t):
        for j in range(3):
            wide[j, 8 + span - 16 : 8 + span, :] = halo[t, place[j]].astype(jnp.float32)
        lax.fori_loop(0, hs, functools.partial(near_block, t), 0)
        for b in range(per):
            grads_of(t, local_rows[b], corr=corr_of(per + b, span + b * WIDE, total))
            part[local_rows[b], :] = conv_of(per + b, span, span + (b + 1) * WIDE)
        add_gram([(per + b, per + c) for b, c in near_pairs])
        lax.fori_loop(0, hs, functools.partial(far_block, False, t), 0)
        for b in range(per):
            grads_of(t, local_rows[b], conv=part[local_rows[b], :] + conv_of(per + b, 0, span))

    def finish_block(t, i, carry):
        b = lax.rem(mine + 1 + i, hs)
        base = pl.multiple_of(b * LANES, LANES)
        for p in range(LANES // ROWS):
            first = base + p * ROWS
            for j in range(3):
                acc = jnp.zeros((ROWS, LANES), jnp.float32)
                source = wide[j, pl.ds(own_base + first + 8, ROWS), :]
                for k in range(kt):
                    shifted = fgrad[j, pl.ds(first + k, ROWS), :]
                    acc = acc + weight[t, j, k : k + 1, :] * shifted
                    terms = (shifted * source).reshape(ROWS // 8, 8, LANES)
                    gs_acc[t, j, k] += jnp.sum(terms, 0)
                gp_send[t, j, pl.ds(first, ROWS), :] = acc.astype(jnp.bfloat16)

        @pl.when(i < hs - 1)
        def _():
            gp_copy(half * hs + b, t, me).start()

        return carry

    def gp_copy(q, t, src):
        return send_to(
            gp_send.at[t, :, tile(lax.rem(q, hs)), :], gp_out.at[:, :, lanes_of(src, t)],
            gp_ssem.at[t, q], gp_rsem.at[t, src], (q, mych),
        )

    filter_scale = 1.0 / math.sqrt(total * group_owners * WIDE)
    fa_copy = lambda q, src: send_to(
        fa_send.at[q], fa_recv.at[src], fa_ssem.at[q], fa_rsem.at[src], (q, mych)
    )

    def one_tile(t, carry):
        @pl.when(half == 0)
        def _():
            early_part(t)

        @pl.when(half == 1)
        def _():
            late_part(t)

        lax.fori_loop(0, hs - 1, functools.partial(finish_block, t), 0)

        @pl.when(t == half)
        def _():
            add_gram(far_pairs)

        @pl.when(t == 1)
        def _():
            for d, line in enumerate(diagonal_sums(gram, ns)):
                fa_send[d] = jnp.broadcast_to(line * filter_scale, (8, LANES))
            for q in everyone:
                fa_copy(q, me).start()
            fa_recv[me] = fa_send[me]

        finish_block(t, hs - 1, carry)
        gp_out[:, :, lanes_of(me, t)] = gp_send[t, :, tile(mine), :]
        return carry

    lax.fori_loop(0, 2, one_tile, 0)

    short_scale = 1.0 / math.sqrt(total)
    for t in range(2):
        for j in range(3):
            lines = [jnp.sum(gs_acc[t, j, k], 0, keepdims=True) for k in range(kt)]
            lines += [jnp.zeros((1, LANES), jnp.float32)] * (8 - kt)
            gs_send[t, j] = jnp.concatenate(lines, 0) * short_scale
    partner = far[0]
    pair = send_to(gs_send, gs_pair, pair_sem.at[0], pair_sem.at[1], (partner, mych))
    pair.start()

    for q in everyone:
        fa_copy(q, q).wait_recv()
    for g in range(groups):
        owners = [h * hs + g * group_owners + i for h in range(2) for i in range(group_owners)]
        summed = fa_recv[owners[0]]
        for q in owners[1:]:
            summed = summed + fa_recv[q]
        fb_send[g] = summed
    fb_copy = lambda c, src: send_to(
        fb_send, fb_recv.at[src], fb_ssem.at[c], fb_rsem.at[src], (me, c)
    )
    for _, c in ch_peers:
        fb_copy(c, mych).start()
    fb_recv[mych] = fb_send[...]
    pair.wait()
    gs_sum[...] = gs_send[...] + gs_pair[...]
    gs_copy = lambda q, src: send_to(
        gs_sum, gs_recv.at[lax.rem(src, hs)], gs_ssem.at[q], gs_rsem.at[src], (q, mych)
    )
    for q in near:
        gs_copy(q, me).start()
    gs_recv[mine] = gs_sum[...]

    for _, c in ch_peers:
        fb_copy(c, c).wait_recv()
    width = LANES // nc
    for c in range(nc):
        for g in range(groups):
            line = fb_recv[c, g]
            piece = line[:, 0:width]
            for other in range(1, nc):
                piece = jnp.where(
                    mych == other, line[:, other * width : (other + 1) * width], piece
                )
            at = c * groups + g
            gf_out[at : at + 1, :] = piece[0:1, :]

    for q in near:
        gs_copy(q, q).wait_recv()
    for q in range(hs):
        for t in range(2):
            lanes = slice((2 * q + t) * LANES, (2 * q + t + 1) * LANES)
            for j in range(3):
                gs_out[j, :, lanes] = gs_recv[q, t, j, 0:kt, :]

    for q in everyone:
        tap_copy(q, me).wait_send()
        fa_copy(q, me).wait_send()
    for q in near:
        gs_copy(q, me).wait_send()
        for t in range(2):
            for copy in near_copies(q, t, me):
                copy.wait_send()
            gp_copy(q, t, me).wait_send()
            gp_copy(q, t, q).wait_recv()
    for _, c in ch_peers:
        fb_copy(c, mych).wait_send()

    @pl.when(half == 0)
    def _():
        for q in far:
            for t in range(2):
                mix_copy(q, t, me).wait_send()

    @pl.when(half == 1)
    def _():
        for q in far:
            for t in range(2):
                for copy in gate_copies(q, t, me):
                    copy.wait_send()

    @pl.when((me == hs - 1) | (me == hs))
    def _():
        for q in far:
            for t in range(2):
                halo_copy(q, t, me, 0).wait_send()


def resident(projected, cotangent, short_weight, long_filter):
    row_count, streams, chan_count = projected.shape
    kt = short_weight.shape[1]
    groups = long_filter.shape[0]
    ns, nc = lax.axis_size("seq"), lax.axis_size("ch")
    total = row_count * ns
    span = total // 2
    f32, bf16 = jnp.float32, jnp.bfloat16
    dma = pltpu.SemaphoreType.DMA
    vmem = pl.BlockSpec(memory_space=pltpu.VMEM)
    anywhere = pl.BlockSpec(memory_space=pltpu.HBM)
    operands = [
        pltpu.with_memory_space_constraint(x, pltpu.HBM)
        for x in (jnp.transpose(projected, (1, 0, 2)), cotangent, short_weight, long_filter)
    ]
    grad_proj, grad_short, grad_filter = pl.pallas_call(
        functools.partial(resident_kernel, ns, nc, kt, groups),
        out_shape=(
            jax.ShapeDtypeStruct((streams, row_count, chan_count), bf16),
            jax.ShapeDtypeStruct((streams, kt, chan_count), f32),
            jax.ShapeDtypeStruct((groups * nc, row_count // nc), f32),
        ),
        in_specs=[anywhere] * 4,
        out_specs=(vmem, vmem, vmem),
        scratch_shapes=[
            pltpu.VMEM((2, 3, kt, LANES), f32),
            pltpu.VMEM((groups, LANES), f32),
            pltpu.VMEM((ns, 4, LANES, LANES), bf16),
            pltpu.VMEM((2, ns, 4, LANES, LANES), bf16),
            pltpu.VMEM((2, 3, 16, LANES), bf16),
            pltpu.VMEM((3, total + 8, LANES), f32),
            pltpu.VMEM((2, span + 16, LANES), f32),
            pltpu.VMEM((total, WIDE), bf16),
            pltpu.VMEM((total, WIDE), bf16),
            pltpu.VMEM((span, LANES), f32),
            pltpu.VMEM((16, LANES), f32),
            pltpu.VMEM((3, span + 16, LANES), f32),
            pltpu.VMEM((2, 3, span, LANES), bf16),
            pltpu.VMEM((groups, 8, LANES), f32),
            pltpu.VMEM((ns, 8, LANES), f32),
            pltpu.VMEM((WIDE, total), bf16),
            pltpu.VMEM((WIDE, total), bf16),
            pltpu.VMEM((WIDE, total), bf16),
            pltpu.VMEM((WIDE, total), bf16),
            pltpu.VMEM((WIDE, total), f32),
            pltpu.VMEM((ns, 8, LANES), f32),
            pltpu.VMEM((ns, 8, LANES), f32),
            pltpu.VMEM((groups, 8, LANES), f32),
            pltpu.VMEM((nc, groups, 8, LANES), f32),
            pltpu.VMEM((2, 3, 8, 8, LANES), f32),
            pltpu.VMEM((2, 3, 8, LANES), f32),
            pltpu.VMEM((2, 3, 8, LANES), f32),
            pltpu.VMEM((2, 3, 8, LANES), f32),
            pltpu.VMEM((ns // 2, 2, 3, 8, LANES), f32),
            dma((3,)), dma((3, ns)),
            dma((ns,)), dma((ns,)),
            dma((2, 2, ns)), dma((2, 2, ns)),
            dma((2, ns)), dma((2, ns)),
            dma((ns,)), dma((ns,)),
            dma((ns,)), dma((ns,)),
            dma((nc,)), dma((nc,)),
            dma((2,)),
        ],
        compiler_params=pltpu.CompilerParams(
            collective_id=0, has_side_effects=True, vmem_limit_bytes=48 * 1024 * 1024
        ),
    )(*operands)
    return jnp.transpose(grad_proj, (1, 0, 2)), grad_short, grad_filter


def spread(projected, cotangent, short_weight, long_filter):
    tap_count = short_weight.shape[1]
    row_count = projected.shape[0]
    margin = tap_count - 1
    front_rows = passed_along(projected[row_count - margin :], "seq", 1)
    extended = jnp.concatenate([front_rows, projected], 0)
    features = featurize(extended, short_weight, row_count)
    grad_out = cotangent.astype(jnp.float32)
    mixed_input = features[:, 1] * features[:, 2]
    gated_grad = grad_out * features[:, 0]
    conv_out, corr_out, filt_grad = sequence_plan(mixed_input, gated_grad, long_filter)
    token_count = row_count * lax.axis_size("seq")
    group_width = mixed_input.shape[1] // long_filter.shape[0]
    scaled_grad = filt_grad * (1.0 / math.sqrt(token_count * group_width))
    owned_grad = lax.all_to_all(scaled_grad, "ch", split_axis=1, concat_axis=0, tiled=True)
    feat_grad = jnp.stack(
        [grad_out * conv_out, corr_out * features[:, 2], corr_out * features[:, 1]], 1
    )
    next_rows = passed_along(feat_grad[:margin].astype(jnp.bfloat16), "seq", -1).astype(jnp.float32)
    extended_grad = jnp.concatenate([feat_grad, next_rows], 0)
    grad_proj = jnp.zeros(feat_grad.shape, jnp.float32)
    for offset in range(tap_count):
        grad_proj = (
            grad_proj + short_weight[:, offset, :] * extended_grad[offset : offset + row_count]
        )
    short_terms = []
    for offset in range(tap_count):
        first_row = margin - offset
        short_terms.append(
            jnp.sum(feat_grad * extended[first_row : first_row + row_count].astype(jnp.float32), 0)
        )
    grad_short = lax.psum(jnp.stack(short_terms, 1), "seq") * (1.0 / math.sqrt(token_count))
    return (grad_proj.astype(jnp.bfloat16), grad_short, owned_grad)


def local(projected, cotangent, short_weight, long_filter):
    row_count, _, chan_count = projected.shape
    seq_count = lax.axis_size("seq")
    group_width = chan_count // long_filter.shape[0]
    fits = (
        row_count == LANES
        and seq_count % 4 == 0
        and chan_count == WIDE * (seq_count // 2)
        and group_width % WIDE == 0
        and short_weight.shape[1] <= 8
    )
    plan = resident if fits else spread
    return plan(projected, cotangent, short_weight, long_filter)


def solution(mesh):
    return jax.shard_map(
        local,
        mesh=mesh,
        in_specs=(P("seq", None, "ch"), P("seq", "ch"), P(None, None, "ch"), P("ch", "seq")),
        out_specs=(P("seq", None, "ch"), P(None, None, "ch"), P(None, ("seq", "ch"))),
        check_vma=False,
    )
```

```python
import functools
import math

import jax
import jax.numpy as jnp
from jax import lax
from jax.experimental import pallas as pl
from jax.experimental.pallas import tpu as pltpu
from jax.sharding import PartitionSpec as P

highest = lax.Precision.HIGHEST
MESH = pl.DeviceIdType.MESH
LANES = 128
WIDE = 256
ROWS = 64


def passed_along(block, axis, distance):
    devices = range(lax.axis_size(axis))
    route = [(i - distance, i) for i in devices if i - distance in devices]
    return lax.ppermute(block, axis, route)


def einsum_high(form, table, operand):
    return jnp.einsum(form, table, operand, precision=highest)


def angle_table(first, second, length):
    product = first[:, None] * second[None, :] % length
    radians = product.astype(jnp.float32) * (2.0 * math.pi / length)
    return (jnp.cos(radians), jnp.sin(radians))


def complex_dft(cosine, sine, real_part, imag_part, joined, sign):
    table = jnp.stack(
        [jnp.stack([cosine, -sign * sine], 0), jnp.stack([sign * sine, cosine], 0)], 0
    )
    stacked = jnp.stack([real_part, imag_part], 0)
    result = jnp.einsum(joined, table, stacked, precision=highest)
    return (result[0], result[1])


def rotate(real_part, imag_part, cosine, sine, sign):
    return (
        real_part * cosine - sign * imag_part * sine,
        imag_part * cosine + sign * real_part * sine,
    )


def combine(mixed_re, mixed_im, grad_re, grad_im, filt_re, filt_im):
    conv_re = filt_re * mixed_re - filt_im * mixed_im
    conv_im = filt_re * mixed_im + filt_im * mixed_re
    corr_re = filt_re * grad_re + filt_im * grad_im
    corr_im = filt_re * grad_im - filt_im * grad_re
    cross_re = mixed_re * grad_re + mixed_im * grad_im
    cross_im = mixed_re * grad_im - mixed_im * grad_re
    return (conv_re - corr_im, conv_im + corr_re, cross_re, cross_im)


def featurize(extended, weights, row_count):
    tap_count = weights.shape[1]
    accumulated = jnp.zeros((row_count,) + extended.shape[1:], jnp.float32)
    for offset in range(tap_count):
        first_row = tap_count - 1 - offset
        accumulated = accumulated + weights[:, offset, :] * extended[
            first_row : first_row + row_count
        ].astype(jnp.float32)
    return accumulated


def transpose_pair(signals, filters):
    return (
        lax.all_to_all(signals, "seq", split_axis=0, concat_axis=1, tiled=True),
        lax.all_to_all(filters, "seq", split_axis=0, concat_axis=1, tiled=True),
    )


def sequence_plan(mixed_input, gated_grad, long_filter):
    row_count, chan_count = mixed_input.shape
    group_count = long_filter.shape[0]
    seq_count = lax.axis_size("seq")
    seq_index = lax.axis_index("seq")
    per_block = row_count // seq_count
    fft_length = 2 * row_count * seq_count
    freq_index = jnp.arange(2 * seq_count, dtype=jnp.int32)
    block_index = jnp.arange(seq_count, dtype=jnp.int32)
    row_index = jnp.arange(row_count, dtype=jnp.int32)
    signals = jnp.stack([mixed_input, gated_grad], 1)[:, None]
    filters = jnp.transpose(long_filter)[:, None]
    sig_cols, filt_cols = transpose_pair(signals, filters)
    cos_one, sin_one = angle_table(freq_index, block_index, 2 * seq_count)
    sig_re = einsum_high("kb,abxc->kaxc", cos_one, sig_cols)
    sig_im = -einsum_high("kb,abxc->kaxc", sin_one, sig_cols)
    filt_re = einsum_high("kb,abg->kag", cos_one, filt_cols)
    filt_im = -einsum_high("kb,abg->kag", sin_one, filt_cols)
    positions = seq_index * per_block + jnp.arange(per_block, dtype=jnp.int32)
    cos_twist, sin_twist = angle_table(freq_index, positions, fft_length)
    sig_re, sig_im = rotate(
        sig_re, sig_im, cos_twist[:, :, None, None], sin_twist[:, :, None, None], -1.0
    )
    filt_re, filt_im = rotate(filt_re, filt_im, cos_twist[:, :, None], sin_twist[:, :, None], -1.0)
    sig_rows, filt_rows = transpose_pair(
        jnp.stack([sig_re, sig_im], 2), jnp.stack([filt_re, filt_im], 2)
    )
    cos_two, sin_two = angle_table(row_index, row_index, row_count)
    spec_re, spec_im = complex_dft(
        cos_two, sin_two, sig_rows[:, :, 0], sig_rows[:, :, 1], "pqka,qjaxc->pjkxc", -1.0
    )
    hspec_re, hspec_im = complex_dft(
        cos_two, sin_two, filt_rows[:, :, 0], filt_rows[:, :, 1], "pqka,qjag->pjkg", -1.0
    )
    leading = spec_re.shape[:2]
    group_shape = leading + (group_count, chan_count // group_count)
    wave_re, wave_im, cross_re, cross_im = combine(
        spec_re[:, :, 0].reshape(group_shape),
        spec_im[:, :, 0].reshape(group_shape),
        spec_re[:, :, 1].reshape(group_shape),
        spec_im[:, :, 1].reshape(group_shape),
        hspec_re[..., None],
        hspec_im[..., None],
    )
    wave_re = wave_re.reshape(leading + (chan_count,))
    wave_im = wave_im.reshape(leading + (chan_count,))
    cross_re = jnp.sum(cross_re, -1)
    cross_im = jnp.sum(cross_im, -1)
    back_re, back_im = complex_dft(cos_two, sin_two, wave_re, wave_im, "pqak,qjkc->pajc", 1.0)
    cback_re, cback_im = complex_dft(cos_two, sin_two, cross_re, cross_im, "pqak,qjkg->pajg", 1.0)
    pair_freq = seq_index * 2 + jnp.arange(2, dtype=jnp.int32)
    cos_back, sin_back = angle_table(row_index, pair_freq, fft_length)
    back_re, back_im = rotate(back_re, back_im, cos_back[:, :, None], sin_back[:, :, None], 1.0)
    cback_re, cback_im = rotate(cback_re, cback_im, cos_back[:, :, None], sin_back[:, :, None], 1.0)
    wave_cols, cross_cols = transpose_pair(
        jnp.stack([back_re, back_im], 2), jnp.stack([cback_re, cback_im], 2)
    )
    cos_three, sin_three = angle_table(block_index, freq_index, 2 * seq_count)
    time_re, time_im = complex_dft(
        cos_three, sin_three, wave_cols[:, :, 0], wave_cols[:, :, 1], "pqbk,qakc->pbac", 1.0
    )
    cross_time = einsum_high("bk,akg->bag", cos_three, cross_cols[:, :, 0]) - einsum_high(
        "bk,akg->bag", sin_three, cross_cols[:, :, 1]
    )
    inverse_scale = 1.0 / fft_length
    wave_out, cross_out = transpose_pair(
        jnp.stack([time_re, time_im], 2) * inverse_scale, cross_time * inverse_scale
    )
    return (wave_out[0, :, 0], wave_out[0, :, 1], jnp.transpose(cross_out[0]))


def split_halves(value):
    top = value.astype(jnp.bfloat16)
    rest = (value - top.astype(jnp.float32)).astype(jnp.bfloat16)
    return top, rest


def dot32(left, right):
    return jnp.dot(left, right, preferred_element_type=jnp.float32)


def dot32_t(left, right):
    return lax.dot_general(
        left, right, (((1,), (1,)), ((), ())), preferred_element_type=jnp.float32
    )


def tile(index, width=LANES):
    return pl.ds(pl.multiple_of(index * width, width), width)


def send_to(src, dst, send_sem, recv_sem, peer):
    return pltpu.make_async_remote_copy(
        src_ref=src,
        dst_ref=dst,
        send_sem=send_sem,
        recv_sem=recv_sem,
        device_id=peer,
        device_id_type=MESH,
    )


def build_filters(taps, ns, low_hi, low_lo, up_hi, up_lo):
    row = lax.broadcasted_iota(jnp.int32, (LANES, LANES), 0)
    col = lax.broadcasted_iota(jnp.int32, (LANES, LANES), 1)
    flip = (row + col == LANES - 1).astype(jnp.float32)
    zero = jnp.zeros((LANES, LANES), jnp.float32)
    zero16 = zero.astype(jnp.bfloat16)
    flipped = jnp.dot(
        taps[...].reshape(ns * 8, LANES), flip, precision=highest,
        preferred_element_type=jnp.float32,
    )
    last_up, last_low = zero, zero
    top = ns - WIDE // LANES
    low_hi[:, (ns - 1) * LANES :] = jnp.concatenate([zero16, zero16], 0)
    low_lo[:, (ns - 1) * LANES :] = jnp.concatenate([zero16, zero16], 0)
    up_hi[LANES:, :LANES] = zero16
    up_lo[LANES:, :LANES] = zero16
    for d in range(ns):
        forward = jnp.concatenate([taps[d]] * (LANES // 8), 0)
        back = jnp.concatenate([flipped[d * 8 : d * 8 + 8]] * (LANES // 8), 0)
        forward = pltpu.roll(forward, 0, 1, stride=1, stride_axis=0)
        back = pltpu.roll(back, 1, 1, stride=1, stride_axis=0)
        up = split_halves(jnp.where(col >= row, forward, last_up))
        low = split_halves(jnp.where(row >= col, back, last_low))
        last_up, last_low = forward, back
        for u in range(WIDE // LANES):
            v = d + u
            if v < ns:
                up_hi[u * LANES : (u + 1) * LANES, v * LANES : (v + 1) * LANES] = up[0]
                up_lo[u * LANES : (u + 1) * LANES, v * LANES : (v + 1) * LANES] = up[1]
            v = top + u - d
            if 0 <= v < ns:
                low_hi[u * LANES : (u + 1) * LANES, v * LANES : (v + 1) * LANES] = low[0]
                low_lo[u * LANES : (u + 1) * LANES, v * LANES : (v + 1) * LANES] = low[1]


def diagonal_sums(gram, ns):
    row = lax.broadcasted_iota(jnp.int32, (LANES, LANES), 0)
    col = lax.broadcasted_iota(jnp.int32, (LANES, LANES), 1)
    turned = []
    for d in range(ns):
        block = gram[LANES:, d * LANES : (d + 1) * LANES]
        if d + 1 < ns:
            block = block + gram[:LANES, (d + 1) * LANES : (d + 2) * LANES]
        turned.append(pltpu.roll(block, 1, 1, stride=1, stride_axis=0))
    turned.append(jnp.zeros((LANES, LANES), jnp.float32))
    return [
        jnp.sum(jnp.where(col <= row, turned[d], turned[d + 1]), 0, keepdims=True)
        for d in range(ns)
    ]


def dot_three(hi, lo, signal):
    width = signal.shape[1] // 2
    both = dot32(hi, signal)
    return both[:, :width] + both[:, width:] + dot32(lo, signal[:, :width])


EARLY = (slice(0, 1), slice(1, 3))
LATE = (slice(1, 3), slice(0, 1))


def resident_kernel(
    ns, nc, kt, groups,
    proj, cot, weight_in, filt_in,
    gp_out, gs_out, gf_out,
    weight, filt, packed, pin, halo, wide, feat, mixed, gated, part, fgrad, gp_send,
    tap_send, taps, low_hi, low_lo, up_hi, up_lo, gram,
    fa_send, fa_recv, fb_send, fb_recv, gs_acc, gs_send, gs_pair, gs_sum, gs_recv,
    local_sem, pack_sem, tap_ssem, tap_rsem, in_send, in_recv, gp_ssem, gp_rsem, gs_ssem, gs_rsem,
    fa_ssem, fa_rsem, fb_ssem, fb_rsem, pair_sem,
):
    me = lax.axis_index("seq")
    mych = lax.axis_index("ch")
    hs = ns // 2
    total = ns * LANES
    span = total // 2
    half = me // hs
    mine = lax.rem(me, hs)
    own_base = pl.multiple_of(half * span, span)
    group_owners = hs // groups
    near = [half * hs + lax.rem(mine + i, hs) for i in range(1, hs)]
    far = [(1 - half) * hs + lax.rem(mine + i, hs) for i in range(hs)]
    everyone = near + far
    ch_peers = [(me, lax.rem(mych + i, nc)) for i in range(1, nc)]
    lanes_of = lambda q, t: tile(lax.rem(q, hs) * 2 + t)

    own = [
        pltpu.make_async_copy(filt_in, filt, local_sem.at[0]),
    ]
    for t in range(2):
        own.append(
            pltpu.make_async_copy(
                weight_in.at[:, :, lanes_of(me, t)], weight.at[t], local_sem.at[1 + t]
            )
        )
    packs = []
    for c in range(2 * hs):
        lanes = slice(c * LANES, (c + 1) * LANES)
        packs += [
            pltpu.make_async_copy(
                proj.at[1:3, :, lanes], packed.at[c, 0:2], pack_sem.at[0, c]
            ),
            pltpu.make_async_copy(
                proj.at[0:1, :, lanes], packed.at[c, 2:3], pack_sem.at[1, c]
            ),
            pltpu.make_async_copy(cot.at[:, lanes], packed.at[c, 3], pack_sem.at[2, c]),
        ]
    own += packs
    for copy in own:
        copy.start()
    barrier = pltpu.get_barrier_semaphore()
    for q in everyone:
        pl.semaphore_signal(barrier, inc=1, device_id=(q, mych), device_id_type=MESH)
    for peer in ch_peers:
        pl.semaphore_signal(barrier, inc=1, device_id=peer, device_id_type=MESH)
    own[0].wait()
    for g in range(groups):
        tap_send[g] = jnp.broadcast_to(filt[g : g + 1, :], (8, LANES))
    pl.semaphore_wait(barrier, ns + nc - 2)

    def tap_copy(q, src):
        return send_to(
            tap_send.at[lax.rem(q, hs) // group_owners], taps.at[src],
            tap_ssem.at[q], tap_rsem.at[src], (q, mych),
        )

    def halo_copy(q, t, src, first):
        return send_to(
            packed.at[lax.rem(q, hs) * 2 + t, :, pl.ds(first, 16)], halo.at[t],
            in_send.at[t, 1, q], in_recv.at[t, 1, 0], (q, mych),
        )

    def stream_copy(q, t, src, streams):
        return send_to(
            packed.at[lax.rem(q, hs) * 2 + t, streams], pin.at[t, src, streams],
            in_send.at[t, 0, q], in_recv.at[t, 0, src], (q, mych),
        )

    def near_copies(q, t, src):
        return (stream_copy(q, t, src, slice(0, 4)),)

    def mix_copy(q, t, src):
        return stream_copy(q, t, src, slice(0, 2))

    def gate_copies(q, t, src):
        return (stream_copy(q, t, src, slice(2, 4)),)

    for q in everyone:
        tap_copy(q, me).start()
    for copy in packs:
        copy.wait()

    @pl.when(me == hs - 1)
    def _():
        for t in range(2):
            for q in far:
                halo_copy(q, t, me, LANES - 16).start()

    @pl.when(me == hs)
    def _():
        for t in range(2):
            for q in far:
                halo_copy(q, t, me, 0).start()

    for t in range(2):
        for i in range(hs):
            @pl.when(half == 0)
            def _():
                mix_copy(far[i], t, me).start()

            @pl.when(half == 1)
            def _():
                for copy in gate_copies(far[i], t, me):
                    copy.start()

            if i < hs - 1:
                for copy in near_copies(near[i], t, me):
                    copy.start()

    taps[me] = tap_send[mine // group_owners]
    gram[...] = jnp.zeros(gram.shape, jnp.float32)
    for j in range(3):
        wide[j, 0:8, :] = jnp.zeros((8, LANES), jnp.float32)
        fgrad[j, span : span + 16, :] = jnp.zeros((16, LANES), jnp.float32)
        for t in range(2):
            for k in range(kt):
                gs_acc[t, j, k] = jnp.zeros((8, LANES), jnp.float32)
    for q in everyone:
        tap_copy(q, q).wait_recv()
    build_filters(taps, ns, low_hi, low_lo, up_hi, up_lo)
    for copy in own[1:3]:
        copy.wait()
    for t in range(2):
        pin[t, me] = packed[mine * 2 + t]
    for t in range(2):
        halo_copy(far[0], t, 0, 0).wait_recv()

    place = (2, 0, 1)

    def to_wide(t, j, b):
        first = pl.multiple_of(b * LANES, LANES)
        block = pin[t, b, place[j]]
        wide[j, pl.ds(first + 8, LANES), :] = block.astype(jnp.float32)

    def cot_rows(t, b, first, rows):
        return pin[t, b, 3, pl.ds(first, rows), :].astype(jnp.float32)

    def feature(t, j, first, rows):
        acc = jnp.zeros((rows, LANES), jnp.float32)
        for k in range(kt):
            acc = acc + weight[t, j, k : k + 1, :] * wide[j, pl.ds(first + 8 - k, rows), :]
        return acc

    def keep(store, rows, value):
        top, rest = split_halves(value)
        store[rows, 0:LANES] = top
        store[rows, LANES:] = rest

    def near_block(t, i, carry):
        b = half * hs + i

        @pl.when(b != me)
        def _():
            for copy in near_copies(b, t, b):
                copy.wait_recv()

        base = pl.multiple_of(b * LANES, LANES)
        for j in range(3):
            to_wide(t, j, b)
        for p in range(LANES // ROWS):
            first = base + p * ROWS
            rows = pl.ds(first, ROWS)
            kept = pl.ds(pl.multiple_of(i * LANES, LANES) + p * ROWS, ROWS)
            one, two = feature(t, 1, first, ROWS), feature(t, 2, first, ROWS)
            feat[0, kept, :] = one
            feat[1, kept, :] = two
            keep(mixed, rows, one * two)
            keep(gated, rows, cot_rows(t, b, p * ROWS, ROWS) * feature(t, 0, first, ROWS))
        return carry

    def far_block(early, t, i, carry):
        b = (1 - half) * hs + i
        base = pl.multiple_of(b * LANES, LANES)
        for copy in gate_copies(b, t, b) if early else (mix_copy(b, t, b),):
            copy.wait_recv()
        for j in (0,) if early else (1, 2):
            to_wide(t, j, b)
        for p in range(LANES // ROWS):
            first = base + p * ROWS
            rows = pl.ds(first, ROWS)
            if early:
                gate = feature(t, 0, first, ROWS)
                keep(gated, rows, cot_rows(t, b, p * ROWS, ROWS) * gate)
            else:
                keep(mixed, rows, feature(t, 1, first, ROWS) * feature(t, 2, first, ROWS))
        return carry

    flip = (
        lax.broadcasted_iota(jnp.int32, (WIDE, WIDE), 0)
        + lax.broadcasted_iota(jnp.int32, (WIDE, WIDE), 1)
        == WIDE - 1
    ).astype(jnp.float32).astype(jnp.bfloat16)

    def add_gram(pairs):
        for b in sorted({b for b, _ in pairs}):
            left = dot32(flip, mixed[b * WIDE : (b + 1) * WIDE, :]).astype(jnp.bfloat16)
            for c in sorted(c for first, c in pairs if first == b):
                right = gated[c * WIDE : (c + 1) * WIDE, :]
                top = right[:, :LANES]
                cols = slice((c - b) * WIDE, (c - b + 1) * WIDE)
                gram[:, cols] += dot32_t(left, jnp.concatenate([top, top], 1)) + dot32_t(
                    left[:, :LANES], right[:, LANES:]
                )

    def conv_of(b, first, last, rows=WIDE):
        start = total - (b + 1) * WIDE
        cols = slice(start + first, start + last)
        return dot_three(low_hi[:rows, cols], low_lo[:rows, cols], mixed[first:last, :])

    def corr_of(a, first, last, rows=WIDE):
        cols = slice(first - a * WIDE, last - a * WIDE)
        return dot_three(up_hi[:rows, cols], up_lo[:rows, cols], gated[first:last, :])

    def grads_of(t, rows, conv=None, corr=None):
        if conv is not None:
            size = min(rows.stop - rows.start, LANES)
            blocks = range(rows.start // LANES, max(rows.stop // LANES, rows.start // LANES + 1))
            grads = [cot_rows(t, half * hs + b, 0, size) for b in blocks]
            fgrad[0, rows, :] = jnp.concatenate(grads, 0) * conv
        if corr is not None:
            fgrad[1, rows, :] = corr * feat[1, rows, :]
            fgrad[2, rows, :] = corr * feat[0, rows, :]

    per = span // WIDE
    local_rows = [slice(b * WIDE, (b + 1) * WIDE) for b in range(per)]
    edge = slice(span, span + 16)
    near_pairs = [(b, c) for b in range(per) for c in range(b, per)]
    far_pairs = [(b, c) for b in range(per) for c in range(per, 2 * per)]

    def finish_block(streams, t, i, carry):
        b = lax.rem(mine + 1 + i, hs)
        base = pl.multiple_of(b * LANES, LANES)
        for p in range(LANES // ROWS):
            first = base + p * ROWS
            for j in range(streams.start, streams.stop):
                acc = jnp.zeros((ROWS, LANES), jnp.float32)
                source = wide[j, pl.ds(own_base + first + 8, ROWS), :]
                for k in range(kt):
                    shifted = fgrad[j, pl.ds(first + k, ROWS), :]
                    acc = acc + weight[t, j, k : k + 1, :] * shifted
                    terms = (shifted * source).reshape(ROWS // 8, 8, LANES)
                    gs_acc[t, j, k] += jnp.sum(terms, 0)
                gp_send[t, j, pl.ds(first, ROWS), :] = acc.astype(jnp.bfloat16)

        @pl.when(i < hs - 1)
        def _():
            gp_copy(half * hs + b, t, me, streams).start()

        return carry

    def gp_copy(q, t, src, streams):
        return send_to(
            gp_send.at[t, streams, tile(lax.rem(q, hs)), :],
            gp_out.at[streams, :, lanes_of(src, t)],
            gp_ssem.at[t, streams.start % 2, q], gp_rsem.at[t, streams.start % 2, src], (q, mych),
        )

    def early_part(t):
        for j in (1, 2):
            wide[j, 8 + span : 8 + span + 16, :] = halo[t, place[j]].astype(jnp.float32)
        lax.fori_loop(0, hs, functools.partial(near_block, t), 0)
        mixed[span : span + LANES, :] = jnp.zeros((LANES, WIDE), jnp.bfloat16)
        one, two = feature(t, 1, span, 16), feature(t, 2, span, 16)
        feat[0, edge, :] = one
        feat[1, edge, :] = two
        keep(mixed, edge, one * two)
        for b in range(per):
            grads_of(t, local_rows[b], conv=conv_of(b, 0, (b + 1) * WIDE))
            part[local_rows[b], :] = corr_of(b, b * WIDE, span)
        edge_conv = conv_of(per, 0, span + LANES, 16)
        fgrad[0, edge, :] = halo[t, 3].astype(jnp.float32) * edge_conv
        lax.fori_loop(0, hs, functools.partial(finish_block, EARLY[0], t), 0)
        add_gram(near_pairs)
        lax.fori_loop(0, hs, functools.partial(far_block, True, t), 0)
        for b in range(per):
            grads_of(t, local_rows[b], corr=part[local_rows[b], :] + corr_of(b, span, total))
        grads_of(t, edge, corr=corr_of(per, span, total, 16))
        lax.fori_loop(0, hs - 1, functools.partial(finish_block, EARLY[1], t), 0)

    def late_part(t):
        for j in range(3):
            wide[j, 8 + span - 16 : 8 + span, :] = halo[t, place[j]].astype(jnp.float32)
        lax.fori_loop(0, hs, functools.partial(near_block, t), 0)
        for b in range(per):
            grads_of(t, local_rows[b], corr=corr_of(per + b, span + b * WIDE, total))
            part[local_rows[b], :] = conv_of(per + b, span, span + (b + 1) * WIDE)
        lax.fori_loop(0, hs, functools.partial(finish_block, LATE[0], t), 0)
        add_gram([(per + b, per + c) for b, c in near_pairs])
        lax.fori_loop(0, hs, functools.partial(far_block, False, t), 0)
        for b in range(per):
            grads_of(t, local_rows[b], conv=part[local_rows[b], :] + conv_of(per + b, 0, span))
        lax.fori_loop(0, hs - 1, functools.partial(finish_block, LATE[1], t), 0)

    filter_scale = 1.0 / math.sqrt(total * group_owners * WIDE)
    fa_copy = lambda q, src: send_to(
        fa_send.at[q], fa_recv.at[src], fa_ssem.at[q], fa_rsem.at[src], (q, mych)
    )

    def one_tile(t, carry):
        @pl.when(half == 0)
        def _():
            early_part(t)

        @pl.when(half == 1)
        def _():
            late_part(t)

        @pl.when(t == half)
        def _():
            add_gram(far_pairs)

        @pl.when(t == 1)
        def _():
            for d, line in enumerate(diagonal_sums(gram, ns)):
                fa_send[d] = jnp.broadcast_to(line * filter_scale, (8, LANES))
            for q in everyone:
                fa_copy(q, me).start()
            fa_recv[me] = fa_send[me]

        @pl.when(half == 0)
        def _():
            finish_block(EARLY[1], t, hs - 1, carry)

        @pl.when(half == 1)
        def _():
            finish_block(LATE[1], t, hs - 1, carry)

        gp_out[:, :, lanes_of(me, t)] = gp_send[t, :, tile(mine), :]
        return carry

    lax.fori_loop(0, 2, one_tile, 0)

    short_scale = 1.0 / math.sqrt(total)
    for t in range(2):
        for j in range(3):
            lines = [jnp.sum(gs_acc[t, j, k], 0, keepdims=True) for k in range(kt)]
            lines += [jnp.zeros((1, LANES), jnp.float32)] * (8 - kt)
            gs_send[t, j] = jnp.concatenate(lines, 0) * short_scale
    partner = far[0]
    pair = send_to(gs_send, gs_pair, pair_sem.at[0], pair_sem.at[1], (partner, mych))
    pair.start()

    for q in everyone:
        fa_copy(q, q).wait_recv()
    for g in range(groups):
        owners = [h * hs + g * group_owners + i for h in range(2) for i in range(group_owners)]
        summed = fa_recv[owners[0]]
        for q in owners[1:]:
            summed = summed + fa_recv[q]
        fb_send[g] = summed
    fb_copy = lambda c, src: send_to(
        fb_send, fb_recv.at[src], fb_ssem.at[c], fb_rsem.at[src], (me, c)
    )
    for _, c in ch_peers:
        fb_copy(c, mych).start()
    fb_recv[mych] = fb_send[...]
    pair.wait()
    gs_sum[...] = gs_send[...] + gs_pair[...]
    gs_copy = lambda q, src: send_to(
        gs_sum, gs_recv.at[lax.rem(src, hs)], gs_ssem.at[q], gs_rsem.at[src], (q, mych)
    )
    for q in near:
        gs_copy(q, me).start()
    gs_recv[mine] = gs_sum[...]

    for _, c in ch_peers:
        fb_copy(c, c).wait_recv()
    width = LANES // nc
    for c in range(nc):
        for g in range(groups):
            line = fb_recv[c, g]
            piece = line[:, 0:width]
            for other in range(1, nc):
                piece = jnp.where(
                    mych == other, line[:, other * width : (other + 1) * width], piece
                )
            at = c * groups + g
            gf_out[at : at + 1, :] = piece[0:1, :]

    for q in near:
        gs_copy(q, q).wait_recv()
    for q in range(hs):
        for t in range(2):
            lanes = slice((2 * q + t) * LANES, (2 * q + t + 1) * LANES)
            for j in range(3):
                gs_out[j, :, lanes] = gs_recv[q, t, j, 0:kt, :]

    for q in everyone:
        tap_copy(q, me).wait_send()
        fa_copy(q, me).wait_send()
    for q in near:
        gs_copy(q, me).wait_send()
        for t in range(2):
            for copy in near_copies(q, t, me):
                copy.wait_send()
    for _, c in ch_peers:
        fb_copy(c, mych).wait_send()

    def returned(parts):
        for q in near:
            for t in range(2):
                for streams in parts:
                    gp_copy(q, t, me, streams).wait_send()
                    gp_copy(q, t, q, streams).wait_recv()

    @pl.when(half == 0)
    def _():
        returned(EARLY)
        for q in far:
            for t in range(2):
                mix_copy(q, t, me).wait_send()

    @pl.when(half == 1)
    def _():
        returned(LATE)
        for q in far:
            for t in range(2):
                for copy in gate_copies(q, t, me):
                    copy.wait_send()

    @pl.when((me == hs - 1) | (me == hs))
    def _():
        for q in far:
            for t in range(2):
                halo_copy(q, t, me, 0).wait_send()


def resident(projected, cotangent, short_weight, long_filter):
    row_count, streams, chan_count = projected.shape
    kt = short_weight.shape[1]
    groups = long_filter.shape[0]
    ns, nc = lax.axis_size("seq"), lax.axis_size("ch")
    total = row_count * ns
    span = total // 2
    f32, bf16 = jnp.float32, jnp.bfloat16
    dma = pltpu.SemaphoreType.DMA
    vmem = pl.BlockSpec(memory_space=pltpu.VMEM)
    anywhere = pl.BlockSpec(memory_space=pltpu.HBM)
    operands = [
        pltpu.with_memory_space_constraint(x, pltpu.HBM)
        for x in (jnp.transpose(projected, (1, 0, 2)), cotangent, short_weight, long_filter)
    ]
    grad_proj, grad_short, grad_filter = pl.pallas_call(
        functools.partial(resident_kernel, ns, nc, kt, groups),
        out_shape=(
            jax.ShapeDtypeStruct((streams, row_count, chan_count), bf16),
            jax.ShapeDtypeStruct((streams, kt, chan_count), f32),
            jax.ShapeDtypeStruct((groups * nc, row_count // nc), f32),
        ),
        in_specs=[anywhere] * 4,
        out_specs=(vmem, vmem, vmem),
        scratch_shapes=[
            pltpu.VMEM((2, 3, kt, LANES), f32),
            pltpu.VMEM((groups, LANES), f32),
            pltpu.VMEM((ns, 4, LANES, LANES), bf16),
            pltpu.VMEM((2, ns, 4, LANES, LANES), bf16),
            pltpu.VMEM((2, 4, 16, LANES), bf16),
            pltpu.VMEM((3, total + 8, LANES), f32),
            pltpu.VMEM((2, span + 16, LANES), f32),
            pltpu.VMEM((total, WIDE), bf16),
            pltpu.VMEM((total, WIDE), bf16),
            pltpu.VMEM((span, LANES), f32),
            pltpu.VMEM((3, span + 16, LANES), f32),
            pltpu.VMEM((2, 3, span, LANES), bf16),
            pltpu.VMEM((groups, 8, LANES), f32),
            pltpu.VMEM((ns, 8, LANES), f32),
            pltpu.VMEM((WIDE, total), bf16),
            pltpu.VMEM((WIDE, total), bf16),
            pltpu.VMEM((WIDE, total), bf16),
            pltpu.VMEM((WIDE, total), bf16),
            pltpu.VMEM((WIDE, total), f32),
            pltpu.VMEM((ns, 8, LANES), f32),
            pltpu.VMEM((ns, 8, LANES), f32),
            pltpu.VMEM((groups, 8, LANES), f32),
            pltpu.VMEM((nc, groups, 8, LANES), f32),
            pltpu.VMEM((2, 3, 8, 8, LANES), f32),
            pltpu.VMEM((2, 3, 8, LANES), f32),
            pltpu.VMEM((2, 3, 8, LANES), f32),
            pltpu.VMEM((2, 3, 8, LANES), f32),
            pltpu.VMEM((ns // 2, 2, 3, 8, LANES), f32),
            dma((3,)), dma((3, ns)),
            dma((ns,)), dma((ns,)),
            dma((2, 2, ns)), dma((2, 2, ns)),
            dma((2, 2, ns)), dma((2, 2, ns)),
            dma((ns,)), dma((ns,)),
            dma((ns,)), dma((ns,)),
            dma((nc,)), dma((nc,)),
            dma((2,)),
        ],
        compiler_params=pltpu.CompilerParams(
            collective_id=0, has_side_effects=True, vmem_limit_bytes=48 * 1024 * 1024
        ),
    )(*operands)
    return jnp.transpose(grad_proj, (1, 0, 2)), grad_short, grad_filter


def spread(projected, cotangent, short_weight, long_filter):
    tap_count = short_weight.shape[1]
    row_count = projected.shape[0]
    margin = tap_count - 1
    front_rows = passed_along(projected[row_count - margin :], "seq", 1)
    extended = jnp.concatenate([front_rows, projected], 0)
    features = featurize(extended, short_weight, row_count)
    grad_out = cotangent.astype(jnp.float32)
    mixed_input = features[:, 1] * features[:, 2]
    gated_grad = grad_out * features[:, 0]
    conv_out, corr_out, filt_grad = sequence_plan(mixed_input, gated_grad, long_filter)
    token_count = row_count * lax.axis_size("seq")
    group_width = mixed_input.shape[1] // long_filter.shape[0]
    scaled_grad = filt_grad * (1.0 / math.sqrt(token_count * group_width))
    owned_grad = lax.all_to_all(scaled_grad, "ch", split_axis=1, concat_axis=0, tiled=True)
    feat_grad = jnp.stack(
        [grad_out * conv_out, corr_out * features[:, 2], corr_out * features[:, 1]], 1
    )
    next_rows = passed_along(feat_grad[:margin].astype(jnp.bfloat16), "seq", -1).astype(jnp.float32)
    extended_grad = jnp.concatenate([feat_grad, next_rows], 0)
    grad_proj = jnp.zeros(feat_grad.shape, jnp.float32)
    for offset in range(tap_count):
        grad_proj = (
            grad_proj + short_weight[:, offset, :] * extended_grad[offset : offset + row_count]
        )
    short_terms = []
    for offset in range(tap_count):
        first_row = margin - offset
        short_terms.append(
            jnp.sum(feat_grad * extended[first_row : first_row + row_count].astype(jnp.float32), 0)
        )
    grad_short = lax.psum(jnp.stack(short_terms, 1), "seq") * (1.0 / math.sqrt(token_count))
    return (grad_proj.astype(jnp.bfloat16), grad_short, owned_grad)


def local(projected, cotangent, short_weight, long_filter):
    row_count, _, chan_count = projected.shape
    seq_count = lax.axis_size("seq")
    group_width = chan_count // long_filter.shape[0]
    fits = (
        row_count == LANES
        and seq_count % 4 == 0
        and chan_count == WIDE * (seq_count // 2)
        and group_width % WIDE == 0
        and short_weight.shape[1] <= 8
    )
    plan = resident if fits else spread
    return plan(projected, cotangent, short_weight, long_filter)


def solution(mesh):
    return jax.shard_map(
        local,
        mesh=mesh,
        in_specs=(P("seq", None, "ch"), P("seq", "ch"), P(None, None, "ch"), P("ch", "seq")),
        out_specs=(P("seq", None, "ch"), P(None, None, "ch"), P(None, ("seq", "ch"))),
        check_vma=False,
    )
```

```python
import functools
import math

import jax
import jax.numpy as jnp
from jax import lax
from jax.experimental import pallas as pl
from jax.experimental.pallas import tpu as pltpu
from jax.sharding import PartitionSpec as P

highest = lax.Precision.HIGHEST
MESH = pl.DeviceIdType.MESH
LANES = 128
WIDE = 256
ROWS = 128


def passed_along(block, axis, distance):
    devices = range(lax.axis_size(axis))
    route = [(i - distance, i) for i in devices if i - distance in devices]
    return lax.ppermute(block, axis, route)


def einsum_high(form, table, operand):
    return jnp.einsum(form, table, operand, precision=highest)


def angle_table(first, second, length):
    product = first[:, None] * second[None, :] % length
    radians = product.astype(jnp.float32) * (2.0 * math.pi / length)
    return (jnp.cos(radians), jnp.sin(radians))


def complex_dft(cosine, sine, real_part, imag_part, joined, sign):
    table = jnp.stack(
        [jnp.stack([cosine, -sign * sine], 0), jnp.stack([sign * sine, cosine], 0)], 0
    )
    stacked = jnp.stack([real_part, imag_part], 0)
    result = jnp.einsum(joined, table, stacked, precision=highest)
    return (result[0], result[1])


def rotate(real_part, imag_part, cosine, sine, sign):
    return (
        real_part * cosine - sign * imag_part * sine,
        imag_part * cosine + sign * real_part * sine,
    )


def combine(mixed_re, mixed_im, grad_re, grad_im, filt_re, filt_im):
    conv_re = filt_re * mixed_re - filt_im * mixed_im
    conv_im = filt_re * mixed_im + filt_im * mixed_re
    corr_re = filt_re * grad_re + filt_im * grad_im
    corr_im = filt_re * grad_im - filt_im * grad_re
    cross_re = mixed_re * grad_re + mixed_im * grad_im
    cross_im = mixed_re * grad_im - mixed_im * grad_re
    return (conv_re - corr_im, conv_im + corr_re, cross_re, cross_im)


def featurize(extended, weights, row_count):
    tap_count = weights.shape[1]
    accumulated = jnp.zeros((row_count,) + extended.shape[1:], jnp.float32)
    for offset in range(tap_count):
        first_row = tap_count - 1 - offset
        accumulated = accumulated + weights[:, offset, :] * extended[
            first_row : first_row + row_count
        ].astype(jnp.float32)
    return accumulated


def transpose_pair(signals, filters):
    return (
        lax.all_to_all(signals, "seq", split_axis=0, concat_axis=1, tiled=True),
        lax.all_to_all(filters, "seq", split_axis=0, concat_axis=1, tiled=True),
    )


def sequence_plan(mixed_input, gated_grad, long_filter):
    row_count, chan_count = mixed_input.shape
    group_count = long_filter.shape[0]
    seq_count = lax.axis_size("seq")
    seq_index = lax.axis_index("seq")
    per_block = row_count // seq_count
    fft_length = 2 * row_count * seq_count
    freq_index = jnp.arange(2 * seq_count, dtype=jnp.int32)
    block_index = jnp.arange(seq_count, dtype=jnp.int32)
    row_index = jnp.arange(row_count, dtype=jnp.int32)
    signals = jnp.stack([mixed_input, gated_grad], 1)[:, None]
    filters = jnp.transpose(long_filter)[:, None]
    sig_cols, filt_cols = transpose_pair(signals, filters)
    cos_one, sin_one = angle_table(freq_index, block_index, 2 * seq_count)
    sig_re = einsum_high("kb,abxc->kaxc", cos_one, sig_cols)
    sig_im = -einsum_high("kb,abxc->kaxc", sin_one, sig_cols)
    filt_re = einsum_high("kb,abg->kag", cos_one, filt_cols)
    filt_im = -einsum_high("kb,abg->kag", sin_one, filt_cols)
    positions = seq_index * per_block + jnp.arange(per_block, dtype=jnp.int32)
    cos_twist, sin_twist = angle_table(freq_index, positions, fft_length)
    sig_re, sig_im = rotate(
        sig_re, sig_im, cos_twist[:, :, None, None], sin_twist[:, :, None, None], -1.0
    )
    filt_re, filt_im = rotate(filt_re, filt_im, cos_twist[:, :, None], sin_twist[:, :, None], -1.0)
    sig_rows, filt_rows = transpose_pair(
        jnp.stack([sig_re, sig_im], 2), jnp.stack([filt_re, filt_im], 2)
    )
    cos_two, sin_two = angle_table(row_index, row_index, row_count)
    spec_re, spec_im = complex_dft(
        cos_two, sin_two, sig_rows[:, :, 0], sig_rows[:, :, 1], "pqka,qjaxc->pjkxc", -1.0
    )
    hspec_re, hspec_im = complex_dft(
        cos_two, sin_two, filt_rows[:, :, 0], filt_rows[:, :, 1], "pqka,qjag->pjkg", -1.0
    )
    leading = spec_re.shape[:2]
    group_shape = leading + (group_count, chan_count // group_count)
    wave_re, wave_im, cross_re, cross_im = combine(
        spec_re[:, :, 0].reshape(group_shape),
        spec_im[:, :, 0].reshape(group_shape),
        spec_re[:, :, 1].reshape(group_shape),
        spec_im[:, :, 1].reshape(group_shape),
        hspec_re[..., None],
        hspec_im[..., None],
    )
    wave_re = wave_re.reshape(leading + (chan_count,))
    wave_im = wave_im.reshape(leading + (chan_count,))
    cross_re = jnp.sum(cross_re, -1)
    cross_im = jnp.sum(cross_im, -1)
    back_re, back_im = complex_dft(cos_two, sin_two, wave_re, wave_im, "pqak,qjkc->pajc", 1.0)
    cback_re, cback_im = complex_dft(cos_two, sin_two, cross_re, cross_im, "pqak,qjkg->pajg", 1.0)
    pair_freq = seq_index * 2 + jnp.arange(2, dtype=jnp.int32)
    cos_back, sin_back = angle_table(row_index, pair_freq, fft_length)
    back_re, back_im = rotate(back_re, back_im, cos_back[:, :, None], sin_back[:, :, None], 1.0)
    cback_re, cback_im = rotate(cback_re, cback_im, cos_back[:, :, None], sin_back[:, :, None], 1.0)
    wave_cols, cross_cols = transpose_pair(
        jnp.stack([back_re, back_im], 2), jnp.stack([cback_re, cback_im], 2)
    )
    cos_three, sin_three = angle_table(block_index, freq_index, 2 * seq_count)
    time_re, time_im = complex_dft(
        cos_three, sin_three, wave_cols[:, :, 0], wave_cols[:, :, 1], "pqbk,qakc->pbac", 1.0
    )
    cross_time = einsum_high("bk,akg->bag", cos_three, cross_cols[:, :, 0]) - einsum_high(
        "bk,akg->bag", sin_three, cross_cols[:, :, 1]
    )
    inverse_scale = 1.0 / fft_length
    wave_out, cross_out = transpose_pair(
        jnp.stack([time_re, time_im], 2) * inverse_scale, cross_time * inverse_scale
    )
    return (wave_out[0, :, 0], wave_out[0, :, 1], jnp.transpose(cross_out[0]))


def split_halves(value):
    top = value.astype(jnp.bfloat16)
    rest = (value - top.astype(jnp.float32)).astype(jnp.bfloat16)
    return top, rest


def dot32(left, right):
    return jnp.dot(left, right, preferred_element_type=jnp.float32)


def dot32_t(left, right):
    return lax.dot_general(
        left, right, (((1,), (1,)), ((), ())), preferred_element_type=jnp.float32
    )


def tile(index, width=LANES):
    return pl.ds(pl.multiple_of(index * width, width), width)


def send_to(src, dst, send_sem, recv_sem, peer):
    return pltpu.make_async_remote_copy(
        src_ref=src,
        dst_ref=dst,
        send_sem=send_sem,
        recv_sem=recv_sem,
        device_id=peer,
        device_id_type=MESH,
    )


def build_filters(taps, ns, low_hi, low_lo, up_hi, up_lo):
    row = lax.broadcasted_iota(jnp.int32, (LANES, LANES), 0)
    col = lax.broadcasted_iota(jnp.int32, (LANES, LANES), 1)
    flip = (row + col == LANES - 1).astype(jnp.float32)
    zero = jnp.zeros((LANES, LANES), jnp.float32)
    zero16 = zero.astype(jnp.bfloat16)
    flipped = jnp.dot(
        taps[...].reshape(ns * 8, LANES), flip, precision=highest,
        preferred_element_type=jnp.float32,
    )
    last_up, last_low = zero, zero
    top = ns - WIDE // LANES
    low_hi[:, (ns - 1) * LANES :] = jnp.concatenate([zero16, zero16], 0)
    low_lo[:, (ns - 1) * LANES :] = jnp.concatenate([zero16, zero16], 0)
    up_hi[LANES:, :LANES] = zero16
    up_lo[LANES:, :LANES] = zero16
    for d in range(ns):
        forward = jnp.concatenate([taps[d]] * (LANES // 8), 0)
        back = jnp.concatenate([flipped[d * 8 : d * 8 + 8]] * (LANES // 8), 0)
        forward = pltpu.roll(forward, 0, 1, stride=1, stride_axis=0)
        back = pltpu.roll(back, 1, 1, stride=1, stride_axis=0)
        up = split_halves(jnp.where(col >= row, forward, last_up))
        low = split_halves(jnp.where(row >= col, back, last_low))
        last_up, last_low = forward, back
        for u in range(WIDE // LANES):
            v = d + u
            if v < ns:
                up_hi[u * LANES : (u + 1) * LANES, v * LANES : (v + 1) * LANES] = up[0]
                up_lo[u * LANES : (u + 1) * LANES, v * LANES : (v + 1) * LANES] = up[1]
            v = top + u - d
            if 0 <= v < ns:
                low_hi[u * LANES : (u + 1) * LANES, v * LANES : (v + 1) * LANES] = low[0]
                low_lo[u * LANES : (u + 1) * LANES, v * LANES : (v + 1) * LANES] = low[1]


def diagonal_sums(gram, ns):
    row = lax.broadcasted_iota(jnp.int32, (LANES, LANES), 0)
    col = lax.broadcasted_iota(jnp.int32, (LANES, LANES), 1)
    turned = []
    for d in range(ns):
        block = gram[LANES:, d * LANES : (d + 1) * LANES]
        if d + 1 < ns:
            block = block + gram[:LANES, (d + 1) * LANES : (d + 2) * LANES]
        turned.append(pltpu.roll(block, 1, 1, stride=1, stride_axis=0))
    turned.append(jnp.zeros((LANES, LANES), jnp.float32))
    return [
        jnp.sum(jnp.where(col <= row, turned[d], turned[d + 1]), 0, keepdims=True)
        for d in range(ns)
    ]


def dot_three(hi, lo, signal):
    width = signal.shape[1] // 2
    both = dot32(hi, signal)
    return both[:, :width] + both[:, width:] + dot32(lo, signal[:, :width])


def resident_kernel(
    ns, nc, kt, groups,
    proj, cot, weight_in, filt_in,
    gp_out, gs_out, gf_out,
    weight, filt, packed, pin, halo, wide, feat, mixed, gated, part, part_edge, fgrad, gp_send,
    tap_send, taps, low_hi, low_lo, up_hi, up_lo, gram,
    fa_send, fa_recv, fb_send, fb_recv, gs_acc, gs_send, gs_pair, gs_sum, gs_recv,
    local_sem, pack_sem, tap_ssem, tap_rsem, in_send, in_recv, gp_ssem, gp_rsem, gs_ssem, gs_rsem,
    fa_ssem, fa_rsem, fb_ssem, fb_rsem, pair_sem,
):
    me = lax.axis_index("seq")
    mych = lax.axis_index("ch")
    hs = ns // 2
    total = ns * LANES
    span = total // 2
    half = me // hs
    mine = lax.rem(me, hs)
    own_base = pl.multiple_of(half * span, span)
    group_owners = hs // groups
    near = [half * hs + lax.rem(mine + i, hs) for i in range(1, hs)]
    far = [(1 - half) * hs + lax.rem(mine + i, hs) for i in range(hs)]
    everyone = near + far
    ch_peers = [(me, lax.rem(mych + i, nc)) for i in range(1, nc)]
    lanes_of = lambda q, t: tile(lax.rem(q, hs) * 2 + t)

    own = [
        pltpu.make_async_copy(filt_in, filt, local_sem.at[0]),
    ]
    for t in range(2):
        own.append(
            pltpu.make_async_copy(
                weight_in.at[:, :, lanes_of(me, t)], weight.at[t], local_sem.at[1 + t]
            )
        )
    packs = []
    for c in range(2 * hs):
        lanes = slice(c * LANES, (c + 1) * LANES)
        packs += [
            pltpu.make_async_copy(
                proj.at[1:3, :, lanes], packed.at[c, 0:2], pack_sem.at[0, c]
            ),
            pltpu.make_async_copy(
                proj.at[0:1, :, lanes], packed.at[c, 2:3], pack_sem.at[1, c]
            ),
            pltpu.make_async_copy(cot.at[:, lanes], packed.at[c, 3], pack_sem.at[2, c]),
        ]
    own += packs
    for copy in own:
        copy.start()
    barrier = pltpu.get_barrier_semaphore()
    for q in everyone:
        pl.semaphore_signal(barrier, inc=1, device_id=(q, mych), device_id_type=MESH)
    for peer in ch_peers:
        pl.semaphore_signal(barrier, inc=1, device_id=peer, device_id_type=MESH)
    own[0].wait()
    for g in range(groups):
        tap_send[g] = jnp.broadcast_to(filt[g : g + 1, :], (8, LANES))
    pl.semaphore_wait(barrier, ns + nc - 2)

    def tap_copy(q, src):
        return send_to(
            tap_send.at[lax.rem(q, hs) // group_owners], taps.at[src],
            tap_ssem.at[q], tap_rsem.at[src], (q, mych),
        )

    def halo_copy(q, t, src, first):
        return send_to(
            packed.at[lax.rem(q, hs) * 2 + t, 0:3, pl.ds(first, 16)], halo.at[t],
            in_send.at[t, 1, q], in_recv.at[t, 1, 0], (q, mych),
        )

    def stream_copy(q, t, src, streams):
        return send_to(
            packed.at[lax.rem(q, hs) * 2 + t, streams], pin.at[t, src, streams],
            in_send.at[t, 0, q], in_recv.at[t, 0, src], (q, mych),
        )

    def near_copies(q, t, src):
        return (stream_copy(q, t, src, slice(0, 4)),)

    def mix_copy(q, t, src):
        return stream_copy(q, t, src, slice(0, 2))

    def gate_copies(q, t, src):
        return (stream_copy(q, t, src, slice(2, 4)),)

    for q in everyone:
        tap_copy(q, me).start()
    for copy in packs:
        copy.wait()

    @pl.when(me == hs - 1)
    def _():
        for t in range(2):
            for q in far:
                halo_copy(q, t, me, LANES - 16).start()

    @pl.when(me == hs)
    def _():
        for t in range(2):
            for q in far:
                halo_copy(q, t, me, 0).start()

    for t in range(2):
        for i in range(hs):
            @pl.when(half == 0)
            def _():
                mix_copy(far[i], t, me).start()

            @pl.when(half == 1)
            def _():
                for copy in gate_copies(far[i], t, me):
                    copy.start()

            if i < hs - 1:
                for copy in near_copies(near[i], t, me):
                    copy.start()

    taps[me] = tap_send[mine // group_owners]
    gram[...] = jnp.zeros(gram.shape, jnp.float32)
    for j in range(3):
        wide[j, 0:8, :] = jnp.zeros((8, LANES), jnp.float32)
        fgrad[j, span : span + 16, :] = jnp.zeros((16, LANES), jnp.float32)
        for t in range(2):
            for k in range(kt):
                gs_acc[t, j, k] = jnp.zeros((8, LANES), jnp.float32)
    for q in everyone:
        tap_copy(q, q).wait_recv()
    build_filters(taps, ns, low_hi, low_lo, up_hi, up_lo)
    for copy in own[1:3]:
        copy.wait()
    for t in range(2):
        pin[t, me] = packed[mine * 2 + t]
    for t in range(2):
        halo_copy(far[0], t, 0, 0).wait_recv()

    place = (2, 0, 1)

    def to_wide(t, j, b):
        first = pl.multiple_of(b * LANES, LANES)
        block = pin[t, b, place[j]]
        wide[j, pl.ds(first + 8, LANES), :] = block.astype(jnp.float32)

    def cot_rows(t, b, first, rows):
        return pin[t, b, 3, pl.ds(first, rows), :].astype(jnp.float32)

    def feature(t, j, first, rows):
        acc = jnp.zeros((rows, LANES), jnp.float32)
        for k in range(kt):
            acc = acc + weight[t, j, k : k + 1, :] * wide[j, pl.ds(first + 8 - k, rows), :]
        return acc

    def keep(store, rows, value):
        top, rest = split_halves(value)
        store[rows, 0:LANES] = top
        store[rows, LANES:] = rest

    def near_block(t, i, carry):
        b = half * hs + i

        @pl.when(b != me)
        def _():
            for copy in near_copies(b, t, b):
                copy.wait_recv()

        base = pl.multiple_of(b * LANES, LANES)
        for j in range(3):
            to_wide(t, j, b)
        for p in range(LANES // ROWS):
            first = base + p * ROWS
            rows = pl.ds(first, ROWS)
            kept = pl.ds(pl.multiple_of(i * LANES, LANES) + p * ROWS, ROWS)
            one, two = feature(t, 1, first, ROWS), feature(t, 2, first, ROWS)
            feat[0, kept, :] = one
            feat[1, kept, :] = two
            keep(mixed, rows, one * two)
            keep(gated, rows, cot_rows(t, b, p * ROWS, ROWS) * feature(t, 0, first, ROWS))
        return carry

    def far_block(early, t, i, carry):
        b = (1 - half) * hs + i
        base = pl.multiple_of(b * LANES, LANES)
        for copy in gate_copies(b, t, b) if early else (mix_copy(b, t, b),):
            copy.wait_recv()
        for j in (0,) if early else (1, 2):
            to_wide(t, j, b)
        for p in range(LANES // ROWS):
            first = base + p * ROWS
            rows = pl.ds(first, ROWS)
            if early:
                gate = feature(t, 0, first, ROWS)
                keep(gated, rows, cot_rows(t, b, p * ROWS, ROWS) * gate)
            else:
                keep(mixed, rows, feature(t, 1, first, ROWS) * feature(t, 2, first, ROWS))
        return carry

    flip = (
        lax.broadcasted_iota(jnp.int32, (WIDE, WIDE), 0)
        + lax.broadcasted_iota(jnp.int32, (WIDE, WIDE), 1)
        == WIDE - 1
    ).astype(jnp.float32).astype(jnp.bfloat16)

    def add_gram(pairs):
        for b in sorted({b for b, _ in pairs}):
            left = dot32(flip, mixed[b * WIDE : (b + 1) * WIDE, :]).astype(jnp.bfloat16)
            for c in sorted(c for first, c in pairs if first == b):
                right = gated[c * WIDE : (c + 1) * WIDE, :]
                top = right[:, :LANES]
                cols = slice((c - b) * WIDE, (c - b + 1) * WIDE)
                gram[:, cols] += dot32_t(left, jnp.concatenate([top, top], 1)) + dot32_t(
                    left[:, :LANES], right[:, LANES:]
                )

    def conv_of(b, first, last, rows=WIDE):
        start = total - (b + 1) * WIDE
        cols = slice(start + first, start + last)
        return dot_three(low_hi[:rows, cols], low_lo[:rows, cols], mixed[first:last, :])

    def corr_of(a, first, last, rows=WIDE):
        cols = slice(first - a * WIDE, last - a * WIDE)
        return dot_three(up_hi[:rows, cols], up_lo[:rows, cols], gated[first:last, :])

    def grads_of(t, rows, conv=None, corr=None):
        if conv is not None:
            size = min(rows.stop - rows.start, LANES)
            blocks = range(rows.start // LANES, max(rows.stop // LANES, rows.start // LANES + 1))
            grads = [cot_rows(t, half * hs + b, 0, size) for b in blocks]
            fgrad[0, rows, :] = jnp.concatenate(grads, 0) * conv
        if corr is not None:
            fgrad[1, rows, :] = corr * feat[1, rows, :]
            fgrad[2, rows, :] = corr * feat[0, rows, :]

    per = span // WIDE
    local_rows = [slice(b * WIDE, (b + 1) * WIDE) for b in range(per)]
    edge = slice(span, span + 16)
    near_pairs = [(b, c) for b in range(per) for c in range(b, per)]
    far_pairs = [(b, c) for b in range(per) for c in range(per, 2 * per)]

    def early_part(t):
        for j in (1, 2):
            wide[j, 8 + span : 8 + span + 16, :] = halo[t, place[j]].astype(jnp.float32)
        lax.fori_loop(0, hs, functools.partial(near_block, t), 0)
        mixed[span : span + LANES, :] = jnp.zeros((LANES, WIDE), jnp.bfloat16)
        one, two = feature(t, 1, span, 16), feature(t, 2, span, 16)
        feat[0, edge, :] = one
        feat[1, edge, :] = two
        keep(mixed, edge, one * two)
        for b in range(per):
            grads_of(t, local_rows[b], conv=conv_of(b, 0, (b + 1) * WIDE))
            part[local_rows[b], :] = corr_of(b, b * WIDE, span)
        part_edge[...] = conv_of(per, 0, span + LANES, 16)
        add_gram(near_pairs)
        lax.fori_loop(0, hs, functools.partial(far_block, True, t), 0)
        for b in range(per):
            grads_of(t, local_rows[b], corr=part[local_rows[b], :] + corr_of(b, span, total))
        grads_of(t, edge, conv=part_edge[...], corr=corr_of(per, span, total, 16))

    def late_part(t):
        for j in range(3):
            wide[j, 8 + span - 16 : 8 + span, :] = halo[t, place[j]].astype(jnp.float32)
        lax.fori_loop(0, hs, functools.partial(near_block, t), 0)
        for b in range(per):
            grads_of(t, local_rows[b], corr=corr_of(per + b, span + b * WIDE, total))
            part[local_rows[b], :] = conv_of(per + b, span, span + (b + 1) * WIDE)
        add_gram([(per + b, per + c) for b, c in near_pairs])
        lax.fori_loop(0, hs, functools.partial(far_block, False, t), 0)
        for b in range(per):
            grads_of(t, local_rows[b], conv=part[local_rows[b], :] + conv_of(per + b, 0, span))

    def finish_block(t, i, carry):
        b = lax.rem(mine + 1 + i, hs)
        base = pl.multiple_of(b * LANES, LANES)
        for p in range(LANES // ROWS):
            first = base + p * ROWS
            for j in range(3):
                acc = jnp.zeros((ROWS, LANES), jnp.float32)
                source = wide[j, pl.ds(own_base + first + 8, ROWS), :]
                for k in range(kt):
                    shifted = fgrad[j, pl.ds(first + k, ROWS), :]
                    acc = acc + weight[t, j, k : k + 1, :] * shifted
                    terms = (shifted * source).reshape(ROWS // 8, 8, LANES)
                    gs_acc[t, j, k] += jnp.sum(terms, 0)
                gp_send[t, j, pl.ds(first, ROWS), :] = acc.astype(jnp.bfloat16)

        @pl.when(i < hs - 1)
        def _():
            gp_copy(half * hs + b, t, me).start()

        return carry

    def gp_copy(q, t, src):
        return send_to(
            gp_send.at[t, :, tile(lax.rem(q, hs)), :], gp_out.at[:, :, lanes_of(src, t)],
            gp_ssem.at[t, q], gp_rsem.at[t, src], (q, mych),
        )

    filter_scale = 1.0 / math.sqrt(total * group_owners * WIDE)
    fa_copy = lambda q, src: send_to(
        fa_send.at[q], fa_recv.at[src], fa_ssem.at[q], fa_rsem.at[src], (q, mych)
    )

    def one_tile(t, carry):
        @pl.when(half == 0)
        def _():
            early_part(t)

        @pl.when(half == 1)
        def _():
            late_part(t)

        lax.fori_loop(0, hs - 1, functools.partial(finish_block, t), 0)

        @pl.when(t == half)
        def _():
            add_gram(far_pairs)

        @pl.when(t == 1)
        def _():
            for d, line in enumerate(diagonal_sums(gram, ns)):
                fa_send[d] = jnp.broadcast_to(line * filter_scale, (8, LANES))
            for q in everyone:
                fa_copy(q, me).start()
            fa_recv[me] = fa_send[me]

        finish_block(t, hs - 1, carry)
        gp_out[:, :, lanes_of(me, t)] = gp_send[t, :, tile(mine), :]
        return carry

    lax.fori_loop(0, 2, one_tile, 0)

    short_scale = 1.0 / math.sqrt(total)
    for t in range(2):
        for j in range(3):
            lines = [jnp.sum(gs_acc[t, j, k], 0, keepdims=True) for k in range(kt)]
            lines += [jnp.zeros((1, LANES), jnp.float32)] * (8 - kt)
            gs_send[t, j] = jnp.concatenate(lines, 0) * short_scale
    partner = far[0]
    pair = send_to(gs_send, gs_pair, pair_sem.at[0], pair_sem.at[1], (partner, mych))
    pair.start()

    for q in everyone:
        fa_copy(q, q).wait_recv()
    for g in range(groups):
        owners = [h * hs + g * group_owners + i for h in range(2) for i in range(group_owners)]
        summed = fa_recv[owners[0]]
        for q in owners[1:]:
            summed = summed + fa_recv[q]
        fb_send[g] = summed
    fb_copy = lambda c, src: send_to(
        fb_send, fb_recv.at[src], fb_ssem.at[c], fb_rsem.at[src], (me, c)
    )
    for _, c in ch_peers:
        fb_copy(c, mych).start()
    fb_recv[mych] = fb_send[...]
    pair.wait()
    gs_sum[...] = gs_send[...] + gs_pair[...]
    gs_copy = lambda q, src: send_to(
        gs_sum, gs_recv.at[lax.rem(src, hs)], gs_ssem.at[q], gs_rsem.at[src], (q, mych)
    )
    for q in near:
        gs_copy(q, me).start()
    gs_recv[mine] = gs_sum[...]

    for _, c in ch_peers:
        fb_copy(c, c).wait_recv()
    width = LANES // nc
    for c in range(nc):
        for g in range(groups):
            line = fb_recv[c, g]
            piece = line[:, 0:width]
            for other in range(1, nc):
                piece = jnp.where(
                    mych == other, line[:, other * width : (other + 1) * width], piece
                )
            at = c * groups + g
            gf_out[at : at + 1, :] = piece[0:1, :]

    for q in near:
        gs_copy(q, q).wait_recv()
    for q in range(hs):
        for t in range(2):
            lanes = slice((2 * q + t) * LANES, (2 * q + t + 1) * LANES)
            for j in range(3):
                gs_out[j, :, lanes] = gs_recv[q, t, j, 0:kt, :]

    for q in everyone:
        tap_copy(q, me).wait_send()
        fa_copy(q, me).wait_send()
    for q in near:
        gs_copy(q, me).wait_send()
        for t in range(2):
            for copy in near_copies(q, t, me):
                copy.wait_send()
            gp_copy(q, t, me).wait_send()
            gp_copy(q, t, q).wait_recv()
    for _, c in ch_peers:
        fb_copy(c, mych).wait_send()

    @pl.when(half == 0)
    def _():
        for q in far:
            for t in range(2):
                mix_copy(q, t, me).wait_send()

    @pl.when(half == 1)
    def _():
        for q in far:
            for t in range(2):
                for copy in gate_copies(q, t, me):
                    copy.wait_send()

    @pl.when((me == hs - 1) | (me == hs))
    def _():
        for q in far:
            for t in range(2):
                halo_copy(q, t, me, 0).wait_send()


def resident(projected, cotangent, short_weight, long_filter):
    row_count, streams, chan_count = projected.shape
    kt = short_weight.shape[1]
    groups = long_filter.shape[0]
    ns, nc = lax.axis_size("seq"), lax.axis_size("ch")
    total = row_count * ns
    span = total // 2
    f32, bf16 = jnp.float32, jnp.bfloat16
    dma = pltpu.SemaphoreType.DMA
    vmem = pl.BlockSpec(memory_space=pltpu.VMEM)
    anywhere = pl.BlockSpec(memory_space=pltpu.HBM)
    operands = [
        pltpu.with_memory_space_constraint(x, pltpu.HBM)
        for x in (jnp.transpose(projected, (1, 0, 2)), cotangent, short_weight, long_filter)
    ]
    grad_proj, grad_short, grad_filter = pl.pallas_call(
        functools.partial(resident_kernel, ns, nc, kt, groups),
        out_shape=(
            jax.ShapeDtypeStruct((streams, row_count, chan_count), bf16),
            jax.ShapeDtypeStruct((streams, kt, chan_count), f32),
            jax.ShapeDtypeStruct((groups * nc, row_count // nc), f32),
        ),
        in_specs=[anywhere] * 4,
        out_specs=(vmem, vmem, vmem),
        scratch_shapes=[
            pltpu.VMEM((2, 3, kt, LANES), f32),
            pltpu.VMEM((groups, LANES), f32),
            pltpu.VMEM((ns, 4, LANES, LANES), bf16),
            pltpu.VMEM((2, ns, 4, LANES, LANES), bf16),
            pltpu.VMEM((2, 3, 16, LANES), bf16),
            pltpu.VMEM((3, total + 8, LANES), f32),
            pltpu.VMEM((2, span + 16, LANES), f32),
            pltpu.VMEM((total, WIDE), bf16),
            pltpu.VMEM((total, WIDE), bf16),
            pltpu.VMEM((span, LANES), f32),
            pltpu.VMEM((16, LANES), f32),
            pltpu.VMEM((3, span + 16, LANES), f32),
            pltpu.VMEM((2, 3, span, LANES), bf16),
            pltpu.VMEM((groups, 8, LANES), f32),
            pltpu.VMEM((ns, 8, LANES), f32),
            pltpu.VMEM((WIDE, total), bf16),
            pltpu.VMEM((WIDE, total), bf16),
            pltpu.VMEM((WIDE, total), bf16),
            pltpu.VMEM((WIDE, total), bf16),
            pltpu.VMEM((WIDE, total), f32),
            pltpu.VMEM((ns, 8, LANES), f32),
            pltpu.VMEM((ns, 8, LANES), f32),
            pltpu.VMEM((groups, 8, LANES), f32),
            pltpu.VMEM((nc, groups, 8, LANES), f32),
            pltpu.VMEM((2, 3, 8, 8, LANES), f32),
            pltpu.VMEM((2, 3, 8, LANES), f32),
            pltpu.VMEM((2, 3, 8, LANES), f32),
            pltpu.VMEM((2, 3, 8, LANES), f32),
            pltpu.VMEM((ns // 2, 2, 3, 8, LANES), f32),
            dma((3,)), dma((3, ns)),
            dma((ns,)), dma((ns,)),
            dma((2, 2, ns)), dma((2, 2, ns)),
            dma((2, ns)), dma((2, ns)),
            dma((ns,)), dma((ns,)),
            dma((ns,)), dma((ns,)),
            dma((nc,)), dma((nc,)),
            dma((2,)),
        ],
        compiler_params=pltpu.CompilerParams(
            collective_id=0, has_side_effects=True, vmem_limit_bytes=48 * 1024 * 1024
        ),
    )(*operands)
    return jnp.transpose(grad_proj, (1, 0, 2)), grad_short, grad_filter


def spread(projected, cotangent, short_weight, long_filter):
    tap_count = short_weight.shape[1]
    row_count = projected.shape[0]
    margin = tap_count - 1
    front_rows = passed_along(projected[row_count - margin :], "seq", 1)
    extended = jnp.concatenate([front_rows, projected], 0)
    features = featurize(extended, short_weight, row_count)
    grad_out = cotangent.astype(jnp.float32)
    mixed_input = features[:, 1] * features[:, 2]
    gated_grad = grad_out * features[:, 0]
    conv_out, corr_out, filt_grad = sequence_plan(mixed_input, gated_grad, long_filter)
    token_count = row_count * lax.axis_size("seq")
    group_width = mixed_input.shape[1] // long_filter.shape[0]
    scaled_grad = filt_grad * (1.0 / math.sqrt(token_count * group_width))
    owned_grad = lax.all_to_all(scaled_grad, "ch", split_axis=1, concat_axis=0, tiled=True)
    feat_grad = jnp.stack(
        [grad_out * conv_out, corr_out * features[:, 2], corr_out * features[:, 1]], 1
    )
    next_rows = passed_along(feat_grad[:margin].astype(jnp.bfloat16), "seq", -1).astype(jnp.float32)
    extended_grad = jnp.concatenate([feat_grad, next_rows], 0)
    grad_proj = jnp.zeros(feat_grad.shape, jnp.float32)
    for offset in range(tap_count):
        grad_proj = (
            grad_proj + short_weight[:, offset, :] * extended_grad[offset : offset + row_count]
        )
    short_terms = []
    for offset in range(tap_count):
        first_row = margin - offset
        short_terms.append(
            jnp.sum(feat_grad * extended[first_row : first_row + row_count].astype(jnp.float32), 0)
        )
    grad_short = lax.psum(jnp.stack(short_terms, 1), "seq") * (1.0 / math.sqrt(token_count))
    return (grad_proj.astype(jnp.bfloat16), grad_short, owned_grad)


def local(projected, cotangent, short_weight, long_filter):
    row_count, _, chan_count = projected.shape
    seq_count = lax.axis_size("seq")
    group_width = chan_count // long_filter.shape[0]
    fits = (
        row_count == LANES
        and seq_count % 4 == 0
        and chan_count == WIDE * (seq_count // 2)
        and group_width % WIDE == 0
        and short_weight.shape[1] <= 8
    )
    plan = resident if fits else spread
    return plan(projected, cotangent, short_weight, long_filter)


def solution(mesh):
    return jax.shard_map(
        local,
        mesh=mesh,
        in_specs=(P("seq", None, "ch"), P("seq", "ch"), P(None, None, "ch"), P("ch", "seq")),
        out_specs=(P("seq", None, "ch"), P(None, None, "ch"), P(None, ("seq", "ch"))),
        check_vma=False,
    )
```
